32 devices in a mesh: seg: 8 (over y, x, core), sub: 4 (over z).
Axes of the slice: x: 2, y: 2, z: 4, core: 2. Of those that a mesh axis runs over, the one named last changes fastest.
Arguments:
- fields: float32 [7, 256, 512], P(None, 'seg', 'sub'), may hold values from -1.5 to 3, as said below
- region_levels: int32 [8, 4], replicated, may hold values from 0 to 2, as said below
Outputs:
- new_fields: float32 [7, 256, 512], P(None, 'seg', 'sub')
The draws below stay inside these ranges and needn't reach their ends.
Inputs may be any that keep to these rules, and one draw needn't show every extreme that they name: `region_levels`: root regions sharing a side or a corner differ by at most one level; some root region is at level 2. `fields`: component 0 (density) lies between 1 and 3; tile entries in a tile's unused room are not read.
All inputs are finite; a program needn't handle non-finite values.
Results may differ from the reference program's by a relative error of at most 0.0003.
Values sent between devices are 32-bit elements; how exact they have to be, the bound alone decides.
A program may use at most 64 MiB of HBM per device.

```python
import math
from functools import partial
import jax
import jax.numpy as jnp
from jax import lax

GRID_Y = 256
GRID_X = 512
N_SEG = 8
N_SUB = 4


def draw_fields(key, part):
    key = jax.random.fold_in(key, 5)
    keys = jax.random.split(key, 7)
    grid_shape = (GRID_Y, GRID_X)
    density = jnp.exp(jax.random.uniform(keys[0], grid_shape, jnp.float32, 0.0, math.log(3.0)))
    speed_x = 0.25 * jax.random.truncated_normal(keys[1], -2.0, 2.0, grid_shape, jnp.float32)
    speed_y = 0.25 * jax.random.truncated_normal(keys[2], -2.0, 2.0, grid_shape, jnp.float32)
    speed_z = 0.25 * jax.random.truncated_normal(keys[3], -2.0, 2.0, grid_shape, jnp.float32)
    field_z = 0.3 * jax.random.truncated_normal(keys[4], -2.0, 2.0, grid_shape, jnp.float32)
    face_x = 0.3 * jax.random.truncated_normal(keys[5], -2.0, 2.0, grid_shape, jnp.float32)
    face_y = 0.3 * jax.random.truncated_normal(keys[6], -2.0, 2.0, grid_shape, jnp.float32)
    return jnp.stack([density, density * speed_x, density * speed_y, density * speed_z, field_z, face_x, face_y]).astype(jnp.float32)


def draw_region_levels(key, part):
    key = jax.random.fold_in(key, 11)
    keys = jax.random.split(key, 2)
    seed_count = max(N_SEG // 2, 1)
    start_row = jax.random.randint(keys[0], (), 0, N_SEG)
    start_col = jax.random.randint(keys[1], (), 0, N_SUB)
    counter = jnp.arange(seed_count, dtype=jnp.int32)
    seed_rows = (start_row + 2 * counter) % N_SEG
    seed_cols = (start_col + 5 * counter) % N_SUB
    row_gap = jnp.abs(jnp.arange(N_SEG, dtype=jnp.int32)[:, None] - seed_rows[None, :])
    row_gap = jnp.minimum(row_gap, N_SEG - row_gap)
    col_gap = jnp.abs(jnp.arange(N_SUB, dtype=jnp.int32)[:, None] - seed_cols[None, :])
    col_gap = jnp.minimum(col_gap, N_SUB - col_gap)
    distance = jnp.min(jnp.maximum(row_gap[:, None, :], col_gap[None, :, :]), axis=2)
    return (2 - jnp.minimum(distance, 2)).astype(jnp.int32)


def block_scale(rng, extent, cuts, smallest, high):
    gain, own = 1.0, jax.random.fold_in(rng, 6)
    for dim, parts in cuts:
        heights = jnp.exp(jax.random.uniform(jax.random.fold_in(own, dim), (parts,), jnp.float32, smallest / len(cuts), high / len(cuts)))
        gain = gain * jnp.repeat(heights, extent[dim] // parts).reshape([-1 if axis == dim else 1 for axis in range(len(extent))])
    return gain


def setup_inputs(seed: int = 0) -> dict:
    seeds = jax.random.split(jax.random.key(seed), 3)
    fields = draw_fields(jax.random.fold_in(seeds[2], 71), 0)
    region_levels = draw_region_levels(jax.random.fold_in(seeds[2], 71), 0)
    return dict(fields=fields, region_levels=region_levels)


SOUND_SQUARED = 1.0
STEP_SIZE = 0.08

def minmod(before_diff, after_diff):
    return 0.5 * (jnp.sign(before_diff) + jnp.sign(after_diff)) * jnp.minimum(jnp.abs(before_diff), jnp.abs(after_diff))

def riemann(left_state, right_state, normal):

    def pieces(values):
        density, speed_n, speed_t, speed_z, field_t, field_z = values
        field_square = normal * normal + field_t * field_t + field_z * field_z
        pressure = SOUND_SQUARED * density + 0.5 * field_square
        moment = density * speed_n
        fluxes = jnp.stack([moment, moment * speed_n + pressure - normal * normal, moment * speed_t - normal * field_t, moment * speed_z - normal * field_z, field_t * speed_n - normal * speed_t, field_z * speed_n - normal * speed_z])
        conserved = jnp.stack([density, moment, density * speed_t, density * speed_z, field_t, field_z])
        signal = jnp.abs(speed_n) + jnp.sqrt(SOUND_SQUARED + field_square / density)
        return (fluxes, conserved, signal)
    flux_left, cons_left, signal_left = pieces(left_state)
    flux_right, cons_right, signal_right = pieces(right_state)
    fastest = jnp.maximum(signal_left, signal_right)
    return 0.5 * (flux_left + flux_right) - 0.5 * fastest * (cons_right - cons_left)

def sweep_faces(primitives, normal):
    before_diff = primitives[:, :, 1:-1] - primitives[:, :, :-2]
    after_diff = primitives[:, :, 2:] - primitives[:, :, 1:-1]
    slopes = minmod(before_diff, after_diff)
    left_state = primitives[:, :, 1:-2] + 0.5 * slopes[:, :, :-1]
    right_state = primitives[:, :, 2:-1] - 0.5 * slopes[:, :, 1:]
    return riemann(left_state, right_state, normal[:, 2:-1])

def advance(ghosted, row_count, col_count, spacing):
    density = ghosted[0, :-1, :-1]
    speed_x = ghosted[1, :-1, :-1] / density
    speed_y = ghosted[2, :-1, :-1] / density
    speed_z = ghosted[3, :-1, :-1] / density
    field_z = ghosted[4, :-1, :-1]
    face_x = ghosted[5]
    face_y = ghosted[6]
    centre_x = 0.5 * (face_x[:-1, :-1] + face_x[:-1, 1:])
    centre_y = 0.5 * (face_y[:-1, :-1] + face_y[1:, :-1])
    along_x = sweep_faces(jnp.stack([density, speed_x, speed_y, speed_z, centre_y, field_z]), face_x[:-1, :-1])
    along_y = sweep_faces(jnp.stack([density, speed_y, speed_x, speed_z, centre_x, field_z]).transpose(0, 2, 1), face_y[:-1, :-1].T)
    step_ratio = STEP_SIZE / spacing
    flux_x = along_x[:, 3:row_count + 3, :]
    diff_x = flux_x[:, :, 2:col_count + 2] - flux_x[:, :, 1:col_count + 1]
    flux_y = along_y[:, 3:col_count + 3, :]
    diff_y = (flux_y[:, :, 2:row_count + 2] - flux_y[:, :, 1:row_count + 1]).transpose(0, 2, 1)
    change = jnp.stack([diff_x[0] + diff_y[0], diff_x[1] + diff_y[2], diff_x[2] + diff_y[1], diff_x[3] + diff_y[3], diff_x[5] + diff_y[5]])
    cell_update = ghosted[:5, 3:row_count + 3, 3:col_count + 3] - step_ratio * change
    edge_x = along_x[4, 2:row_count + 4, 1:col_count + 2]
    edge_y = along_y[4, 2:col_count + 4, 1:row_count + 2]
    edge_field = 0.25 * ((edge_y[1:] + edge_y[:-1]).T - (edge_x[1:] + edge_x[:-1]))
    return (cell_update, edge_field)

def halve_once(region_block):
    cell_part = 0.5 * (region_block[:5, 0::2, :] + region_block[:5, 1::2, :])
    cell_part = 0.5 * (cell_part[:, :, 0::2] + cell_part[:, :, 1::2])
    face_x = region_block[5, :, 0::2]
    face_x = 0.5 * (face_x[0::2] + face_x[1::2])
    face_y = region_block[6, 0::2, :]
    face_y = 0.5 * (face_y[:, 0::2] + face_y[:, 1::2])
    return jnp.concatenate([cell_part, face_x[None], face_y[None]], axis=0)

def coarsen(region_block, halvings):
    for repeat_count in range(halvings):
        region_block = halve_once(region_block)
    return region_block

def inject(region_tile, refine_level):
    factor = 4 >> refine_level
    row_count = region_tile.shape[1] // factor
    col_count = region_tile.shape[2] // factor
    part_used = region_tile[:, :row_count, :col_count]
    return jnp.repeat(jnp.repeat(part_used, factor, axis=1), factor, axis=2)

def publish_step(ghosted, refine_level, fine_rows, fine_cols):
    factor = 4 >> refine_level
    row_count = fine_rows // factor
    col_count = fine_cols // factor
    cell_update, edge_field = advance(ghosted, row_count, col_count, float(factor))
    cell_padded = jnp.zeros((5, fine_rows, fine_cols), jnp.float32).at[:, :row_count, :col_count].set(cell_update)
    published = jnp.zeros((fine_rows + 1, fine_cols + 1), jnp.float32).at[::factor, ::factor].set(edge_field)
    return (cell_padded, published)

def image_pass(window, refine_level, fine_rows, fine_cols):
    factor = 4 >> refine_level
    ghosted = coarsen(window, 2 - refine_level)
    margin = 12 // factor - 3
    ghosted = ghosted[:, margin:margin + fine_rows // factor + 6, margin:margin + fine_cols // factor + 6]
    return publish_step(ghosted, refine_level, fine_rows, fine_cols)

def corner(current, values_list, levels_list, refine_level):
    values = jnp.stack(values_list)
    levels = jnp.stack(levels_list)
    highest = jnp.max(levels)
    chosen = (levels == highest).astype(jnp.float32)
    average = jnp.sum(chosen * values) / jnp.sum(chosen)
    return jnp.where(highest > refine_level, average, current)

def correct(edge_field, halo_edges, near_levels, refine_level, factor, row_count, col_count):
    fine_rows = halo_edges.shape[0] - 3
    fine_cols = halo_edges.shape[1] - 3
    initial = edge_field
    bottom_line = halo_edges[0, 1:fine_cols + 2:factor]
    top_line = halo_edges[fine_rows + 2, 1:fine_cols + 2:factor]
    left_line = halo_edges[1:fine_rows + 2:factor, 0]
    right_line = halo_edges[1:fine_rows + 2:factor, fine_cols + 2]
    edge_field = edge_field.at[0, :].set(jnp.where(near_levels[0, 1] > refine_level, bottom_line, edge_field[0, :]))
    edge_field = edge_field.at[row_count, :].set(jnp.where(near_levels[2, 1] > refine_level, top_line, edge_field[row_count, :]))
    edge_field = edge_field.at[:, 0].set(jnp.where(near_levels[1, 0] > refine_level, left_line, edge_field[:, 0]))
    edge_field = edge_field.at[:, col_count].set(jnp.where(near_levels[1, 2] > refine_level, right_line, edge_field[:, col_count]))
    lower_left = corner(initial[0, 0], [halo_edges[0, 1], halo_edges[1, 0], halo_edges[0, 0]], [near_levels[0, 1], near_levels[1, 0], near_levels[0, 0]], refine_level)
    lower_right = corner(initial[0, col_count], [halo_edges[0, fine_cols + 1], halo_edges[1, fine_cols + 2], halo_edges[0, fine_cols + 2]], [near_levels[0, 1], near_levels[1, 2], near_levels[0, 2]], refine_level)
    upper_left = corner(initial[row_count, 0], [halo_edges[fine_rows + 2, 1], halo_edges[fine_rows + 1, 0], halo_edges[fine_rows + 2, 0]], [near_levels[2, 1], near_levels[1, 0], near_levels[2, 0]], refine_level)
    upper_right = corner(initial[row_count, col_count], [halo_edges[fine_rows + 2, fine_cols + 1], halo_edges[fine_rows + 1, fine_cols + 2], halo_edges[fine_rows + 2, fine_cols + 2]], [near_levels[2, 1], near_levels[1, 2], near_levels[2, 2]], refine_level)
    edge_field = edge_field.at[0, 0].set(lower_left)
    edge_field = edge_field.at[0, col_count].set(lower_right)
    edge_field = edge_field.at[row_count, 0].set(upper_left)
    edge_field = edge_field.at[row_count, col_count].set(upper_right)
    return edge_field

def faces_pass(cell_padded, published, halo_edges, current, start_fields, near_levels, refine_level, blending):
    fine_rows = current.shape[1]
    fine_cols = current.shape[2]
    factor = 4 >> refine_level
    row_count = fine_rows // factor
    col_count = fine_cols // factor
    edge_field = published[::factor, ::factor]
    edge_field = correct(edge_field, halo_edges, near_levels, refine_level, factor, row_count, col_count)
    step_ratio = STEP_SIZE / float(factor)
    face_x = current[5, :row_count, :col_count] - step_ratio * (edge_field[1:, :-1] - edge_field[:-1, :-1])
    face_y = current[6, :row_count, :col_count] + step_ratio * (edge_field[:-1, 1:] - edge_field[:-1, :-1])
    updated = jnp.concatenate([cell_padded[:, :row_count, :col_count], face_x[None], face_y[None]], axis=0)
    if blending:
        updated = 0.5 * (start_fields[:, :row_count, :col_count] + updated)
    return jnp.zeros((7, fine_rows, fine_cols), jnp.float32).at[:, :row_count, :col_count].set(updated)

def section(region_tiles, start_tiles, region_levels, blending):
    fine_rows = region_tiles.shape[3]
    fine_cols = region_tiles.shape[4]
    region_count = N_SEG * N_SUB
    injects = [partial(inject, refine_level=refine_level) for refine_level in range(3)]
    image_branches = [partial(image_pass, refine_level=refine_level, fine_rows=fine_rows, fine_cols=fine_cols) for refine_level in range(3)]
    face_branches = [partial(faces_pass, refine_level=refine_level, blending=blending) for refine_level in range(3)]

    def beside_all(region_index):
        seg_index = region_index // N_SUB
        sub_index = region_index % N_SUB
        rows_wanted = ((seg_index + jnp.arange(-1, 2, dtype=jnp.int32)) % N_SEG).astype(jnp.int32)
        cols_wanted = ((sub_index + jnp.arange(-1, 2, dtype=jnp.int32)) % N_SUB).astype(jnp.int32)
        return (seg_index, sub_index, rows_wanted, cols_wanted)

    def first_pass(region_index):
        seg_index, sub_index, rows_wanted, cols_wanted = beside_all(region_index)
        band_list = []
        for row_pos in range(3):
            strip_list = []
            for col_pos in range(3):
                neighbour_tile = region_tiles[rows_wanted[row_pos], cols_wanted[col_pos]]
                neighbour_level = region_levels[rows_wanted[row_pos], cols_wanted[col_pos]]
                strip_list.append(lax.switch(neighbour_level, injects, neighbour_tile))
            band_list.append(jnp.concatenate(strip_list, axis=2))
        assembled = jnp.concatenate(band_list, axis=1)
        window = assembled[:, fine_rows - 12:2 * fine_rows + 12, fine_cols - 12:2 * fine_cols + 12]
        return lax.switch(region_levels[seg_index, sub_index], image_branches, window)
    cell_all, publish_all = lax.map(first_pass, jnp.arange(region_count, dtype=jnp.int32))
    cell_all = cell_all.reshape(N_SEG, N_SUB, 5, fine_rows, fine_cols)
    publish_all = publish_all.reshape(N_SEG, N_SUB, fine_rows + 1, fine_cols + 1)

    def second_pass(region_index):
        seg_index, sub_index, rows_wanted, cols_wanted = beside_all(region_index)
        band_list = []
        for row_pos in range(3):
            strip_list = []
            for col_pos in range(3):
                strip_list.append(publish_all[rows_wanted[row_pos], cols_wanted[col_pos]])
            band_list.append(jnp.concatenate(strip_list, axis=1))
        assembled = jnp.concatenate(band_list, axis=0)
        halo_edges = assembled[fine_rows:2 * fine_rows + 3, fine_cols:2 * fine_cols + 3]
        near_levels = region_levels[rows_wanted][:, cols_wanted]
        return lax.switch(region_levels[seg_index, sub_index], face_branches, cell_all[seg_index, sub_index], publish_all[seg_index, sub_index], halo_edges, region_tiles[seg_index, sub_index], start_tiles[seg_index, sub_index], near_levels)
    result = lax.map(second_pass, jnp.arange(region_count, dtype=jnp.int32))
    return result.reshape(N_SEG, N_SUB, 7, fine_rows, fine_cols)

def reference(fields, region_levels):
    fine_rows = fields.shape[1] // N_SEG
    fine_cols = fields.shape[2] // N_SUB
    region_tiles = fields.reshape(7, N_SEG, fine_rows, N_SUB, fine_cols).transpose(1, 3, 0, 2, 4)
    midpoint = section(region_tiles, region_tiles, region_levels, False)
    final_tiles = section(midpoint, region_tiles, region_levels, True)
    return final_tiles.transpose(2, 0, 3, 1, 4).reshape(7, N_SEG * fine_rows, N_SUB * fine_cols)
```

```python
import functools

import jax
import jax.numpy as jnp
from jax import lax
from jax.experimental import pallas as pl
from jax.experimental.pallas import tpu as pltpu
from jax.sharding import PartitionSpec as P

STEP_SIZE = 0.08
MESH = pl.DeviceIdType.MESH
F32, BF16, I32 = jnp.float32, jnp.bfloat16, jnp.int32
ROWS, COLS = 32, 128
AROUND = [(1, 0), (1, 1), (1, -1), (-1, 0), (-1, 1), (-1, -1), (0, -1), (0, 1)]


def iota(shape, axis):
    return lax.broadcasted_iota(I32, shape, axis)


def pick(level, values):
    return jnp.where(level == 0, values[0], jnp.where(level == 1, values[1], values[2]))


def halves(value, axis):
    high = value.astype(BF16)
    low = (value - high.astype(F32)).astype(BF16)
    return jnp.concatenate([high, low], axis=axis)


def dot(a, b, dims=((1,), (0,))):
    return lax.dot_general(a, b, (dims, ((), ())), preferred_element_type=F32)


def twice(matrix, axis):
    matrix = matrix.astype(BF16)
    return jnp.concatenate([matrix, matrix], axis=axis)


def resample(source, target, delta):
    source = jnp.where(delta < 0, source >> 1, source)
    target = jnp.where(delta > 0, target >> 1, target)
    return jnp.where(source == target, jnp.where(delta < 0, 0.5, 1.0), 0.0).astype(F32)


def roll(value, shift, axis):
    return pltpu.roll(value, shift % value.shape[axis], axis)


def minmod(a, b):
    return jnp.maximum(jnp.minimum(a, b), 0.0) + jnp.minimum(jnp.maximum(a, b), 0.0)


def sweep(primitives, normal, axis):
    left, right = [], []
    for value in primitives:
        before = value - roll(value, 1, axis)
        half = 0.5 * minmod(before, roll(before, -1, axis))
        left.append(roll(value + half, 1, axis))
        right.append(value - half)

    def pieces(values):
        density, speed_n, speed_t, speed_z, field_t, field_z = values
        square = normal * normal + field_t * field_t + field_z * field_z
        moment = density * speed_n
        cons = [density, moment, density * speed_t, density * speed_z, field_t, field_z]
        flux = [
            moment,
            moment * speed_n + (density + 0.5 * square) - normal * normal,
            moment * speed_t - normal * field_t,
            moment * speed_z - normal * field_z,
            field_t * speed_n - normal * speed_t,
            field_z * speed_n - normal * speed_z,
        ]
        return flux, cons, jnp.abs(speed_n) + jnp.sqrt(1.0 + square / density)

    flux_l, cons_l, signal_l = pieces(left)
    flux_r, cons_r, signal_r = pieces(right)
    fastest = jnp.maximum(signal_l, signal_r)
    return [
        0.5 * ((fl + fr) - fastest * (cr - cl))
        for fl, fr, cl, cr in zip(flux_l, flux_r, cons_l, cons_r)
    ]


def strip_choices(block, upper, sub8, odd_lane):
    same, coarse, fine = block, [], []
    sign = 1 if upper else -1
    edge = 7 if upper else 0
    for comp in range(7):
        value = block[comp]
        if comp == 6:
            pair = roll(value, 1, 0) if upper else value
        else:
            pair = 0.5 * (value + roll(value, sign, 0))
        if comp == 5:
            pair = jnp.where(odd_lane, roll(pair, 1, 1), pair)
        coarse.append(
            jnp.where(
                sub8 == edge,
                pair,
                jnp.where(sub8 == edge - sign, roll(pair, sign, 0), roll(pair, 2 * sign, 0)),
            )
        )
        fine.append(jnp.where(sub8 == edge, value, roll(value, -sign, 0)))
    return same, coarse, fine


def kernel(
    seg_count, sub_count, fields, levels, out,
    ghosted, current, row_out, row_in, col_out, col_in, line_out, line_in,
    lane_maps, row_maps, send_sem, recv_sem,
):
    seg, sub = lax.axis_index("seg"), lax.axis_index("sub")

    def place(offset):
        return (
            lax.rem(seg + (seg_count + offset[0]), seg_count),
            lax.rem(sub + (sub_count + offset[1]), sub_count),
        )

    places = [place(offset) for offset in AROUND]
    barrier = pltpu.get_barrier_semaphore()
    for target in places:
        pl.semaphore_signal(barrier, inc=1, device_id=target, device_id_type=MESH)

    level = levels[seg, sub]
    near = {offset: levels[p[0], p[1]] for offset, p in zip(AROUND, places)}
    rows = pick(level, (8, 16, 32))
    cols = pick(level, (32, 64, 128))
    ratio = pick(level, [jnp.float32(STEP_SIZE / h) for h in (4.0, 2.0, 1.0)])
    delta = {offset: near[offset] - level for offset in AROUND}

    i, j = iota((COLS, COLS), 0), iota((COLS, COLS), 1)
    for k, offset in enumerate(AROUND[:6]):
        if offset[1] == 0:
            matrix = resample(i, j, delta[offset])
        elif offset[1] == 1:
            matrix = jnp.where(j >= 125, resample(i - cols, j - COLS, delta[offset]), 0.0)
        else:
            first = j - pick(near[offset], (32, 64, 0))
            ok = (first >= 0) & (first < 3)
            matrix = jnp.where(ok, resample(i, first, delta[offset]), 0.0)
        lane_maps[k] = twice(matrix, 0)
    i, j = iota((256, 256), 0), iota((256, 256), 1)
    together = (i >> 5) == (j >> 5)
    face_rows = (i >> 5) == 6
    i, j = i & 31, j & 31
    for k, offset in enumerate(AROUND[6:]):
        d = delta[offset]
        faces = jnp.where(d < 0, jnp.where(i == 2 * j, 1.0, 0.0), resample(i, j, d))
        matrix = jnp.where(together, jnp.where(face_rows, faces, resample(i, j, d)), 0.0)
        row_maps[k] = twice(matrix, 0)
    k, i = iota((16, COLS), 0), iota((16, COLS), 1)
    to_right = k >= 8
    k = k & 7
    is_face = k >= 3
    k = k - jnp.where(is_face, 3, 0) - jnp.where(to_right, 3, 0)
    i = i - jnp.where(to_right, cols, 0)

    def column_pick(d):
        faces = jnp.where(d < 0, jnp.where(i == 2 * k, 1.0, 0.0), resample(i, k, d))
        return jnp.where(is_face, faces, resample(i, k, d))

    column_map = twice(
        jnp.where(to_right, column_pick(delta[(0, 1)]), column_pick(delta[(0, -1)])), 1
    )
    k, i = iota((16, 256), 0), iota((16, 256), 1)
    column_place = twice(
        jnp.where((k < 3) & (i == k + 253), 1.0, 0.0)
        + jnp.where((k >= 8) & (k < 11) & (i == cols + k - 8), 1.0, 0.0),
        0,
    )
    k, i = iota((8, 256), 0), iota((8, 256), 1)
    line_pick = twice(
        jnp.where(((k == 2) & (i == 0)) | ((k == 3) & (i == cols)), 1.0, 0.0), 1
    )
    i, j = iota((256, COLS), 0), iota((256, COLS), 1)
    line_map = jnp.concatenate(
        [
            twice(jnp.where(i == 2 * j, 1.0, 0.0), 0),
            twice(jnp.where(i >= 0, 1.0, 0.0), 0),
        ],
        axis=0,
    )
    k, i = iota((8, COLS), 0), iota((8, COLS), 1)
    line_place = twice(
        jnp.where(((k == 0) & (i == 0)) | ((k == 1) & (i == cols)), 1.0, 0.0), 0
    )

    sub8, lane8 = iota((8, COLS), 0), iota((8, COLS), 1)
    odd_lane = (lane8 & 1) == 1
    upper8 = sub8 >= 4
    inside8 = lane8 < cols
    row40, lane40 = iota((40, 256), 0), iota((40, 256), 1)
    corner_ok = (row40 <= rows) & (lane40 <= cols)
    row32, lane32 = iota((ROWS, COLS), 0), iota((ROWS, COLS), 1)
    cell_ok = (row32 < rows) & (lane32 < cols)

    pl.semaphore_wait(barrier, len(AROUND))

    copies = []

    def send(section, index, source, target):
        copy = pltpu.make_async_remote_copy(
            src_ref=source,
            dst_ref=target,
            send_sem=send_sem.at[section, index],
            recv_sem=recv_sem.at[section, index],
            device_id=places[index % 8],
            device_id_type=MESH,
        )
        copy.start()
        copies.append(copy)
        return copy

    for section in range(2):
        if section == 0:
            state = [jnp.where(cell_ok, fields[c], 0.0) for c in range(7)]
        else:
            state = [current[c] for c in range(7)]

        halo = []
        for k, offset in enumerate(AROUND[6:]):
            if k == 0:
                stacked = jnp.concatenate(state + [jnp.zeros((ROWS, COLS), F32)], axis=0)
                columns = dot(column_map, halves(stacked, 1), ((1,), (1,)))
                lane = iota((8, 256), 1) >> 5
            part = columns[8 * k : 8 * k + 8]
            part = jnp.where(lane == 5, roll(part, -3, 0), part)
            col_out[section, k] = dot(halves(part, 1), row_maps[k])
            halo.append(
                send(section, 6 + k, col_out.at[section, k], col_in.at[section, k])
            )
        for upper in (True, False):
            if upper:
                block = [
                    pick(level, (v[0:8], v[8:16], v[24:32])) for v in state
                ]
            else:
                block = [v[0:8] for v in state]
            choices = strip_choices(block, upper, sub8, odd_lane)
            for k in range(0, 3) if upper else range(3, 6):
                d = delta[AROUND[k]]
                chosen = [
                    jnp.where(d == 0, a, jnp.where(d < 0, b, c)) for a, b, c in zip(*choices)
                ]
                chosen.append(jnp.zeros((8, COLS), F32))
                packed = [
                    jnp.where(upper8 == upper, chosen[2 * m], roll(chosen[2 * m + 1], 4, 0))
                    for m in range(4)
                ]
                packed = jnp.concatenate(packed, axis=0)
                row_out[section, k] = dot(halves(packed, 1), lane_maps[k])
                halo.append(send(section, k, row_out.at[section, k], row_in.at[section, k]))
        for copy in halo:
            copy.wait_recv()

        received = jnp.concatenate([col_in[section, 1], col_in[section, 0]], axis=0)
        sides = dot(halves(received, 0), column_place, ((0,), (0,)))
        for c in range(7):
            def strip(k):
                block = row_in[section, k, 8 * (c // 2) : 8 * (c // 2) + 8]
                return roll(block, 4, 0) if c % 2 else block

            low = [
                jnp.where(inside8, strip(0), strip(2)),
                jnp.where(lane8 < 64, strip(2), strip(1)),
            ]
            high = [
                jnp.where(inside8, strip(3), strip(5)),
                jnp.where(lane8 < 64, strip(5), strip(4)),
            ]
            for h in range(2):
                lanes = slice(128 * h, 128 * h + 128)
                for b in range(4):
                    block = sides[32 * c + 8 * b : 32 * c + 8 * b + 8, lanes]
                    if h == 0:
                        block = jnp.where(inside8, state[c][8 * b : 8 * b + 8], block)
                    if b in (1, 2):
                        block = jnp.where(level == b - 1, high[h], block)
                    ghosted[c, 8 * b : 8 * b + 8, lanes] = block
                ghosted[c, 32:40, lanes] = jnp.where(upper8, low[h], high[h])

        density = ghosted[0]
        inverse = 1.0 / density
        speed_x, speed_y, speed_z = (ghosted[c] * inverse for c in (1, 2, 3))
        field_z, face_x, face_y = ghosted[4], ghosted[5], ghosted[6]
        centre_x = 0.5 * (face_x + roll(face_x, -1, 1))
        centre_y = 0.5 * (face_y + roll(face_y, -1, 0))
        flux_x = sweep([density, speed_x, speed_y, speed_z, centre_y, field_z], face_x, 1)
        flux_y = sweep([density, speed_y, speed_x, speed_z, centre_x, field_z], face_y, 0)
        edge = 0.25 * (
            (flux_y[4] + roll(flux_y[4], 1, 1)) - (flux_x[4] + roll(flux_x[4], 1, 0))
        )
        edge = jnp.where(corner_ok, edge, 0.0)

        tall = jnp.concatenate([edge, jnp.zeros((88, 256), F32)], axis=0)
        lines = dot(line_pick, halves(tall, 1), ((1,), (1,)))
        lines = jnp.concatenate([lines, jnp.zeros((8, 128), F32)], axis=1)
        k, i = iota((8, 256), 0), iota((8, 256), 1)
        first_row = edge[0:1]
        last_row = pick(level, (edge[8:9], edge[16:17], edge[32:33]))
        lines = jnp.where(k == 0, first_row, jnp.where(k == 1, last_row, lines))
        ends = jnp.where(k < 6, first_row, last_row)
        ends = jnp.where((k >= 4) & (i == jnp.where((k & 1) == 0, 0, cols)), ends, 0.0)
        line_out[section] = dot(
            jnp.concatenate([halves(lines, 1), halves(ends, 1)], axis=1), line_map
        )
        shared = [
            send(section, 8 + k, line_out.at[section], line_in.at[section, k])
            for k in range(8)
        ]

        change = [
            (roll(flux_x[a], -1, 1) - flux_x[a]) + (roll(flux_y[b], -1, 0) - flux_y[b])
            for a, b in ((0, 0), (1, 2), (2, 1), (3, 3), (5, 5))
        ]

        def finish(c, value):
            if section == 0:
                current[c] = jnp.where(cell_ok, value, 0.0)
            else:
                out[c] = jnp.where(cell_ok, 0.5 * (fields[c] + value), 0.0)

        for c in range(5):
            finish(c, state[c] - ratio * change[c][:ROWS, :COLS])

        for copy in shared:
            copy.wait_recv()

        def border(offset):
            back = AROUND.index((-offset[0], -offset[1]))
            return line_in[section, back], near[offset] > level

        below, w_below = border((-1, 0))
        above, w_above = border((1, 0))
        left, w_left = border((0, -1))
        right, w_right = border((0, 1))
        sides = jnp.where(
            sub8 == 0, left[3:4], jnp.where(sub8 == 1, right[2:3], 0.0)
        )
        sides = dot(halves(sides, 0), line_place, ((0,), (0,)))[:24]
        row24, lane24 = iota((24, COLS), 0), iota((24, COLS), 1)
        part = edge[:24, :COLS]
        on_low, on_high = row24 == 0, row24 == rows
        on_left, on_right = lane24 == 0, lane24 == cols

        def flag(condition):
            return jnp.where(condition, 1.0, 0.0).astype(F32)

        part = jnp.where(on_low, flag(w_below) * below[1:2] + (1.0 - flag(w_below)) * part, part)
        part = jnp.where(on_high, flag(w_above) * above[0:1] + (1.0 - flag(w_above)) * part, part)
        part = jnp.where(on_left, flag(w_left) * sides + (1.0 - flag(w_left)) * part, part)
        part = jnp.where(on_right, flag(w_right) * sides + (1.0 - flag(w_right)) * part, part)
        for vertical, beside, horizontal, v_row, h_row, offset in (
            ((below, w_below), (left, w_left), (on_low, on_left), 6, 5, (-1, -1)),
            ((below, w_below), (right, w_right), (on_low, on_right), 7, 4, (-1, 1)),
            ((above, w_above), (left, w_left), (on_high, on_left), 4, 7, (1, -1)),
            ((above, w_above), (right, w_right), (on_high, on_right), 5, 6, (1, 1)),
        ):
            far, w_far = border(offset)
            d_row = 11 - (4 + (2 if offset[0] > 0 else 0) + (1 if offset[1] > 0 else 0))
            a, b, c = flag(vertical[1]), flag(beside[1]), flag(w_far)
            count = a + b + c
            share = jnp.where(count > 2.5, jnp.float32(1.0 / 3.0), jnp.where(count > 1.5, 0.5, 1.0))
            value = share * (
                a * vertical[0][v_row : v_row + 1]
                + b * beside[0][h_row : h_row + 1]
                + c * far[d_row + 0 : d_row + 1]
            )
            keep = flag(count < 0.5)
            part = jnp.where(
                horizontal[0] & horizontal[1], keep * edge[:24, :COLS] + (1.0 - keep) * value, part
            )
        top = jnp.concatenate([part, edge[:24, COLS:]], axis=1)
        edge = jnp.concatenate([top, edge[24:]], axis=0)
        finish(5, state[5] - ratio * (roll(edge, -1, 0) - edge)[:ROWS, :COLS])
        finish(6, state[6] + ratio * (roll(edge, -1, 1) - edge)[:ROWS, :COLS])

    for copy in copies:
        copy.wait_send()


def on_device(seg_count, sub_count, fields, region_levels):
    vmem = pl.BlockSpec(memory_space=pltpu.VMEM)
    return pl.pallas_call(
        functools.partial(kernel, seg_count, sub_count),
        out_shape=jax.ShapeDtypeStruct(fields.shape, F32),
        in_specs=[vmem, pl.BlockSpec(memory_space=pltpu.SMEM)],
        out_specs=vmem,
        scratch_shapes=[
            pltpu.VMEM((7, 40, 256), F32),
            pltpu.VMEM((7, ROWS, COLS), F32),
            pltpu.VMEM((2, 6, 32, COLS), F32),
            pltpu.VMEM((2, 6, 32, COLS), F32),
            pltpu.VMEM((2, 2, 8, 256), F32),
            pltpu.VMEM((2, 2, 8, 256), F32),
            pltpu.VMEM((2, 8, COLS), F32),
            pltpu.VMEM((2, 8, 8, COLS), F32),
            pltpu.VMEM((6, 256, COLS), BF16),
            pltpu.VMEM((2, 512, 256), BF16),
            pltpu.SemaphoreType.DMA((2, 16)),
            pltpu.SemaphoreType.DMA((2, 16)),
        ],
        compiler_params=pltpu.CompilerParams(
            collective_id=0, has_side_effects=True, vmem_limit_bytes=32 * 1024 * 1024
        ),
    )(fields, region_levels)


def solution(mesh):
    body = functools.partial(on_device, mesh.shape["seg"], mesh.shape["sub"])
    return jax.shard_map(
        body,
        mesh=mesh,
        in_specs=(P(None, "seg", "sub"), P()),
        out_specs=P(None, "seg", "sub"),
        check_vma=False,
    )
```

```python
import functools

import jax
import jax.numpy as jnp
from jax import lax
from jax.experimental import pallas as pl
from jax.experimental.pallas import tpu as pltpu
from jax.sharding import PartitionSpec as P

STEP_SIZE = 0.08
MESH = pl.DeviceIdType.MESH
F32, BF16, I32 = jnp.float32, jnp.bfloat16, jnp.int32
ROWS, COLS = 32, 128
AROUND = [(1, 0), (1, 1), (1, -1), (-1, 0), (-1, 1), (-1, -1), (0, -1), (0, 1)]


def iota(shape, axis):
    return lax.broadcasted_iota(I32, shape, axis)


def pick(level, values):
    return jnp.where(level == 0, values[0], jnp.where(level == 1, values[1], values[2]))


def halves(value, axis):
    high = value.astype(BF16)
    low = (value - high.astype(F32)).astype(BF16)
    return jnp.concatenate([high, low], axis=axis)


def dot(a, b, dims=((1,), (0,))):
    return lax.dot_general(a, b, (dims, ((), ())), preferred_element_type=F32)


def twice(matrix, axis):
    matrix = matrix.astype(BF16)
    return jnp.concatenate([matrix, matrix], axis=axis)


def resample(source, target, delta):
    source = jnp.where(delta < 0, source >> 1, source)
    target = jnp.where(delta > 0, target >> 1, target)
    return jnp.where(source == target, jnp.where(delta < 0, 0.5, 1.0), 0.0).astype(F32)


def roll(value, shift, axis):
    return pltpu.roll(value, shift % value.shape[axis], axis)


def minmod(a, b):
    return jnp.maximum(jnp.minimum(a, b), 0.0) + jnp.minimum(jnp.maximum(a, b), 0.0)


def sweep(primitives, normal, axis):
    left, right = [], []
    for value in primitives:
        before = value - roll(value, 1, axis)
        half = 0.5 * minmod(before, roll(before, -1, axis))
        left.append(roll(value + half, 1, axis))
        right.append(value - half)

    def pieces(values):
        density, speed_n, speed_t, speed_z, field_t, field_z = values
        square = normal * normal + field_t * field_t + field_z * field_z
        moment = density * speed_n
        cons = [density, moment, density * speed_t, density * speed_z, field_t, field_z]
        flux = [
            moment,
            moment * speed_n + (density + 0.5 * square) - normal * normal,
            moment * speed_t - normal * field_t,
            moment * speed_z - normal * field_z,
            field_t * speed_n - normal * speed_t,
            field_z * speed_n - normal * speed_z,
        ]
        return flux, cons, jnp.abs(speed_n) + jnp.sqrt(1.0 + square / density)

    flux_l, cons_l, signal_l = pieces(left)
    flux_r, cons_r, signal_r = pieces(right)
    fastest = jnp.maximum(signal_l, signal_r)
    return [
        0.5 * ((fl + fr) - fastest * (cr - cl))
        for fl, fr, cl, cr in zip(flux_l, flux_r, cons_l, cons_r)
    ]


def strip_choices(block, upper, sub8, odd_lane):
    same, coarse, fine = block, [], []
    sign = 1 if upper else -1
    edge = 7 if upper else 0
    for comp in range(7):
        value = block[comp]
        if comp == 6:
            pair = roll(value, 1, 0) if upper else value
        else:
            pair = 0.5 * (value + roll(value, sign, 0))
        if comp == 5:
            pair = jnp.where(odd_lane, roll(pair, 1, 1), pair)
        coarse.append(
            jnp.where(
                sub8 == edge,
                pair,
                jnp.where(sub8 == edge - sign, roll(pair, sign, 0), roll(pair, 2 * sign, 0)),
            )
        )
        fine.append(jnp.where(sub8 == edge, value, roll(value, -sign, 0)))
    return same, coarse, fine


def kernel(
    seg_count, sub_count, fields_hbm, levels_hbm, out,
    fields, levels, ghosted, current, row_out, row_in, col_out, col_in, line_out, line_in,
    lane_maps, row_maps, send_sem, recv_sem, fetch_sem,
):
    fetches = [
        pltpu.make_async_copy(levels_hbm, levels, fetch_sem.at[0]),
        pltpu.make_async_copy(fields_hbm, fields, fetch_sem.at[1]),
    ]
    for fetch in fetches:
        fetch.start()
    seg, sub = lax.axis_index("seg"), lax.axis_index("sub")

    def place(offset):
        return (
            lax.rem(seg + (seg_count + offset[0]), seg_count),
            lax.rem(sub + (sub_count + offset[1]), sub_count),
        )

    places = [place(offset) for offset in AROUND]
    barrier = pltpu.get_barrier_semaphore()
    for target in places:
        pl.semaphore_signal(barrier, inc=1, device_id=target, device_id_type=MESH)

    fetches[0].wait()
    level = levels[sub, seg]
    near = {offset: levels[p[1], p[0]] for offset, p in zip(AROUND, places)}
    rows = pick(level, (8, 16, 32))
    cols = pick(level, (32, 64, 128))
    ratio = pick(level, [jnp.float32(STEP_SIZE / h) for h in (4.0, 2.0, 1.0)])
    delta = {offset: near[offset] - level for offset in AROUND}

    i, j = iota((COLS, COLS), 0), iota((COLS, COLS), 1)
    for k, offset in enumerate(AROUND[:6]):
        if offset[1] == 0:
            matrix = resample(i, j, delta[offset])
        elif offset[1] == 1:
            matrix = jnp.where(j >= 125, resample(i - cols, j - COLS, delta[offset]), 0.0)
        else:
            first = j - pick(near[offset], (32, 64, 0))
            ok = (first >= 0) & (first < 3)
            matrix = jnp.where(ok, resample(i, first, delta[offset]), 0.0)
        lane_maps[k] = twice(matrix, 0)
    i, j = iota((256, 256), 0), iota((256, 256), 1)
    together = (i >> 5) == (j >> 5)
    face_rows = (i >> 5) == 6
    i, j = i & 31, j & 31
    for k, offset in enumerate(AROUND[6:]):
        d = delta[offset]
        faces = jnp.where(d < 0, jnp.where(i == 2 * j, 1.0, 0.0), resample(i, j, d))
        matrix = jnp.where(together, jnp.where(face_rows, faces, resample(i, j, d)), 0.0)
        row_maps[k] = twice(matrix, 0)
    k, i = iota((16, COLS), 0), iota((16, COLS), 1)
    to_right = k >= 8
    k = k & 7
    is_face = k >= 3
    k = k - jnp.where(is_face, 3, 0) - jnp.where(to_right, 3, 0)
    i = i - jnp.where(to_right, cols, 0)

    def column_pick(d):
        faces = jnp.where(d < 0, jnp.where(i == 2 * k, 1.0, 0.0), resample(i, k, d))
        return jnp.where(is_face, faces, resample(i, k, d))

    column_map = twice(
        jnp.where(to_right, column_pick(delta[(0, 1)]), column_pick(delta[(0, -1)])), 1
    )
    k, i = iota((16, 256), 0), iota((16, 256), 1)
    column_place = twice(
        jnp.where((k < 3) & (i == k + 253), 1.0, 0.0)
        + jnp.where((k >= 8) & (k < 11) & (i == cols + k - 8), 1.0, 0.0),
        0,
    )
    k, i = iota((8, 256), 0), iota((8, 256), 1)
    line_pick = twice(
        jnp.where(((k == 2) & (i == 0)) | ((k == 3) & (i == cols)), 1.0, 0.0), 1
    )
    i, j = iota((256, COLS), 0), iota((256, COLS), 1)
    line_map = jnp.concatenate(
        [
            twice(jnp.where(i == 2 * j, 1.0, 0.0), 0),
            twice(jnp.where(i >= 0, 1.0, 0.0), 0),
        ],
        axis=0,
    )
    k, i = iota((8, COLS), 0), iota((8, COLS), 1)
    line_place = twice(
        jnp.where(((k == 0) & (i == 0)) | ((k == 1) & (i == cols)), 1.0, 0.0), 0
    )

    sub8, lane8 = iota((8, COLS), 0), iota((8, COLS), 1)
    odd_lane = (lane8 & 1) == 1
    upper8 = sub8 >= 4
    inside8 = lane8 < cols
    row40, lane40 = iota((40, 256), 0), iota((40, 256), 1)
    corner_ok = (row40 <= rows) & (lane40 <= cols)
    row32, lane32 = iota((ROWS, COLS), 0), iota((ROWS, COLS), 1)
    cell_ok = (row32 < rows) & (lane32 < cols)

    fetches[1].wait()
    copies = []

    def send(section, index, source, target):
        copy = pltpu.make_async_remote_copy(
            src_ref=source,
            dst_ref=target,
            send_sem=send_sem.at[section, index],
            recv_sem=recv_sem.at[section, index],
            device_id=places[index % 8],
            device_id_type=MESH,
        )
        copy.start()
        copies.append(copy)
        return copy

    for section in range(2):
        if section == 0:
            state = [jnp.where(cell_ok, fields[c], 0.0) for c in range(7)]
        else:
            state = [current[c] for c in range(7)]

        halo = []
        for k, offset in enumerate(AROUND[6:]):
            if k == 0:
                stacked = jnp.concatenate(state + [jnp.zeros((ROWS, COLS), F32)], axis=0)
                columns = dot(column_map, halves(stacked, 1), ((1,), (1,)))
                lane = iota((8, 256), 1) >> 5
            part = columns[8 * k : 8 * k + 8]
            part = jnp.where(lane == 5, roll(part, -3, 0), part)
            col_out[section, k] = dot(halves(part, 1), row_maps[k])
        for upper in (True, False):
            if upper:
                block = [
                    pick(level, (v[0:8], v[8:16], v[24:32])) for v in state
                ]
            else:
                block = [v[0:8] for v in state]
            choices = strip_choices(block, upper, sub8, odd_lane)
            for k in range(0, 3) if upper else range(3, 6):
                d = delta[AROUND[k]]
                chosen = [
                    jnp.where(d == 0, a, jnp.where(d < 0, b, c)) for a, b, c in zip(*choices)
                ]
                chosen.append(jnp.zeros((8, COLS), F32))
                packed = [
                    jnp.where(upper8 == upper, chosen[2 * m], roll(chosen[2 * m + 1], 4, 0))
                    for m in range(4)
                ]
                packed = jnp.concatenate(packed, axis=0)
                row_out[section, k] = dot(halves(packed, 1), lane_maps[k])
        if section == 0:
            pl.semaphore_wait(barrier, len(AROUND))
        for k in range(2):
            halo.append(send(section, 6 + k, col_out.at[section, k], col_in.at[section, k]))
        for k in range(6):
            halo.append(send(section, k, row_out.at[section, k], row_in.at[section, k]))
        for copy in halo:
            copy.wait_recv()

        received = jnp.concatenate([col_in[section, 1], col_in[section, 0]], axis=0)
        sides = dot(halves(received, 0), column_place, ((0,), (0,)))
        for c in range(7):
            def strip(k):
                block = row_in[section, k, 8 * (c // 2) : 8 * (c // 2) + 8]
                return roll(block, 4, 0) if c % 2 else block

            low = [
                jnp.where(inside8, strip(0), strip(2)),
                jnp.where(lane8 < 64, strip(2), strip(1)),
            ]
            high = [
                jnp.where(inside8, strip(3), strip(5)),
                jnp.where(lane8 < 64, strip(5), strip(4)),
            ]
            for h in range(2):
                lanes = slice(128 * h, 128 * h + 128)
                for b in range(4):
                    block = sides[32 * c + 8 * b : 32 * c + 8 * b + 8, lanes]
                    if h == 0:
                        block = jnp.where(inside8, state[c][8 * b : 8 * b + 8], block)
                    if b in (1, 2):
                        block = jnp.where(level == b - 1, high[h], block)
                    ghosted[c, 8 * b : 8 * b + 8, lanes] = block
                ghosted[c, 32:40, lanes] = jnp.where(upper8, low[h], high[h])

        density = ghosted[0]
        inverse = 1.0 / density
        speed_x, speed_y, speed_z = (ghosted[c] * inverse for c in (1, 2, 3))
        field_z, face_x, face_y = ghosted[4], ghosted[5], ghosted[6]
        centre_x = 0.5 * (face_x + roll(face_x, -1, 1))
        centre_y = 0.5 * (face_y + roll(face_y, -1, 0))
        flux_x = sweep([density, speed_x, speed_y, speed_z, centre_y, field_z], face_x, 1)
        flux_y = sweep([density, speed_y, speed_x, speed_z, centre_x, field_z], face_y, 0)
        edge = 0.25 * (
            (flux_y[4] + roll(flux_y[4], 1, 1)) - (flux_x[4] + roll(flux_x[4], 1, 0))
        )
        edge = jnp.where(corner_ok, edge, 0.0)

        tall = jnp.concatenate([edge, jnp.zeros((88, 256), F32)], axis=0)
        lines = dot(line_pick, halves(tall, 1), ((1,), (1,)))
        lines = jnp.concatenate([lines, jnp.zeros((8, 128), F32)], axis=1)
        k, i = iota((8, 256), 0), iota((8, 256), 1)
        first_row = edge[0:1]
        last_row = pick(level, (edge[8:9], edge[16:17], edge[32:33]))
        lines = jnp.where(k == 0, first_row, jnp.where(k == 1, last_row, lines))
        ends = jnp.where(k < 6, first_row, last_row)
        ends = jnp.where((k >= 4) & (i == jnp.where((k & 1) == 0, 0, cols)), ends, 0.0)
        line_out[section] = dot(
            jnp.concatenate([halves(lines, 1), halves(ends, 1)], axis=1), line_map
        )
        shared = [
            send(section, 8 + k, line_out.at[section], line_in.at[section, k])
            for k in range(8)
        ]

        change = [
            (roll(flux_x[a], -1, 1) - flux_x[a]) + (roll(flux_y[b], -1, 0) - flux_y[b])
            for a, b in ((0, 0), (1, 2), (2, 1), (3, 3), (5, 5))
        ]

        def finish(c, value):
            if section == 0:
                current[c] = jnp.where(cell_ok, value, 0.0)
            else:
                out[c] = jnp.where(cell_ok, 0.5 * (fields[c] + value), 0.0)

        for c in range(5):
            finish(c, state[c] - ratio * change[c][:ROWS, :COLS])

        for copy in shared:
            copy.wait_recv()

        def border(offset):
            back = AROUND.index((-offset[0], -offset[1]))
            return line_in[section, back], near[offset] > level

        below, w_below = border((-1, 0))
        above, w_above = border((1, 0))
        left, w_left = border((0, -1))
        right, w_right = border((0, 1))
        sides = jnp.where(
            sub8 == 0, left[3:4], jnp.where(sub8 == 1, right[2:3], 0.0)
        )
        sides = dot(halves(sides, 0), line_place, ((0,), (0,)))[:24]
        row24, lane24 = iota((24, COLS), 0), iota((24, COLS), 1)
        part = edge[:24, :COLS]
        on_low, on_high = row24 == 0, row24 == rows
        on_left, on_right = lane24 == 0, lane24 == cols

        def flag(condition):
            return jnp.where(condition, 1.0, 0.0).astype(F32)

        part = jnp.where(on_low, flag(w_below) * below[1:2] + (1.0 - flag(w_below)) * part, part)
        part = jnp.where(on_high, flag(w_above) * above[0:1] + (1.0 - flag(w_above)) * part, part)
        part = jnp.where(on_left, flag(w_left) * sides + (1.0 - flag(w_left)) * part, part)
        part = jnp.where(on_right, flag(w_right) * sides + (1.0 - flag(w_right)) * part, part)
        for vertical, beside, horizontal, v_row, h_row, offset in (
            ((below, w_below), (left, w_left), (on_low, on_left), 6, 5, (-1, -1)),
            ((below, w_below), (right, w_right), (on_low, on_right), 7, 4, (-1, 1)),
            ((above, w_above), (left, w_left), (on_high, on_left), 4, 7, (1, -1)),
            ((above, w_above), (right, w_right), (on_high, on_right), 5, 6, (1, 1)),
        ):
            far, w_far = border(offset)
            d_row = 11 - (4 + (2 if offset[0] > 0 else 0) + (1 if offset[1] > 0 else 0))
            a, b, c = flag(vertical[1]), flag(beside[1]), flag(w_far)
            count = a + b + c
            share = jnp.where(count > 2.5, jnp.float32(1.0 / 3.0), jnp.where(count > 1.5, 0.5, 1.0))
            value = share * (
                a * vertical[0][v_row : v_row + 1]
                + b * beside[0][h_row : h_row + 1]
                + c * far[d_row + 0 : d_row + 1]
            )
            keep = flag(count < 0.5)
            part = jnp.where(
                horizontal[0] & horizontal[1], keep * edge[:24, :COLS] + (1.0 - keep) * value, part
            )
        top = jnp.concatenate([part, edge[:24, COLS:]], axis=1)
        edge = jnp.concatenate([top, edge[24:]], axis=0)
        finish(5, state[5] - ratio * (roll(edge, -1, 0) - edge)[:ROWS, :COLS])
        finish(6, state[6] + ratio * (roll(edge, -1, 1) - edge)[:ROWS, :COLS])

    for copy in copies:
        copy.wait_send()


def on_device(seg_count, sub_count, fields, region_levels):
    vmem = pl.BlockSpec(memory_space=pltpu.VMEM)
    region_levels = region_levels.T
    fields = pltpu.with_memory_space_constraint(fields, pltpu.HBM)
    region_levels = pltpu.with_memory_space_constraint(region_levels, pltpu.HBM)
    return pl.pallas_call(
        functools.partial(kernel, seg_count, sub_count),
        out_shape=jax.ShapeDtypeStruct(fields.shape, F32),
        in_specs=[pl.BlockSpec(memory_space=pltpu.HBM)] * 2,
        out_specs=vmem,
        scratch_shapes=[
            pltpu.VMEM(fields.shape, F32),
            pltpu.SMEM(region_levels.shape, I32),
            pltpu.VMEM((7, 40, 256), F32),
            pltpu.VMEM((7, ROWS, COLS), F32),
            pltpu.VMEM((2, 6, 32, COLS), F32),
            pltpu.VMEM((2, 6, 32, COLS), F32),
            pltpu.VMEM((2, 2, 8, 256), F32),
            pltpu.VMEM((2, 2, 8, 256), F32),
            pltpu.VMEM((2, 8, COLS), F32),
            pltpu.VMEM((2, 8, 8, COLS), F32),
            pltpu.VMEM((6, 256, COLS), BF16),
            pltpu.VMEM((2, 512, 256), BF16),
            pltpu.SemaphoreType.DMA((2, 16)),
            pltpu.SemaphoreType.DMA((2, 16)),
            pltpu.SemaphoreType.DMA((2,)),
        ],
        compiler_params=pltpu.CompilerParams(
            collective_id=0, has_side_effects=True, vmem_limit_bytes=32 * 1024 * 1024
        ),
    )(fields, region_levels)


def solution(mesh):
    body = functools.partial(on_device, mesh.shape["seg"], mesh.shape["sub"])
    return jax.shard_map(
        body,
        mesh=mesh,
        in_specs=(P(None, "seg", "sub"), P()),
        out_specs=P(None, "seg", "sub"),
        check_vma=False,
    )
```

```python
import functools

import jax
import jax.numpy as jnp
from jax import lax
from jax.experimental import pallas as pl
from jax.experimental.pallas import tpu as pltpu
from jax.sharding import PartitionSpec as P

STEP_SIZE = 0.08
MESH = pl.DeviceIdType.MESH
F32, BF16, I32 = jnp.float32, jnp.bfloat16, jnp.int32
ROWS, COLS = 32, 128
AROUND = [(1, 0), (1, 1), (1, -1), (-1, 0), (-1, 1), (-1, -1), (0, -1), (0, 1)]


def iota(shape, axis):
    return lax.broadcasted_iota(I32, shape, axis)


def pick(level, values):
    return jnp.where(level == 0, values[0], jnp.where(level == 1, values[1], values[2]))


def halves(value, axis):
    high = value.astype(BF16)
    low = (value - high.astype(F32)).astype(BF16)
    return jnp.concatenate([high, low], axis=axis)


def dot(a, b, dims=((1,), (0,))):
    return lax.dot_general(a, b, (dims, ((), ())), preferred_element_type=F32)


def twice(matrix, axis):
    matrix = matrix.astype(BF16)
    return jnp.concatenate([matrix, matrix], axis=axis)


def resample(source, target, delta):
    source = jnp.where(delta < 0, source >> 1, source)
    target = jnp.where(delta > 0, target >> 1, target)
    return jnp.where(source == target, jnp.where(delta < 0, 0.5, 1.0), 0.0).astype(F32)


def roll(value, shift, axis):
    return pltpu.roll(value, shift % value.shape[axis], axis)


def minmod(a, b):
    return jnp.maximum(jnp.minimum(a, b), 0.0) + jnp.minimum(jnp.maximum(a, b), 0.0)


def sweep(primitives, normal, axis):
    left, right = [], []
    for value in primitives:
        before = value - roll(value, 1, axis)
        half = 0.5 * minmod(before, roll(before, -1, axis))
        left.append(roll(value + half, 1, axis))
        right.append(value - half)

    def pieces(values):
        density, speed_n, speed_t, speed_z, field_t, field_z = values
        square = normal * normal + field_t * field_t + field_z * field_z
        moment = density * speed_n
        cons = [density, moment, density * speed_t, density * speed_z, field_t, field_z]
        flux = [
            moment,
            moment * speed_n + (density + 0.5 * square) - normal * normal,
            moment * speed_t - normal * field_t,
            moment * speed_z - normal * field_z,
            field_t * speed_n - normal * speed_t,
            field_z * speed_n - normal * speed_z,
        ]
        return flux, cons, jnp.abs(speed_n) + jnp.sqrt(1.0 + square / density)

    flux_l, cons_l, signal_l = pieces(left)
    flux_r, cons_r, signal_r = pieces(right)
    fastest = jnp.maximum(signal_l, signal_r)
    return [
        0.5 * ((fl + fr) - fastest * (cr - cl))
        for fl, fr, cl, cr in zip(flux_l, flux_r, cons_l, cons_r)
    ]


def strip_choices(block, upper, sub8, odd_lane):
    same, coarse, fine = block, [], []
    sign = 1 if upper else -1
    edge = 7 if upper else 0
    for comp in range(7):
        value = block[comp]
        if comp == 6:
            pair = roll(value, 1, 0) if upper else value
        else:
            pair = 0.5 * (value + roll(value, sign, 0))
        if comp == 5:
            pair = jnp.where(odd_lane, roll(pair, 1, 1), pair)
        coarse.append(
            jnp.where(
                sub8 == edge,
                pair,
                jnp.where(sub8 == edge - sign, roll(pair, sign, 0), roll(pair, 2 * sign, 0)),
            )
        )
        fine.append(jnp.where(sub8 == edge, value, roll(value, -sign, 0)))
    return same, coarse, fine


def kernel(
    seg_count, sub_count, fields_hbm, levels_hbm, out,
    fields, levels, ghosted, current, row_out, row_in, corner_out, corner_in, col_out, col_in, line_out, line_in,
    lane_maps, row_maps, send_sem, recv_sem, fetch_sem,
):
    fetches = [
        pltpu.make_async_copy(levels_hbm, levels, fetch_sem.at[0]),
        pltpu.make_async_copy(fields_hbm, fields, fetch_sem.at[1]),
    ]
    for fetch in fetches:
        fetch.start()
    seg, sub = lax.axis_index("seg"), lax.axis_index("sub")

    def place(offset):
        return (
            lax.rem(seg + (seg_count + offset[0]), seg_count),
            lax.rem(sub + (sub_count + offset[1]), sub_count),
        )

    places = [place(offset) for offset in AROUND]
    barrier = pltpu.get_barrier_semaphore()
    for target in places:
        pl.semaphore_signal(barrier, inc=1, device_id=target, device_id_type=MESH)

    fetches[0].wait()
    level = levels[sub, seg]
    near = {offset: levels[p[1], p[0]] for offset, p in zip(AROUND, places)}
    rows = pick(level, (8, 16, 32))
    cols = pick(level, (32, 64, 128))
    ratio = pick(level, [jnp.float32(STEP_SIZE / h) for h in (4.0, 2.0, 1.0)])
    delta = {offset: near[offset] - level for offset in AROUND}

    i, j = iota((COLS, COLS), 0), iota((COLS, COLS), 1)
    for k, offset in enumerate(AROUND[:6]):
        if offset[1] == 0:
            matrix = resample(i, j, delta[offset])
        elif offset[1] == 1:
            matrix = jnp.where(j >= 125, resample(i - cols, j - COLS, delta[offset]), 0.0)
        else:
            first = j - pick(near[offset], (32, 64, 0))
            ok = (first >= 0) & (first < 3)
            matrix = jnp.where(ok, resample(i, first, delta[offset]), 0.0)
        lane_maps[k] = twice(matrix, 0)
    i, j = iota((256, 256), 0), iota((256, 256), 1)
    together = (i >> 5) == (j >> 5)
    face_rows = (i >> 5) == 6
    i, j = i & 31, j & 31
    for k, offset in enumerate(AROUND[6:]):
        d = delta[offset]
        faces = jnp.where(d < 0, jnp.where(i == 2 * j, 1.0, 0.0), resample(i, j, d))
        matrix = jnp.where(together, jnp.where(face_rows, faces, resample(i, j, d)), 0.0)
        row_maps[k] = twice(matrix, 0)
    k, i = iota((16, COLS), 0), iota((16, COLS), 1)
    to_right = k >= 8
    k = k & 7
    is_face = k >= 3
    k = k - jnp.where(is_face, 3, 0) - jnp.where(to_right, 3, 0)
    i = i - jnp.where(to_right, cols, 0)

    def column_pick(d):
        faces = jnp.where(d < 0, jnp.where(i == 2 * k, 1.0, 0.0), resample(i, k, d))
        return jnp.where(is_face, faces, resample(i, k, d))

    column_map = twice(
        jnp.where(to_right, column_pick(delta[(0, 1)]), column_pick(delta[(0, -1)])), 1
    )
    k, i = iota((16, 256), 0), iota((16, 256), 1)
    column_place = twice(
        jnp.where((k < 3) & (i == k + 253), 1.0, 0.0)
        + jnp.where((k >= 8) & (k < 11) & (i == cols + k - 8), 1.0, 0.0),
        0,
    )
    k, i = iota((8, 256), 0), iota((8, 256), 1)
    line_pick = twice(
        jnp.where(((k == 2) & (i == 0)) | ((k == 3) & (i == cols)), 1.0, 0.0), 1
    )
    i, j = iota((256, COLS), 0), iota((256, COLS), 1)
    line_map = jnp.concatenate(
        [
            twice(jnp.where(i == 2 * j, 1.0, 0.0), 0),
            twice(jnp.where(i >= 0, 1.0, 0.0), 0),
        ],
        axis=0,
    )
    k, i = iota((8, COLS), 0), iota((8, COLS), 1)
    line_place = twice(
        jnp.where(((k == 0) & (i == 0)) | ((k == 1) & (i == cols)), 1.0, 0.0), 0
    )

    sub8, lane8 = iota((8, COLS), 0), iota((8, COLS), 1)
    odd_lane = (lane8 & 1) == 1
    upper8 = sub8 >= 4
    inside8 = lane8 < cols
    row40, lane40 = iota((40, 256), 0), iota((40, 256), 1)
    corner_ok = (row40 <= rows) & (lane40 <= cols)
    row32, lane32 = iota((ROWS, COLS), 0), iota((ROWS, COLS), 1)
    cell_ok = (row32 < rows) & (lane32 < cols)

    fetches[1].wait()
    copies = []

    def send(section, index, source, target):
        copy = pltpu.make_async_remote_copy(
            src_ref=source,
            dst_ref=target,
            send_sem=send_sem.at[section, index],
            recv_sem=recv_sem.at[section, index],
            device_id=places[index % 8],
            device_id_type=MESH,
        )
        copy.start()
        copies.append(copy)
        return copy

    for section in range(2):
        if section == 0:
            state = [jnp.where(cell_ok, fields[c], 0.0) for c in range(7)]
        else:
            state = [current[c] for c in range(7)]

        halo = []
        for k, offset in enumerate(AROUND[6:]):
            if k == 0:
                stacked = jnp.concatenate(state + [jnp.zeros((ROWS, COLS), F32)], axis=0)
                columns = dot(column_map, halves(stacked, 1), ((1,), (1,)))
                lane = iota((8, 256), 1) >> 5
            part = columns[8 * k : 8 * k + 8]
            part = jnp.where(lane == 5, roll(part, -3, 0), part)
            part = dot(halves(part, 1), row_maps[k])
            col_out[section, k] = jnp.where(upper8, roll(part[:, COLS:], 4, 0), part[:, :COLS])
        for upper in (True, False):
            if upper:
                block = [
                    pick(level, (v[0:8], v[8:16], v[24:32])) for v in state
                ]
            else:
                block = [v[0:8] for v in state]
            choices = strip_choices(block, upper, sub8, odd_lane)
            for k in range(0, 3) if upper else range(3, 6):
                d = delta[AROUND[k]]
                chosen = [
                    jnp.where(d == 0, a, jnp.where(d < 0, b, c)) for a, b, c in zip(*choices)
                ]
                chosen.append(jnp.zeros((8, COLS), F32))
                packed = [
                    jnp.where(upper8 == upper, chosen[2 * m], roll(chosen[2 * m + 1], 4, 0))
                    for m in range(4)
                ]
                packed = jnp.concatenate(packed, axis=0)
                packed = dot(halves(packed, 1), lane_maps[k])
                if k % 3 == 0:
                    row_out[section, k // 3] = packed
                else:
                    corner = packed[0:8]
                    for m in range(1, 4):
                        corner = corner + roll(packed[8 * m : 8 * m + 8], 32 * m, 1)
                    corner_out[section, k] = corner
        if section == 0:
            pl.semaphore_wait(barrier, len(AROUND))
        for k in range(2):
            halo.append(send(section, 6 + k, col_out.at[section, k], col_in.at[section, k]))
        for k in (1, 2, 4, 5):
            halo.append(send(section, k, corner_out.at[section, k], corner_in.at[section, k]))
        for k in (0, 3):
            halo.append(
                send(section, k, row_out.at[section, k // 3], row_in.at[section, k // 3])
            )
        for copy in halo:
            copy.wait_recv()

        received = jnp.concatenate(
            [
                jnp.concatenate([part, roll(part, 4, 0)], axis=1)
                for part in (col_in[section, 1], col_in[section, 0])
            ],
            axis=0,
        )
        sides = dot(halves(received, 0), column_place, ((0,), (0,)))
        for c in range(7):
            def strip(k):
                if k % 3 == 0:
                    block = row_in[section, k // 3, 8 * (c // 2) : 8 * (c // 2) + 8]
                else:
                    block = roll(corner_in[section, k], -32 * (c // 2), 1)
                return roll(block, 4, 0) if c % 2 else block

            low = [
                jnp.where(inside8, strip(0), strip(2)),
                jnp.where(lane8 < 64, strip(2), strip(1)),
            ]
            high = [
                jnp.where(inside8, strip(3), strip(5)),
                jnp.where(lane8 < 64, strip(5), strip(4)),
            ]
            for h in range(2):
                lanes = slice(128 * h, 128 * h + 128)
                for b in range(4):
                    block = sides[32 * c + 8 * b : 32 * c + 8 * b + 8, lanes]
                    if h == 0:
                        block = jnp.where(inside8, state[c][8 * b : 8 * b + 8], block)
                    if b in (1, 2):
                        block = jnp.where(level == b - 1, high[h], block)
                    ghosted[c, 8 * b : 8 * b + 8, lanes] = block
                ghosted[c, 32:40, lanes] = jnp.where(upper8, low[h], high[h])

        density = ghosted[0]
        inverse = 1.0 / density
        speed_x, speed_y, speed_z = (ghosted[c] * inverse for c in (1, 2, 3))
        field_z, face_x, face_y = ghosted[4], ghosted[5], ghosted[6]
        centre_x = 0.5 * (face_x + roll(face_x, -1, 1))
        centre_y = 0.5 * (face_y + roll(face_y, -1, 0))
        flux_x = sweep([density, speed_x, speed_y, speed_z, centre_y, field_z], face_x, 1)
        flux_y = sweep([density, speed_y, speed_x, speed_z, centre_x, field_z], face_y, 0)
        edge = 0.25 * (
            (flux_y[4] + roll(flux_y[4], 1, 1)) - (flux_x[4] + roll(flux_x[4], 1, 0))
        )
        edge = jnp.where(corner_ok, edge, 0.0)

        tall = jnp.concatenate([edge, jnp.zeros((88, 256), F32)], axis=0)
        lines = dot(line_pick, halves(tall, 1), ((1,), (1,)))
        lines = jnp.concatenate([lines, jnp.zeros((8, 128), F32)], axis=1)
        k, i = iota((8, 256), 0), iota((8, 256), 1)
        first_row = edge[0:1]
        last_row = pick(level, (edge[8:9], edge[16:17], edge[32:33]))
        lines = jnp.where(k == 0, first_row, jnp.where(k == 1, last_row, lines))
        ends = jnp.where(k < 6, first_row, last_row)
        ends = jnp.where((k >= 4) & (i == jnp.where((k & 1) == 0, 0, cols)), ends, 0.0)
        line_out[section] = dot(
            jnp.concatenate([halves(lines, 1), halves(ends, 1)], axis=1), line_map
        )
        shared = [
            send(section, 8 + k, line_out.at[section], line_in.at[section, k])
            for k in range(8)
        ]

        change = [
            (roll(flux_x[a], -1, 1) - flux_x[a]) + (roll(flux_y[b], -1, 0) - flux_y[b])
            for a, b in ((0, 0), (1, 2), (2, 1), (3, 3), (5, 5))
        ]

        def finish(c, value):
            if section == 0:
                current[c] = jnp.where(cell_ok, value, 0.0)
            else:
                out[c] = jnp.where(cell_ok, 0.5 * (fields[c] + value), 0.0)

        for c in range(5):
            finish(c, state[c] - ratio * change[c][:ROWS, :COLS])

        for copy in shared:
            copy.wait_recv()

        def border(offset):
            back = AROUND.index((-offset[0], -offset[1]))
            return line_in[section, back], near[offset] > level

        below, w_below = border((-1, 0))
        above, w_above = border((1, 0))
        left, w_left = border((0, -1))
        right, w_right = border((0, 1))
        sides = jnp.where(
            sub8 == 0, left[3:4], jnp.where(sub8 == 1, right[2:3], 0.0)
        )
        sides = dot(halves(sides, 0), line_place, ((0,), (0,)))[:24]
        row24, lane24 = iota((24, COLS), 0), iota((24, COLS), 1)
        part = edge[:24, :COLS]
        on_low, on_high = row24 == 0, row24 == rows
        on_left, on_right = lane24 == 0, lane24 == cols

        def flag(condition):
            return jnp.where(condition, 1.0, 0.0).astype(F32)

        part = jnp.where(on_low, flag(w_below) * below[1:2] + (1.0 - flag(w_below)) * part, part)
        part = jnp.where(on_high, flag(w_above) * above[0:1] + (1.0 - flag(w_above)) * part, part)
        part = jnp.where(on_left, flag(w_left) * sides + (1.0 - flag(w_left)) * part, part)
        part = jnp.where(on_right, flag(w_right) * sides + (1.0 - flag(w_right)) * part, part)
        for vertical, beside, horizontal, v_row, h_row, offset in (
            ((below, w_below), (left, w_left), (on_low, on_left), 6, 5, (-1, -1)),
            ((below, w_below), (right, w_right), (on_low, on_right), 7, 4, (-1, 1)),
            ((above, w_above), (left, w_left), (on_high, on_left), 4, 7, (1, -1)),
            ((above, w_above), (right, w_right), (on_high, on_right), 5, 6, (1, 1)),
        ):
            far, w_far = border(offset)
            d_row = 11 - (4 + (2 if offset[0] > 0 else 0) + (1 if offset[1] > 0 else 0))
            a, b, c = flag(vertical[1]), flag(beside[1]), flag(w_far)
            count = a + b + c
            share = jnp.where(count > 2.5, jnp.float32(1.0 / 3.0), jnp.where(count > 1.5, 0.5, 1.0))
            value = share * (
                a * vertical[0][v_row : v_row + 1]
                + b * beside[0][h_row : h_row + 1]
                + c * far[d_row + 0 : d_row + 1]
            )
            keep = flag(count < 0.5)
            part = jnp.where(
                horizontal[0] & horizontal[1], keep * edge[:24, :COLS] + (1.0 - keep) * value, part
            )
        top = jnp.concatenate([part, edge[:24, COLS:]], axis=1)
        edge = jnp.concatenate([top, edge[24:]], axis=0)
        finish(5, state[5] - ratio * (roll(edge, -1, 0) - edge)[:ROWS, :COLS])
        finish(6, state[6] + ratio * (roll(edge, -1, 1) - edge)[:ROWS, :COLS])

    for copy in copies:
        copy.wait_send()


def on_device(seg_count, sub_count, fields, region_levels):
    vmem = pl.BlockSpec(memory_space=pltpu.VMEM)
    region_levels = region_levels.T
    fields = pltpu.with_memory_space_constraint(fields, pltpu.HBM)
    region_levels = pltpu.with_memory_space_constraint(region_levels, pltpu.HBM)
    return pl.pallas_call(
        functools.partial(kernel, seg_count, sub_count),
        out_shape=jax.ShapeDtypeStruct(fields.shape, F32),
        in_specs=[pl.BlockSpec(memory_space=pltpu.HBM)] * 2,
        out_specs=vmem,
        scratch_shapes=[
            pltpu.VMEM(fields.shape, F32),
            pltpu.SMEM(region_levels.shape, I32),
            pltpu.VMEM((7, 40, 256), F32),
            pltpu.VMEM((7, ROWS, COLS), F32),
            pltpu.VMEM((2, 2, 32, COLS), F32),
            pltpu.VMEM((2, 2, 32, COLS), F32),
            pltpu.VMEM((2, 6, 8, COLS), F32),
            pltpu.VMEM((2, 6, 8, COLS), F32),
            pltpu.VMEM((2, 2, 8, COLS), F32),
            pltpu.VMEM((2, 2, 8, COLS), F32),
            pltpu.VMEM((2, 8, COLS), F32),
            pltpu.VMEM((2, 8, 8, COLS), F32),
            pltpu.VMEM((6, 256, COLS), BF16),
            pltpu.VMEM((2, 512, 256), BF16),
            pltpu.SemaphoreType.DMA((2, 16)),
            pltpu.SemaphoreType.DMA((2, 16)),
            pltpu.SemaphoreType.DMA((2,)),
        ],
        compiler_params=pltpu.CompilerParams(
            collective_id=0, has_side_effects=True, vmem_limit_bytes=32 * 1024 * 1024
        ),
    )(fields, region_levels)


def solution(mesh):
    body = functools.partial(on_device, mesh.shape["seg"], mesh.shape["sub"])
    return jax.shard_map(
        body,
        mesh=mesh,
        in_specs=(P(None, "seg", "sub"), P()),
        out_specs=P(None, "seg", "sub"),
        check_vma=False,
    )
```

```python
import functools

import jax
import jax.numpy as jnp
from jax import lax
from jax.experimental import pallas as pl
from jax.experimental.pallas import tpu as pltpu
from jax.sharding import PartitionSpec as P

STEP_SIZE = 0.08
MESH = pl.DeviceIdType.MESH
F32, BF16, I32 = jnp.float32, jnp.bfloat16, jnp.int32
ROWS, COLS = 32, 128
AROUND = [(1, 0), (1, 1), (1, -1), (-1, 0), (-1, 1), (-1, -1), (0, -1), (0, 1)]


def iota(shape, axis):
    return lax.broadcasted_iota(I32, shape, axis)


def pick(level, values):
    return jnp.where(level == 0, values[0], jnp.where(level == 1, values[1], values[2]))


def halves(value, axis):
    high = value.astype(BF16)
    low = (value - high.astype(F32)).astype(BF16)
    return jnp.concatenate([high, low], axis=axis)


def dot(a, b, dims=((1,), (0,))):
    return lax.dot_general(a, b, (dims, ((), ())), preferred_element_type=F32)


def twice(matrix, axis):
    matrix = matrix.astype(BF16)
    return jnp.concatenate([matrix, matrix], axis=axis)


def resample(source, target, delta):
    source = jnp.where(delta < 0, source >> 1, source)
    target = jnp.where(delta > 0, target >> 1, target)
    return jnp.where(source == target, jnp.where(delta < 0, 0.5, 1.0), 0.0).astype(F32)


def roll(value, shift, axis):
    return pltpu.roll(value, shift % value.shape[axis], axis)


def minmod(a, b):
    return jnp.maximum(jnp.minimum(a, b), 0.0) + jnp.minimum(jnp.maximum(a, b), 0.0)


def sweep(primitives, normal, axis):
    left, right = [], []
    for value in primitives:
        before = value - roll(value, 1, axis)
        half = 0.5 * minmod(before, roll(before, -1, axis))
        left.append(roll(value + half, 1, axis))
        right.append(value - half)

    def pieces(values):
        density, speed_n, speed_t, speed_z, field_t, field_z = values
        square = normal * normal + field_t * field_t + field_z * field_z
        moment = density * speed_n
        cons = [density, moment, density * speed_t, density * speed_z, field_t, field_z]
        flux = [
            moment,
            moment * speed_n + (density + 0.5 * square) - normal * normal,
            moment * speed_t - normal * field_t,
            moment * speed_z - normal * field_z,
            field_t * speed_n - normal * speed_t,
            field_z * speed_n - normal * speed_z,
        ]
        return flux, cons, jnp.abs(speed_n) + jnp.sqrt(1.0 + square / density)

    flux_l, cons_l, signal_l = pieces(left)
    flux_r, cons_r, signal_r = pieces(right)
    fastest = jnp.maximum(signal_l, signal_r)
    return [
        0.5 * ((fl + fr) - fastest * (cr - cl))
        for fl, fr, cl, cr in zip(flux_l, flux_r, cons_l, cons_r)
    ]


def strip_choices(block, upper, sub8, odd_lane):
    same, coarse, fine = block, [], []
    sign = 1 if upper else -1
    edge = 7 if upper else 0
    for comp in range(7):
        value = block[comp]
        if comp == 6:
            pair = roll(value, 1, 0) if upper else value
        else:
            pair = 0.5 * (value + roll(value, sign, 0))
        if comp == 5:
            pair = jnp.where(odd_lane, roll(pair, 1, 1), pair)
        coarse.append(
            jnp.where(
                sub8 == edge,
                pair,
                jnp.where(sub8 == edge - sign, roll(pair, sign, 0), roll(pair, 2 * sign, 0)),
            )
        )
        fine.append(jnp.where(sub8 == edge, value, roll(value, -sign, 0)))
    return same, coarse, fine


def kernel(
    seg_count, sub_count, fields_hbm, levels_hbm, out,
    fields, levels, ghosted, current, row_out, row_in, corner_out, corner_in, col_out, col_in, line_out, line_in,
    lane_maps, row_maps, send_sem, recv_sem, fetch_sem,
):
    fetches = [
        pltpu.make_async_copy(levels_hbm, levels, fetch_sem.at[0]),
        pltpu.make_async_copy(fields_hbm, fields, fetch_sem.at[1]),
    ]
    for fetch in fetches:
        fetch.start()
    seg, sub = lax.axis_index("seg"), lax.axis_index("sub")

    def place(offset):
        return (
            lax.rem(seg + (seg_count + offset[0]), seg_count),
            lax.rem(sub + (sub_count + offset[1]), sub_count),
        )

    places = [place(offset) for offset in AROUND]
    barrier = pltpu.get_barrier_semaphore()
    for target in places:
        pl.semaphore_signal(barrier, inc=1, device_id=target, device_id_type=MESH)

    fetches[0].wait()
    level = levels[sub, seg]
    near = {offset: levels[p[1], p[0]] for offset, p in zip(AROUND, places)}
    rows = pick(level, (8, 16, 32))
    cols = pick(level, (32, 64, 128))
    ratio = pick(level, [jnp.float32(STEP_SIZE / h) for h in (4.0, 2.0, 1.0)])
    delta = {offset: near[offset] - level for offset in AROUND}

    i, j = iota((COLS, COLS), 0), iota((COLS, COLS), 1)
    for k, offset in enumerate(AROUND[:6]):
        if offset[1] == 0:
            matrix = resample(i, j, delta[offset])
        elif offset[1] == 1:
            matrix = jnp.where(j >= 125, resample(i - cols, j - COLS, delta[offset]), 0.0)
        else:
            first = j - pick(near[offset], (32, 64, 0))
            ok = (first >= 0) & (first < 3)
            matrix = jnp.where(ok, resample(i, first, delta[offset]), 0.0)
        lane_maps[k] = twice(matrix, 0)
    i, j = iota((256, 256), 0), iota((256, 256), 1)
    together = (i >> 5) == (j >> 5)
    face_rows = (i >> 5) == 6
    i, j = i & 31, j & 31
    for k, offset in enumerate(AROUND[6:]):
        d = delta[offset]
        faces = jnp.where(d < 0, jnp.where(i == 2 * j, 1.0, 0.0), resample(i, j, d))
        matrix = jnp.where(together, jnp.where(face_rows, faces, resample(i, j, d)), 0.0)
        row_maps[k] = twice(matrix, 0)
    k, i = iota((16, COLS), 0), iota((16, COLS), 1)
    to_right = k >= 8
    k = k & 7
    is_face = k >= 3
    k = k - jnp.where(is_face, 3, 0) - jnp.where(to_right, 3, 0)
    i = i - jnp.where(to_right, cols, 0)

    def column_pick(d):
        faces = jnp.where(d < 0, jnp.where(i == 2 * k, 1.0, 0.0), resample(i, k, d))
        return jnp.where(is_face, faces, resample(i, k, d))

    column_map = twice(
        jnp.where(to_right, column_pick(delta[(0, 1)]), column_pick(delta[(0, -1)])), 1
    )
    k, i = iota((16, 256), 0), iota((16, 256), 1)
    column_place = twice(
        jnp.where((k < 3) & (i == k + 253), 1.0, 0.0)
        + jnp.where((k >= 8) & (k < 11) & (i == cols + k - 8), 1.0, 0.0),
        0,
    )
    k, i = iota((8, 256), 0), iota((8, 256), 1)
    line_pick = twice(
        jnp.where(((k == 2) & (i == 0)) | ((k == 3) & (i == cols)), 1.0, 0.0), 1
    )
    i, j = iota((256, COLS), 0), iota((256, COLS), 1)
    line_map = jnp.concatenate(
        [
            twice(jnp.where(i == 2 * j, 1.0, 0.0), 0),
            twice(jnp.where(i >= 0, 1.0, 0.0), 0),
        ],
        axis=0,
    )
    k, i = iota((8, COLS), 0), iota((8, COLS), 1)
    line_place = twice(
        jnp.where(((k == 0) & (i == 0)) | ((k == 1) & (i == cols)), 1.0, 0.0), 0
    )

    sub8, lane8 = iota((8, COLS), 0), iota((8, COLS), 1)
    odd_lane = (lane8 & 1) == 1
    upper8 = sub8 >= 4
    inside8 = lane8 < cols
    row40, lane40 = iota((40, 256), 0), iota((40, 256), 1)
    corner_ok = (row40 <= rows) & (lane40 <= cols)
    row32, lane32 = iota((ROWS, COLS), 0), iota((ROWS, COLS), 1)
    cell_ok = (row32 < rows) & (lane32 < cols)

    fetches[1].wait()
    copies = []

    def send(section, index, source, target):
        copy = pltpu.make_async_remote_copy(
            src_ref=source,
            dst_ref=target,
            send_sem=send_sem.at[section, index],
            recv_sem=recv_sem.at[section, index],
            device_id=places[index % 8],
            device_id_type=MESH,
        )
        copy.start()
        copies.append(copy)
        return copy

    for c in range(7):
        current[c] = jnp.where(cell_ok, fields[c], 0.0)

    @pl.loop(0, 2)
    def _(section):
        copies.clear()
        state = [current[c] for c in range(7)]
        last = section == 1

        halo = []
        for k, offset in enumerate(AROUND[6:]):
            if k == 0:
                stacked = jnp.concatenate(state + [jnp.zeros((ROWS, COLS), F32)], axis=0)
                columns = dot(column_map, halves(stacked, 1), ((1,), (1,)))
                lane = iota((8, 256), 1) >> 5
            part = columns[8 * k : 8 * k + 8]
            part = jnp.where(lane == 5, roll(part, -3, 0), part)
            part = dot(halves(part, 1), row_maps[k])
            col_out[section, k] = jnp.where(upper8, roll(part[:, COLS:], 4, 0), part[:, :COLS])
        for upper in (True, False):
            if upper:
                block = [
                    pick(level, (v[0:8], v[8:16], v[24:32])) for v in state
                ]
            else:
                block = [v[0:8] for v in state]
            choices = strip_choices(block, upper, sub8, odd_lane)
            for k in range(0, 3) if upper else range(3, 6):
                d = delta[AROUND[k]]
                chosen = [
                    jnp.where(d == 0, a, jnp.where(d < 0, b, c)) for a, b, c in zip(*choices)
                ]
                chosen.append(jnp.zeros((8, COLS), F32))
                packed = [
                    jnp.where(upper8 == upper, chosen[2 * m], roll(chosen[2 * m + 1], 4, 0))
                    for m in range(4)
                ]
                packed = jnp.concatenate(packed, axis=0)
                packed = dot(halves(packed, 1), lane_maps[k])
                if k % 3 == 0:
                    row_out[section, k // 3] = packed
                else:
                    corner = packed[0:8]
                    for m in range(1, 4):
                        corner = corner + roll(packed[8 * m : 8 * m + 8], 32 * m, 1)
                    corner_out[section, k] = corner

        @pl.when(section == 0)
        def _():
            pl.semaphore_wait(barrier, len(AROUND))

        for k in range(2):
            halo.append(send(section, 6 + k, col_out.at[section, k], col_in.at[section, k]))
        for k in (1, 2, 4, 5):
            halo.append(send(section, k, corner_out.at[section, k], corner_in.at[section, k]))
        for k in (0, 3):
            halo.append(
                send(section, k, row_out.at[section, k // 3], row_in.at[section, k // 3])
            )
        for copy in halo:
            copy.wait_recv()

        received = jnp.concatenate(
            [
                jnp.concatenate([part, roll(part, 4, 0)], axis=1)
                for part in (col_in[section, 1], col_in[section, 0])
            ],
            axis=0,
        )
        sides = dot(halves(received, 0), column_place, ((0,), (0,)))
        for c in range(7):
            def strip(k):
                if k % 3 == 0:
                    block = row_in[section, k // 3, 8 * (c // 2) : 8 * (c // 2) + 8]
                else:
                    block = roll(corner_in[section, k], -32 * (c // 2), 1)
                return roll(block, 4, 0) if c % 2 else block

            low = [
                jnp.where(inside8, strip(0), strip(2)),
                jnp.where(lane8 < 64, strip(2), strip(1)),
            ]
            high = [
                jnp.where(inside8, strip(3), strip(5)),
                jnp.where(lane8 < 64, strip(5), strip(4)),
            ]
            for h in range(2):
                lanes = slice(128 * h, 128 * h + 128)
                for b in range(4):
                    block = sides[32 * c + 8 * b : 32 * c + 8 * b + 8, lanes]
                    if h == 0:
                        block = jnp.where(inside8, state[c][8 * b : 8 * b + 8], block)
                    if b in (1, 2):
                        block = jnp.where(level == b - 1, high[h], block)
                    ghosted[c, 8 * b : 8 * b + 8, lanes] = block
                ghosted[c, 32:40, lanes] = jnp.where(upper8, low[h], high[h])

        density = ghosted[0]
        inverse = 1.0 / density
        speed_x, speed_y, speed_z = (ghosted[c] * inverse for c in (1, 2, 3))
        field_z, face_x, face_y = ghosted[4], ghosted[5], ghosted[6]
        centre_x = 0.5 * (face_x + roll(face_x, -1, 1))
        centre_y = 0.5 * (face_y + roll(face_y, -1, 0))
        flux_x = sweep([density, speed_x, speed_y, speed_z, centre_y, field_z], face_x, 1)
        flux_y = sweep([density, speed_y, speed_x, speed_z, centre_x, field_z], face_y, 0)
        edge = 0.25 * (
            (flux_y[4] + roll(flux_y[4], 1, 1)) - (flux_x[4] + roll(flux_x[4], 1, 0))
        )
        edge = jnp.where(corner_ok, edge, 0.0)

        tall = jnp.concatenate([edge, jnp.zeros((88, 256), F32)], axis=0)
        lines = dot(line_pick, halves(tall, 1), ((1,), (1,)))
        lines = jnp.concatenate([lines, jnp.zeros((8, 128), F32)], axis=1)
        k, i = iota((8, 256), 0), iota((8, 256), 1)
        first_row = edge[0:1]
        last_row = pick(level, (edge[8:9], edge[16:17], edge[32:33]))
        lines = jnp.where(k == 0, first_row, jnp.where(k == 1, last_row, lines))
        ends = jnp.where(k < 6, first_row, last_row)
        ends = jnp.where((k >= 4) & (i == jnp.where((k & 1) == 0, 0, cols)), ends, 0.0)
        line_out[section] = dot(
            jnp.concatenate([halves(lines, 1), halves(ends, 1)], axis=1), line_map
        )
        shared = [
            send(section, 8 + k, line_out.at[section], line_in.at[section, k])
            for k in range(8)
        ]

        change = [
            (roll(flux_x[a], -1, 1) - flux_x[a]) + (roll(flux_y[b], -1, 0) - flux_y[b])
            for a, b in ((0, 0), (1, 2), (2, 1), (3, 3), (5, 5))
        ]

        def finish(c, value):
            value = jnp.where(last, 0.5 * (fields[c] + value), value)
            current[c] = jnp.where(cell_ok, value, 0.0)

        for c in range(5):
            finish(c, state[c] - ratio * change[c][:ROWS, :COLS])

        for copy in shared:
            copy.wait_recv()

        def border(offset):
            back = AROUND.index((-offset[0], -offset[1]))
            return line_in[section, back], near[offset] > level

        below, w_below = border((-1, 0))
        above, w_above = border((1, 0))
        left, w_left = border((0, -1))
        right, w_right = border((0, 1))
        sides = jnp.where(
            sub8 == 0, left[3:4], jnp.where(sub8 == 1, right[2:3], 0.0)
        )
        sides = dot(halves(sides, 0), line_place, ((0,), (0,)))[:24]
        row24, lane24 = iota((24, COLS), 0), iota((24, COLS), 1)
        part = edge[:24, :COLS]
        on_low, on_high = row24 == 0, row24 == rows
        on_left, on_right = lane24 == 0, lane24 == cols

        def flag(condition):
            return jnp.where(condition, 1.0, 0.0).astype(F32)

        part = jnp.where(on_low, flag(w_below) * below[1:2] + (1.0 - flag(w_below)) * part, part)
        part = jnp.where(on_high, flag(w_above) * above[0:1] + (1.0 - flag(w_above)) * part, part)
        part = jnp.where(on_left, flag(w_left) * sides + (1.0 - flag(w_left)) * part, part)
        part = jnp.where(on_right, flag(w_right) * sides + (1.0 - flag(w_right)) * part, part)
        for vertical, beside, horizontal, v_row, h_row, offset in (
            ((below, w_below), (left, w_left), (on_low, on_left), 6, 5, (-1, -1)),
            ((below, w_below), (right, w_right), (on_low, on_right), 7, 4, (-1, 1)),
            ((above, w_above), (left, w_left), (on_high, on_left), 4, 7, (1, -1)),
            ((above, w_above), (right, w_right), (on_high, on_right), 5, 6, (1, 1)),
        ):
            far, w_far = border(offset)
            d_row = 11 - (4 + (2 if offset[0] > 0 else 0) + (1 if offset[1] > 0 else 0))
            a, b, c = flag(vertical[1]), flag(beside[1]), flag(w_far)
            count = a + b + c
            share = jnp.where(count > 2.5, jnp.float32(1.0 / 3.0), jnp.where(count > 1.5, 0.5, 1.0))
            value = share * (
                a * vertical[0][v_row : v_row + 1]
                + b * beside[0][h_row : h_row + 1]
                + c * far[d_row + 0 : d_row + 1]
            )
            keep = flag(count < 0.5)
            part = jnp.where(
                horizontal[0] & horizontal[1], keep * edge[:24, :COLS] + (1.0 - keep) * value, part
            )
        top = jnp.concatenate([part, edge[:24, COLS:]], axis=1)
        edge = jnp.concatenate([top, edge[24:]], axis=0)
        finish(5, state[5] - ratio * (roll(edge, -1, 0) - edge)[:ROWS, :COLS])
        finish(6, state[6] + ratio * (roll(edge, -1, 1) - edge)[:ROWS, :COLS])

        for copy in copies:
            copy.wait_send()

    for c in range(7):
        out[c] = current[c]


def on_device(seg_count, sub_count, fields, region_levels):
    vmem = pl.BlockSpec(memory_space=pltpu.VMEM)
    region_levels = region_levels.T
    fields = pltpu.with_memory_space_constraint(fields, pltpu.HBM)
    region_levels = pltpu.with_memory_space_constraint(region_levels, pltpu.HBM)
    return pl.pallas_call(
        functools.partial(kernel, seg_count, sub_count),
        out_shape=jax.ShapeDtypeStruct(fields.shape, F32),
        in_specs=[pl.BlockSpec(memory_space=pltpu.HBM)] * 2,
        out_specs=vmem,
        scratch_shapes=[
            pltpu.VMEM(fields.shape, F32),
            pltpu.SMEM(region_levels.shape, I32),
            pltpu.VMEM((7, 40, 256), F32),
            pltpu.VMEM((7, ROWS, COLS), F32),
            pltpu.VMEM((2, 2, 32, COLS), F32),
            pltpu.VMEM((2, 2, 32, COLS), F32),
            pltpu.VMEM((2, 6, 8, COLS), F32),
            pltpu.VMEM((2, 6, 8, COLS), F32),
            pltpu.VMEM((2, 2, 8, COLS), F32),
            pltpu.VMEM((2, 2, 8, COLS), F32),
            pltpu.VMEM((2, 8, COLS), F32),
            pltpu.VMEM((2, 8, 8, COLS), F32),
            pltpu.VMEM((6, 256, COLS), BF16),
            pltpu.VMEM((2, 512, 256), BF16),
            pltpu.SemaphoreType.DMA((2, 16)),
            pltpu.SemaphoreType.DMA((2, 16)),
            pltpu.SemaphoreType.DMA((2,)),
        ],
        compiler_params=pltpu.CompilerParams(
            collective_id=0, has_side_effects=True, vmem_limit_bytes=32 * 1024 * 1024
        ),
    )(fields, region_levels)


def solution(mesh):
    body = functools.partial(on_device, mesh.shape["seg"], mesh.shape["sub"])
    return jax.shard_map(
        body,
        mesh=mesh,
        in_specs=(P(None, "seg", "sub"), P()),
        out_specs=P(None, "seg", "sub"),
        check_vma=False,
    )
```

```python
import functools

import jax
import jax.numpy as jnp
from jax import lax
from jax.experimental import pallas as pl
from jax.experimental.pallas import tpu as pltpu
from jax.sharding import PartitionSpec as P

STEP_SIZE = 0.08
MESH = pl.DeviceIdType.MESH
F32, BF16, I32 = jnp.float32, jnp.bfloat16, jnp.int32
ROWS, COLS = 32, 128
AROUND = [(1, 0), (1, 1), (1, -1), (-1, 0), (-1, 1), (-1, -1), (0, -1), (0, 1)]


def iota(shape, axis):
    return lax.broadcasted_iota(I32, shape, axis)


def pick(level, values):
    return jnp.where(level == 0, values[0], jnp.where(level == 1, values[1], values[2]))


def halves(value, axis):
    high = value.astype(BF16)
    low = (value - high.astype(F32)).astype(BF16)
    return jnp.concatenate([high, low], axis=axis)


def dot(a, b, dims=((1,), (0,))):
    return lax.dot_general(a, b, (dims, ((), ())), preferred_element_type=F32)


def twice(matrix, axis):
    matrix = matrix.astype(BF16)
    return jnp.concatenate([matrix, matrix], axis=axis)


def resample(source, target, delta):
    source = jnp.where(delta < 0, source >> 1, source)
    target = jnp.where(delta > 0, target >> 1, target)
    return jnp.where(source == target, jnp.where(delta < 0, 0.5, 1.0), 0.0).astype(F32)


def roll(value, shift, axis):
    return pltpu.roll(value, shift % value.shape[axis], axis)


def minmod(a, b):
    return jnp.maximum(jnp.minimum(a, b), 0.0) + jnp.minimum(jnp.maximum(a, b), 0.0)


def sweep(primitives, normal, axis):
    left, right = [], []
    for value in primitives:
        if value is None:
            left.append(None)
            right.append(None)
            continue
        before = value - roll(value, 1, axis)
        half = 0.5 * minmod(before, roll(before, -1, axis))
        left.append(roll(value + half, 1, axis))
        right.append(value - half)

    return riemann(left, right, normal)


def riemann(left, right, normal):
    def pieces(values):
        density, speed_n, speed_t, speed_z, field_t, field_z = values
        square = normal * normal + field_t * field_t + field_z * field_z
        moment = density * speed_n
        cons = [density, moment, density * speed_t, None, field_t, field_z]
        flux = [
            moment,
            moment * speed_n + (density + 0.5 * square) - normal * normal,
            moment * speed_t - normal * field_t,
            None,
            field_t * speed_n - normal * speed_t,
            None,
        ]
        if speed_z is not None:
            cons[3] = density * speed_z
            flux[3] = moment * speed_z - normal * field_z
            flux[5] = field_z * speed_n - normal * speed_z
        return flux, cons, jnp.abs(speed_n) + jnp.sqrt(1.0 + square / density)

    flux_l, cons_l, signal_l = pieces(left)
    flux_r, cons_r, signal_r = pieces(right)
    fastest = jnp.maximum(signal_l, signal_r)
    return [
        None if fl is None else 0.5 * ((fl + fr) - fastest * (cr - cl))
        for fl, fr, cl, cr in zip(flux_l, flux_r, cons_l, cons_r)
    ]


def strip_choices(block, upper, sub8, odd_lane):
    same, coarse, fine = block, [], []
    sign = 1 if upper else -1
    edge = 7 if upper else 0
    for comp in range(7):
        value = block[comp]
        if comp == 6:
            pair = roll(value, 1, 0) if upper else value
        else:
            pair = 0.5 * (value + roll(value, sign, 0))
        if comp == 5:
            pair = jnp.where(odd_lane, roll(pair, 1, 1), pair)
        coarse.append(
            jnp.where(
                sub8 == edge,
                pair,
                jnp.where(sub8 == edge - sign, roll(pair, sign, 0), roll(pair, 2 * sign, 0)),
            )
        )
        fine.append(jnp.where(sub8 == edge, value, roll(value, -sign, 0)))
    return same, coarse, fine


def kernel(
    seg_count, sub_count, fields_hbm, levels_hbm, out,
    fields, levels, ghosted, current, row_out, row_in, corner_out, corner_in, col_out, col_in,
    lane_maps, row_maps, fine_map, send_sem, recv_sem, fetch_sem,
):
    fetches = [
        pltpu.make_async_copy(levels_hbm, levels, fetch_sem.at[0]),
        pltpu.make_async_copy(fields_hbm, fields, fetch_sem.at[1]),
    ]
    for fetch in fetches:
        fetch.start()
    seg, sub = lax.axis_index("seg"), lax.axis_index("sub")

    def place(offset):
        return (
            lax.rem(seg + (seg_count + offset[0]), seg_count),
            lax.rem(sub + (sub_count + offset[1]), sub_count),
        )

    places = [place(offset) for offset in AROUND]
    barrier = pltpu.get_barrier_semaphore()
    for target in places:
        pl.semaphore_signal(barrier, inc=1, device_id=target, device_id_type=MESH)

    fetches[0].wait()
    level = levels[sub, seg]
    near = {offset: levels[p[1], p[0]] for offset, p in zip(AROUND, places)}
    rows = pick(level, (8, 16, 32))
    cols = pick(level, (32, 64, 128))
    ratio = pick(level, [jnp.float32(STEP_SIZE / h) for h in (4.0, 2.0, 1.0)])
    delta = {offset: near[offset] - level for offset in AROUND}

    i, j = iota((COLS, COLS), 0), iota((COLS, COLS), 1)
    for k, offset in enumerate(AROUND[:6]):
        if offset[1] == 0:
            matrix = resample(i, j, delta[offset])
        elif offset[1] == 1:
            matrix = jnp.where(j >= 125, resample(i - cols, j - COLS, delta[offset]), 0.0)
        else:
            first = j - pick(near[offset], (32, 64, 0))
            ok = (first >= 0) & (first < 3)
            matrix = jnp.where(ok, resample(i, first, delta[offset]), 0.0)
        lane_maps[k] = twice(matrix, 0)
    i, j = iota((256, 256), 0), iota((256, 256), 1)
    together = (i >> 5) == (j >> 5)
    face_rows = (i >> 5) == 6
    i, j = i & 31, j & 31
    for k, offset in enumerate(AROUND[6:]):
        d = delta[offset]
        faces = jnp.where(d < 0, jnp.where(i == 2 * j, 1.0, 0.0), resample(i, j, d))
        matrix = jnp.where(together, jnp.where(face_rows, faces, resample(i, j, d)), 0.0)
        row_maps[k] = twice(matrix, 0)
    source = (i >> 1) + ((i & 1) << 4)
    fine_map[...] = twice(jnp.where(together, jnp.where(source == j, 1.0, 0.0), 0.0), 0)
    k, i = iota((16, COLS), 0), iota((16, COLS), 1)
    to_right = k >= 8
    k = k & 7
    is_face = k >= 3
    k = k - jnp.where(is_face, 3, 0) - jnp.where(to_right, 3, 0)
    i = i - jnp.where(to_right, cols, 0)

    def column_pick(d):
        faces = jnp.where(d < 0, jnp.where(i == 2 * k, 1.0, 0.0), resample(i, k, d))
        return jnp.where(is_face, faces, resample(i, k, d))

    raw = jnp.where(i == jnp.where(to_right, k - 2, k - 3), 1.0, 0.0)
    is_raw = (iota((16, COLS), 0) & 7) >= 6
    column_map = twice(
        jnp.where(
            is_raw,
            raw,
            jnp.where(to_right, column_pick(delta[(0, 1)]), column_pick(delta[(0, -1)])),
        ),
        1,
    )
    k, i = iota((16, 256), 0), iota((16, 256), 1)
    column_place = twice(
        jnp.where((k < 3) & (i == k + 253), 1.0, 0.0)
        + jnp.where((k >= 8) & (k < 11) & (i == cols + k - 8), 1.0, 0.0),
        0,
    )
    i, j = iota((COLS, COLS), 0), iota((COLS, COLS), 1)
    end = jnp.where(j == 8, 0, jnp.where(j == 9, 1, 2 * COLS))
    border_map = twice(
        jnp.concatenate(
            [
                jnp.where((i >> 1) + ((i & 1) << 6) == j, 1.0, 0.0),
                jnp.where(i == end + cols - 2, 1.0, 0.0),
                jnp.where(i == end, 1.0, 0.0),
            ],
            axis=1,
        ),
        0,
    )
    k, i = iota((8, COLS), 0), iota((8, COLS), 1)
    line_place = twice(
        jnp.where(((k == 0) & (i == 0)) | ((k == 1) & (i == cols)), 1.0, 0.0), 0
    )

    sub8, lane8 = iota((8, COLS), 0), iota((8, COLS), 1)
    odd_lane = (lane8 & 1) == 1
    upper8 = sub8 >= 4
    inside8 = lane8 < cols
    in_side = (lane8 >= 80) & (lane8 < 96)

    def flag(condition):
        return jnp.where(condition, 1.0, 0.0).astype(F32)

    finer = {offset: flag(near[offset] > level) for offset in AROUND}

    def by_sublane(low, middle, high):
        return jnp.where(sub8 < 2, low, jnp.where(sub8 < 6, middle, high))

    finer_left = by_sublane(finer[(-1, -1)], finer[(0, -1)], finer[(1, -1)])
    finer_right = by_sublane(finer[(-1, 1)], finer[(0, 1)], finer[(1, 1)])
    finer_rows = by_sublane(finer[(-1, 0)], 0.0, finer[(1, 0)])
    use_left = jnp.where(lane8 == COLS - 1, finer_left, 0.0) > 0.5
    use_right = jnp.where(lane8 == cols, finer_right, 0.0) > 0.5
    use_rows = jnp.where(inside8, finer_rows, 0.0) > 0.5
    row40, lane40 = iota((40, 256), 0), iota((40, 256), 1)
    corner_ok = (row40 <= rows) & (lane40 <= cols)
    row32, lane32 = iota((ROWS, COLS), 0), iota((ROWS, COLS), 1)
    cell_ok = (row32 < rows) & (lane32 < cols)

    fetches[1].wait()
    copies = []

    def send(section, index, source, target):
        copy = pltpu.make_async_remote_copy(
            src_ref=source,
            dst_ref=target,
            send_sem=send_sem.at[section, index],
            recv_sem=recv_sem.at[section, index],
            device_id=places[index % 8],
            device_id_type=MESH,
        )
        copy.start()
        copies.append(copy)
        return copy

    for section in range(2):
        if section == 0:
            state = [jnp.where(cell_ok, fields[c], 0.0) for c in range(7)]
        else:
            state = [current[c] for c in range(7)]

        halo = []
        for k, offset in enumerate(AROUND[6:]):
            if k == 0:
                stacked = jnp.concatenate(state + [jnp.zeros((ROWS, COLS), F32)], axis=0)
                columns = dot(column_map, halves(stacked, 1), ((1,), (1,)))
                lane = iota((8, 256), 1) >> 5
            part = columns[8 * k : 8 * k + 8]
            fine = dot(halves(part, 1), fine_map[...])
            col_out[section, k, 8:16] = jnp.where(
                upper8, fine[:, :COLS], roll(fine[:, COLS:], 4, 0)
            )
            part = jnp.where(lane == 5, roll(part, -3, 0), part)
            part = dot(halves(part, 1), row_maps[k])
            col_out[section, k, 0:8] = jnp.where(
                upper8, roll(part[:, COLS:], 4, 0), part[:, :COLS]
            )
        border = []
        for v in state:
            top = pick(level, (v[0:8], v[8:16], v[24:32]))
            border.append(
                jnp.where(
                    sub8 < 2,
                    roll(top, 2, 0),
                    jnp.where(
                        sub8 < 4,
                        roll(v[0:8], 2, 0),
                        jnp.where(sub8 < 6, roll(top, 6, 0), roll(v[0:8], 6, 0)),
                    ),
                )
            )
        border = dot(halves(jnp.concatenate(border, axis=0), 1), border_map)
        ends = []
        for part in (border[:, COLS : 2 * COLS], border[:, 2 * COLS :]):
            total = part[0:8]
            for c in range(1, 7):
                total = total + roll(part[8 * c : 8 * c + 8], 16 * c, 1)
            ends.append(total)
        col_out[section, 0, 16:24] = ends[1]
        col_out[section, 1, 16:24] = ends[0]
        for group in range(2):
            up = down = jnp.zeros((8, COLS), F32)
            for q in range(4 if group == 0 else 3):
                c = 4 * group + q
                part = roll(border[8 * c : 8 * c + 8, :COLS], 2 * q, 0)
                up = jnp.where((sub8 >> 1) == q, part, up)
                down = jnp.where((sub8 >> 1) == ((3 + q) & 3), part, down)
            row_out[section, 0, 32 + 8 * group : 40 + 8 * group] = up
            row_out[section, 1, 32 + 8 * group : 40 + 8 * group] = down
        for upper in (True, False):
            if upper:
                block = [
                    pick(level, (v[0:8], v[8:16], v[24:32])) for v in state
                ]
            else:
                block = [v[0:8] for v in state]
            choices = strip_choices(block, upper, sub8, odd_lane)
            for k in range(0, 3) if upper else range(3, 6):
                d = delta[AROUND[k]]
                chosen = [
                    jnp.where(d == 0, a, jnp.where(d < 0, b, c)) for a, b, c in zip(*choices)
                ]
                chosen.append(jnp.zeros((8, COLS), F32))
                packed = [
                    jnp.where(upper8 == upper, chosen[2 * m], roll(chosen[2 * m + 1], 4, 0))
                    for m in range(4)
                ]
                packed = jnp.concatenate(packed, axis=0)
                packed = dot(halves(packed, 1), lane_maps[k])
                if k % 3 == 0:
                    row_out[section, k // 3, 0:32] = packed
                else:
                    corner = packed[0:8]
                    for m in range(1, 4):
                        corner = corner + roll(packed[8 * m : 8 * m + 8], 32 * m, 1)
                    corner_out[section, k] = corner + ends[0 if k % 3 == 1 else 1]
        if section == 0:
            pl.semaphore_wait(barrier, len(AROUND))
        for k in range(2):
            halo.append(send(section, 6 + k, col_out.at[section, k], col_in.at[section, k]))
        for k in (1, 2, 4, 5):
            halo.append(send(section, k, corner_out.at[section, k], corner_in.at[section, k]))
        for k in (0, 3):
            halo.append(
                send(section, k, row_out.at[section, k // 3], row_in.at[section, k // 3])
            )
        for copy in halo:
            copy.wait_recv()

        received = jnp.concatenate(
            [
                jnp.concatenate([part, roll(part, 4, 0)], axis=1)
                for part in (col_in[section, 1, 0:8], col_in[section, 0, 0:8])
            ],
            axis=0,
        )
        sides = dot(halves(received, 0), column_place, ((0,), (0,)))
        for c in range(7):
            def strip(k):
                if k % 3 == 0:
                    block = row_in[section, k // 3, 8 * (c // 2) : 8 * (c // 2) + 8]
                else:
                    block = roll(corner_in[section, k], -32 * (c // 2), 1)
                return roll(block, 4, 0) if c % 2 else block

            low = [
                jnp.where(inside8, strip(0), strip(2)),
                jnp.where(lane8 < 64, strip(2), strip(1)),
            ]
            high = [
                jnp.where(inside8, strip(3), strip(5)),
                jnp.where(lane8 < 64, strip(5), strip(4)),
            ]
            for h in range(2):
                lanes = slice(128 * h, 128 * h + 128)
                for b in range(4):
                    block = sides[32 * c + 8 * b : 32 * c + 8 * b + 8, lanes]
                    if h == 0:
                        block = jnp.where(inside8, state[c][8 * b : 8 * b + 8], block)
                    if b in (1, 2):
                        block = jnp.where(level == b - 1, high[h], block)
                    ghosted[c, 8 * b : 8 * b + 8, lanes] = block
                ghosted[c, 32:40, lanes] = jnp.where(upper8, low[h], high[h])

        density = ghosted[0]
        inverse = 1.0 / density
        speed_x, speed_y, speed_z = (ghosted[c] * inverse for c in (1, 2, 3))
        field_z, face_x, face_y = ghosted[4], ghosted[5], ghosted[6]
        centre_x = 0.5 * (face_x + roll(face_x, -1, 1))
        centre_y = 0.5 * (face_y + roll(face_y, -1, 0))
        flux_x = sweep([density, speed_x, speed_y, speed_z, centre_y, field_z], face_x, 1)
        flux_y = sweep([density, speed_y, speed_x, speed_z, centre_x, field_z], face_y, 0)
        edge = 0.25 * (
            (flux_y[4] + roll(flux_y[4], 1, 1)) - (flux_x[4] + roll(flux_x[4], 1, 0))
        )
        edge = jnp.where(corner_ok, edge, 0.0)

        from_left = by_sublane(
            corner_in[section, 1], col_in[section, 1, 16:24], corner_in[section, 4]
        )
        from_right = by_sublane(
            corner_in[section, 2], col_in[section, 0, 16:24], corner_in[section, 5]
        )
        from_right = jnp.where(level == 0, roll(from_right, 32, 1), roll(from_right, 64, 1))
        beside = []
        for k in (1, 0):
            part = col_in[section, k, 8:16]
            part = jnp.concatenate([part, roll(part, 4, 0)], axis=1)
            beside.append(roll(part, 2, 0) if k == 1 else part)
        own_sides = jnp.where(sub8[:, :1] < 4, columns[6:7], columns[15:16])
        sub_wide = iota((8, 256), 0)

        def side_window(odd):
            left, right = (roll(v, -16, 1) if odd else v for v in beside)
            left = jnp.where(finer[(0, -1)] > 0.5, left, received[2:3])
            right = jnp.where(finer[(0, 1)] > 0.5, right, received[8:9])
            return jnp.where(sub_wide < 2, left, jnp.where(sub_wide < 6, own_sides, right))

        side_windows = [side_window(False), side_window(True)]
        swapped = (0, 2, 1, 3, 4, 6, 5)

        def windows(c):
            first = jnp.where(lane8 == COLS - 1, ghosted[c, 39:40, COLS:], ghosted[c, 39:40, :COLS])
            second = jnp.where(lane8 == COLS - 1, ghosted[c, 0:1, COLS:], ghosted[c, 0:1, :COLS])

            def at_level(low, high):
                value = jnp.where(level == 0, ghosted[c, low : low + 1], ghosted[c, high : high + 1])
                return jnp.where(lane8 == COLS - 1, value[:, COLS:], value[:, :COLS])

            base = jnp.where(
                sub8 < 2,
                first,
                jnp.where(sub8 < 4, second, jnp.where(sub8 < 6, at_level(7, 15), at_level(8, 16))),
            )
            q, rows_of = c % 4, slice(32 + 8 * (c // 4), 40 + 8 * (c // 4))
            fine = jnp.where(
                upper8,
                roll(row_in[section, 1, rows_of], -2 * q, 0),
                roll(row_in[section, 0, rows_of], -2 * q, 0),
            )
            pair = []
            for odd in range(2):
                value = jnp.where(use_rows, roll(fine, 64, 1) if odd else fine, base)
                value = jnp.where(use_left, roll(from_left, 127 - (16 * c + 8 + odd), 1), value)
                value = jnp.where(use_right, roll(from_right, -(16 * c + 8 + odd), 1), value)
                t = swapped[c]
                half = side_windows[odd][:, COLS * (t // 4) : COLS * (t // 4) + COLS]
                pair.append(jnp.where(in_side, roll(half, 80 - 32 * (t % 4), 1), value))
            return pair

        even, odd = zip(*[windows(c) if c != 3 else (None, None) for c in range(7)])

        def primitives_of(v):
            inv = 1.0 / v[0]
            return v[0], v[1] * inv, v[2] * inv, v[4], v[5], v[6]

        even, odd = primitives_of(even), primitives_of(odd)
        odd_before = [roll(v, 1, 1) for v in odd]
        even_before = [roll(v, 1, 1) for v in even]

        def along_rows(v, centre):
            return sweep([v[0], v[2], v[1], None, centre, v[3]], v[5], 0)[4]

        fine_y = along_rows(even, 0.5 * (even[4] + odd[4])) + along_rows(
            odd_before, 0.5 * (odd_before[4] + even[4])
        )

        def across(v):
            centre = 0.5 * (v[5] + roll(v[5], -1, 0))
            return [v[0], v[1], v[2], centre, v[3]]

        left, right = [], []
        for a, b, c, d in zip(*[across(v) for v in (even_before, odd_before, even, odd)]):
            middle = c - b
            left.append(b + 0.5 * minmod(b - a, middle))
            right.append(c - 0.5 * minmod(middle, d - c))
        left.insert(3, None)
        right.insert(3, None)
        fine_x = riemann(left, right, even[4])[4]
        fine_edge = 0.25 * (fine_y - (fine_x + roll(fine_x, 1, 0)))

        change = [
            (roll(flux_x[a], -1, 1) - flux_x[a]) + (roll(flux_y[b], -1, 0) - flux_y[b])
            for a, b in ((0, 0), (1, 2), (2, 1), (3, 3), (5, 5))
        ]

        def finish(c, value):
            if section == 0:
                current[c] = jnp.where(cell_ok, value, 0.0)
            else:
                out[c] = jnp.where(cell_ok, 0.5 * (fields[c] + value), 0.0)

        for c in range(5):
            finish(c, state[c] - ratio * change[c][:ROWS, :COLS])

        sides = jnp.where(sub8 == 0, -fine_edge[2:3], jnp.where(sub8 == 1, -fine_edge[6:7], 0.0))
        sides = jnp.where(in_side, sides, 0.0)
        sides = dot(halves(sides, 0), line_place, ((0,), (0,)))[80:104]
        row24, lane24 = iota((24, COLS), 0), iota((24, COLS), 1)
        part = edge[:24, :COLS]
        on_low, on_high = row24 == 0, row24 == rows
        on_left, on_right = lane24 == 0, lane24 == cols

        def border_flags(row):
            side = finer[(row, 0)]
            first = jnp.maximum(jnp.maximum(side, finer[(0, -1)]), finer[(row, -1)])
            final = jnp.maximum(jnp.maximum(side, finer[(0, 1)]), finer[(row, 1)])
            value = jnp.where(on_left, first, jnp.where(on_right, final, side))
            return jnp.where(lane24 <= cols, value, 0.0) > 0.5

        part = jnp.where(on_left & (finer[(0, -1)] > 0.5), sides, part)
        part = jnp.where(on_right & (finer[(0, 1)] > 0.5), sides, part)
        part = jnp.where(on_low & border_flags(-1), fine_edge[2:3], part)
        part = jnp.where(on_high & border_flags(1), fine_edge[6:7], part)
        top = jnp.concatenate([part, edge[:24, COLS:]], axis=1)
        edge = jnp.concatenate([top, edge[24:]], axis=0)
        finish(5, state[5] - ratio * (roll(edge, -1, 0) - edge)[:ROWS, :COLS])
        finish(6, state[6] + ratio * (roll(edge, -1, 1) - edge)[:ROWS, :COLS])

    for copy in copies:
        copy.wait_send()


def on_device(seg_count, sub_count, fields, region_levels):
    vmem = pl.BlockSpec(memory_space=pltpu.VMEM)
    region_levels = region_levels.T
    fields = pltpu.with_memory_space_constraint(fields, pltpu.HBM)
    region_levels = pltpu.with_memory_space_constraint(region_levels, pltpu.HBM)
    return pl.pallas_call(
        functools.partial(kernel, seg_count, sub_count),
        out_shape=jax.ShapeDtypeStruct(fields.shape, F32),
        in_specs=[pl.BlockSpec(memory_space=pltpu.HBM)] * 2,
        out_specs=vmem,
        scratch_shapes=[
            pltpu.VMEM(fields.shape, F32),
            pltpu.SMEM(region_levels.shape, I32),
            pltpu.VMEM((7, 40, 256), F32),
            pltpu.VMEM((7, ROWS, COLS), F32),
            pltpu.VMEM((2, 2, 48, COLS), F32),
            pltpu.VMEM((2, 2, 48, COLS), F32),
            pltpu.VMEM((2, 6, 8, COLS), F32),
            pltpu.VMEM((2, 6, 8, COLS), F32),
            pltpu.VMEM((2, 2, 24, COLS), F32),
            pltpu.VMEM((2, 2, 24, COLS), F32),
            pltpu.VMEM((6, 256, COLS), BF16),
            pltpu.VMEM((2, 512, 256), BF16),
            pltpu.VMEM((512, 256), BF16),
            pltpu.SemaphoreType.DMA((2, 8)),
            pltpu.SemaphoreType.DMA((2, 8)),
            pltpu.SemaphoreType.DMA((2,)),
        ],
        compiler_params=pltpu.CompilerParams(
            collective_id=0, has_side_effects=True, vmem_limit_bytes=32 * 1024 * 1024
        ),
    )(fields, region_levels)


def solution(mesh):
    body = functools.partial(on_device, mesh.shape["seg"], mesh.shape["sub"])
    return jax.shard_map(
        body,
        mesh=mesh,
        in_specs=(P(None, "seg", "sub"), P()),
        out_specs=P(None, "seg", "sub"),
        check_vma=False,
    )
```

```python
import functools

import jax
import jax.numpy as jnp
from jax import lax
from jax.experimental import pallas as pl
from jax.experimental.pallas import tpu as pltpu
from jax.sharding import PartitionSpec as P

STEP_SIZE = 0.08
MESH = pl.DeviceIdType.MESH
F32, BF16, I32 = jnp.float32, jnp.bfloat16, jnp.int32
ROWS, COLS = 32, 128
AROUND = [(1, 0), (1, 1), (1, -1), (-1, 0), (-1, 1), (-1, -1), (0, -1), (0, 1)]


def iota(shape, axis):
    return lax.broadcasted_iota(I32, shape, axis)


def pick(level, values):
    return jnp.where(level == 0, values[0], jnp.where(level == 1, values[1], values[2]))


def halves(value, axis):
    high = value.astype(BF16)
    low = (value - high.astype(F32)).astype(BF16)
    return jnp.concatenate([high, low], axis=axis)


def dot(a, b, dims=((1,), (0,))):
    return lax.dot_general(a, b, (dims, ((), ())), preferred_element_type=F32)


def twice(matrix, axis):
    matrix = matrix.astype(BF16)
    return jnp.concatenate([matrix, matrix], axis=axis)


def resample(source, target, delta):
    source = jnp.where(delta < 0, source >> 1, source)
    target = jnp.where(delta > 0, target >> 1, target)
    return jnp.where(source == target, jnp.where(delta < 0, 0.5, 1.0), 0.0).astype(F32)


def roll(value, shift, axis):
    return pltpu.roll(value, shift % value.shape[axis], axis)


def minmod(a, b):
    return jnp.maximum(jnp.minimum(a, b), 0.0) + jnp.minimum(jnp.maximum(a, b), 0.0)


def sweep(primitives, normal, axis):
    left, right = [], []
    for value in primitives:
        if value is None:
            left.append(None)
            right.append(None)
            continue
        before = value - roll(value, 1, axis)
        half = 0.5 * minmod(before, roll(before, -1, axis))
        left.append(roll(value + half, 1, axis))
        right.append(value - half)

    return riemann(left, right, normal)


def riemann(left, right, normal):
    def pieces(values):
        density, speed_n, speed_t, speed_z, field_t, field_z = values
        square = normal * normal + field_t * field_t + field_z * field_z
        moment = density * speed_n
        cons = [density, moment, density * speed_t, None, field_t, field_z]
        flux = [
            moment,
            moment * speed_n + (density + 0.5 * square) - normal * normal,
            moment * speed_t - normal * field_t,
            None,
            field_t * speed_n - normal * speed_t,
            None,
        ]
        if speed_z is not None:
            cons[3] = density * speed_z
            flux[3] = moment * speed_z - normal * field_z
            flux[5] = field_z * speed_n - normal * speed_z
        return flux, cons, jnp.abs(speed_n) + jnp.sqrt(1.0 + square / density)

    flux_l, cons_l, signal_l = pieces(left)
    flux_r, cons_r, signal_r = pieces(right)
    fastest = jnp.maximum(signal_l, signal_r)
    return [
        None if fl is None else 0.5 * ((fl + fr) - fastest * (cr - cl))
        for fl, fr, cl, cr in zip(flux_l, flux_r, cons_l, cons_r)
    ]


def strip_choices(block, upper, sub8, odd_lane):
    same, coarse, fine = block, [], []
    sign = 1 if upper else -1
    edge = 7 if upper else 0
    for comp in range(7):
        value = block[comp]
        if comp == 6:
            pair = roll(value, 1, 0) if upper else value
        else:
            pair = 0.5 * (value + roll(value, sign, 0))
        if comp == 5:
            pair = jnp.where(odd_lane, roll(pair, 1, 1), pair)
        coarse.append(
            jnp.where(
                sub8 == edge,
                pair,
                jnp.where(sub8 == edge - sign, roll(pair, sign, 0), roll(pair, 2 * sign, 0)),
            )
        )
        fine.append(jnp.where(sub8 == edge, value, roll(value, -sign, 0)))
    return same, coarse, fine


def kernel(
    seg_count, sub_count, fields_hbm, levels_hbm, out,
    fields, levels, ghosted, current, row_out, row_in, corner_out, corner_in, col_out, col_in,
    lane_maps, row_maps, fine_map, border_map, send_sem, recv_sem, fetch_sem,
):
    fetches = [
        pltpu.make_async_copy(levels_hbm, levels, fetch_sem.at[0]),
        pltpu.make_async_copy(fields_hbm, fields, fetch_sem.at[1]),
    ]
    for fetch in fetches:
        fetch.start()
    seg, sub = lax.axis_index("seg"), lax.axis_index("sub")

    def place(offset):
        return (
            lax.rem(seg + (seg_count + offset[0]), seg_count),
            lax.rem(sub + (sub_count + offset[1]), sub_count),
        )

    places = [place(offset) for offset in AROUND]
    barrier = pltpu.get_barrier_semaphore()
    for target in places:
        pl.semaphore_signal(barrier, inc=1, device_id=target, device_id_type=MESH)

    i, j = iota((COLS, COLS), 0), iota((COLS, COLS), 1)
    together = (i >> 5) == (j >> 5)
    comp_six = (i >> 5) == 2
    source = (i & ~31) + ((i & 31) >> 1) + ((i & 1) << 4)
    fine_map[...] = twice(jnp.where(source == j, 1.0, 0.0), 0)
    end = jnp.where(j == 8, 0, jnp.where(j == 9, 1, 2 * COLS))
    border_map[:, 0:COLS] = twice(jnp.where((i >> 1) + ((i & 1) << 6) == j, 1.0, 0.0), 0)
    border_map[:, 2 * COLS :] = twice(jnp.where(i == end, 1.0, 0.0), 0)

    fetches[0].wait()
    level = levels[sub, seg]
    near = {offset: levels[p[1], p[0]] for offset, p in zip(AROUND, places)}
    rows = pick(level, (8, 16, 32))
    cols = pick(level, (32, 64, 128))
    ratio = pick(level, [jnp.float32(STEP_SIZE / h) for h in (4.0, 2.0, 1.0)])
    delta = {offset: near[offset] - level for offset in AROUND}

    for k, offset in enumerate(AROUND[:6]):
        if offset[1] == 0:
            matrix = resample(i, j, delta[offset])
        elif offset[1] == 1:
            matrix = jnp.where(j >= 125, resample(i - cols, j - COLS, delta[offset]), 0.0)
        else:
            first = j - pick(near[offset], (32, 64, 0))
            ok = (first >= 0) & (first < 3)
            matrix = jnp.where(ok, resample(i, first, delta[offset]), 0.0)
        lane_maps[k] = twice(matrix, 0)
    border_map[:, COLS : 2 * COLS] = twice(jnp.where(i == end + cols - 2, 1.0, 0.0), 0)
    i, j = i & 31, j & 31
    for k, offset in enumerate(AROUND[6:]):
        d = delta[offset]
        matrix = jnp.where(together, resample(i, j, d), 0.0)
        row_maps[k, 0] = twice(matrix, 0)
        faces = jnp.where(together, jnp.where(i == 2 * j, 1.0, 0.0), 0.0)
        row_maps[k, 1] = twice(jnp.where(comp_six & (d < 0), faces, matrix), 0)
    k, i = iota((16, COLS), 0), iota((16, COLS), 1)
    to_right = k >= 8
    k = k & 7
    is_face = k >= 3
    k = k - jnp.where(is_face, 3, 0) - jnp.where(to_right, 3, 0)
    i = i - jnp.where(to_right, cols, 0)

    def column_pick(d):
        faces = jnp.where(d < 0, jnp.where(i == 2 * k, 1.0, 0.0), resample(i, k, d))
        return jnp.where(is_face, faces, resample(i, k, d))

    raw = jnp.where(i == jnp.where(to_right, k - 2, k - 3), 1.0, 0.0)
    is_raw = (iota((16, COLS), 0) & 7) >= 6
    column_map = twice(
        jnp.where(
            is_raw,
            raw,
            jnp.where(to_right, column_pick(delta[(0, 1)]), column_pick(delta[(0, -1)])),
        ),
        1,
    )
    k, i = iota((16, 256), 0), iota((16, 256), 1)
    column_place = twice(
        jnp.where((k < 3) & (i == k + 253), 1.0, 0.0)
        + jnp.where((k >= 8) & (k < 11) & (i == cols + k - 8), 1.0, 0.0),
        0,
    )
    k, i = iota((8, COLS), 0), iota((8, COLS), 1)
    line_place = twice(
        jnp.where(((k == 0) & (i == 0)) | ((k == 1) & (i == cols)), 1.0, 0.0), 0
    )

    sub8, lane8 = iota((8, COLS), 0), iota((8, COLS), 1)
    odd_lane = (lane8 & 1) == 1
    upper8 = sub8 >= 4
    inside8 = lane8 < cols
    in_side = (lane8 >= 80) & (lane8 < 96)

    def flag(condition):
        return jnp.where(condition, 1.0, 0.0).astype(F32)

    finer = {offset: flag(near[offset] > level) for offset in AROUND}

    def by_sublane(low, middle, high):
        return jnp.where(sub8 < 2, low, jnp.where(sub8 < 6, middle, high))

    finer_left = by_sublane(finer[(-1, -1)], finer[(0, -1)], finer[(1, -1)])
    finer_right = by_sublane(finer[(-1, 1)], finer[(0, 1)], finer[(1, 1)])
    finer_rows = by_sublane(finer[(-1, 0)], 0.0, finer[(1, 0)])
    use_left = jnp.where(lane8 == COLS - 1, finer_left, 0.0) > 0.5
    use_right = jnp.where(lane8 == cols, finer_right, 0.0) > 0.5
    use_rows = jnp.where(inside8, finer_rows, 0.0) > 0.5
    row40, lane40 = iota((40, 256), 0), iota((40, 256), 1)
    corner_ok = (row40 <= rows) & (lane40 <= cols)
    row32, lane32 = iota((ROWS, COLS), 0), iota((ROWS, COLS), 1)
    cell_ok = (row32 < rows) & (lane32 < cols)

    fetches[1].wait()
    copies = []

    def send(section, index, source, target):
        copy = pltpu.make_async_remote_copy(
            src_ref=source,
            dst_ref=target,
            send_sem=send_sem.at[section, index],
            recv_sem=recv_sem.at[section, index],
            device_id=places[index % 8],
            device_id_type=MESH,
        )
        copy.start()
        copies.append(copy)
        return copy

    for section in range(2):
        if section == 0:
            state = [jnp.where(cell_ok, fields[c], 0.0) for c in range(7)]
        else:
            state = [current[c] for c in range(7)]

        halo = []
        tops = [pick(level, (v[0:8], v[8:16], v[24:32])) for v in state]
        lows = [v[0:8] for v in state]
        border = [
            jnp.where(
                sub8 < 2,
                roll(top, 2, 0),
                jnp.where(
                    sub8 < 4,
                    roll(low, 2, 0),
                    jnp.where(sub8 < 6, roll(top, 6, 0), roll(low, 6, 0)),
                ),
            )
            for top, low in zip(tops, lows)
        ]
        stacked = jnp.concatenate(state + [jnp.zeros((ROWS, COLS), F32)], axis=0)
        columns = dot(column_map, halves(stacked, 1), ((1,), (1,)))
        border = dot(halves(jnp.concatenate(border, axis=0), 1), border_map[...])
        ends = []
        for part in (border[:, COLS : 2 * COLS], border[:, 2 * COLS :]):
            total = part[0:8]
            for c in range(1, 7):
                total = total + roll(part[8 * c : 8 * c + 8], 16 * c, 1)
            ends.append(total)
        for k in range(2):
            part = columns[8 * k : 8 * k + 8]
            first, second = part[:, :COLS], part[:, COLS:]
            fine = dot(
                jnp.concatenate([halves(first, 1), halves(second, 1)], axis=0), fine_map[...]
            )
            col_out[section, k, 8:16] = jnp.where(upper8, fine[:8], roll(fine[8:], 4, 0))
            second = jnp.where((lane8 >> 5) == 1, roll(second, -3, 0), second)
            first = dot(halves(first, 1), row_maps[k, 0])
            second = dot(halves(second, 1), row_maps[k, 1])
            col_out[section, k, 0:8] = jnp.where(upper8, roll(second, 4, 0), first)
            col_out[section, k, 16:24] = ends[1 - k]
        if section == 0:
            pl.semaphore_wait(barrier, len(AROUND))
        for k in range(2):
            halo.append(send(section, 6 + k, col_out.at[section, k], col_in.at[section, k]))
        for upper in (True, False):
            choices = strip_choices(tops if upper else lows, upper, sub8, odd_lane)
            base = 0 if upper else 3
            for k in (base + 1, base + 2, base):
                d = delta[AROUND[k]]
                chosen = [
                    jnp.where(d == 0, a, jnp.where(d < 0, b, c)) for a, b, c in zip(*choices)
                ]
                chosen.append(jnp.zeros((8, COLS), F32))
                packed = [
                    jnp.where(upper8 == upper, chosen[2 * m], roll(chosen[2 * m + 1], 4, 0))
                    for m in range(4)
                ]
                packed = jnp.concatenate(packed, axis=0)
                packed = dot(halves(packed, 1), lane_maps[k])
                if k != base:
                    corner = packed[0:8] + ends[k - base - 1]
                    for m in range(1, 4):
                        corner = corner + roll(packed[8 * m : 8 * m + 8], 32 * m, 1)
                    corner_out[section, k] = corner
                    halo.append(
                        send(section, k, corner_out.at[section, k], corner_in.at[section, k])
                    )
                    continue
                row_out[section, k // 3, 0:32] = packed
                for group in range(2):
                    block = jnp.zeros((8, COLS), F32)
                    for q in range(4 if group == 0 else 3):
                        c = 4 * group + q
                        part = roll(border[8 * c : 8 * c + 8, :COLS], 2 * q, 0)
                        place_of = q if upper else (3 + q) & 3
                        block = jnp.where((sub8 >> 1) == place_of, part, block)
                    row_out[section, k // 3, 32 + 8 * group : 40 + 8 * group] = block
                halo.append(
                    send(section, k, row_out.at[section, k // 3], row_in.at[section, k // 3])
                )
        for copy in halo:
            copy.wait_recv()

        received = jnp.concatenate(
            [
                jnp.concatenate([part, roll(part, 4, 0)], axis=1)
                for part in (col_in[section, 1, 0:8], col_in[section, 0, 0:8])
            ],
            axis=0,
        )
        sides = dot(halves(received, 0), column_place, ((0,), (0,)))
        for c in range(7):
            def strip(k):
                if k % 3 == 0:
                    block = row_in[section, k // 3, 8 * (c // 2) : 8 * (c // 2) + 8]
                else:
                    block = roll(corner_in[section, k], -32 * (c // 2), 1)
                return roll(block, 4, 0) if c % 2 else block

            low = [
                jnp.where(inside8, strip(0), strip(2)),
                jnp.where(lane8 < 64, strip(2), strip(1)),
            ]
            high = [
                jnp.where(inside8, strip(3), strip(5)),
                jnp.where(lane8 < 64, strip(5), strip(4)),
            ]
            for h in range(2):
                lanes = slice(128 * h, 128 * h + 128)
                for b in range(4):
                    block = sides[32 * c + 8 * b : 32 * c + 8 * b + 8, lanes]
                    if h == 0:
                        block = jnp.where(inside8, state[c][8 * b : 8 * b + 8], block)
                    if b in (1, 2):
                        block = jnp.where(level == b - 1, high[h], block)
                    ghosted[c, 8 * b : 8 * b + 8, lanes] = block
                ghosted[c, 32:40, lanes] = jnp.where(upper8, low[h], high[h])

        density = ghosted[0]
        inverse = 1.0 / density
        speed_x, speed_y, speed_z = (ghosted[c] * inverse for c in (1, 2, 3))
        field_z, face_x, face_y = ghosted[4], ghosted[5], ghosted[6]
        centre_x = 0.5 * (face_x + roll(face_x, -1, 1))
        centre_y = 0.5 * (face_y + roll(face_y, -1, 0))
        prims_x = [density, speed_x, speed_y, speed_z, centre_y, field_z]
        prims_y = [density, speed_y, speed_x, speed_z, centre_x, field_z]
        flux_x = sweep([v[:ROWS] for v in prims_x], face_x[:ROWS], 1)
        prims_x[3] = None
        ghost_x = sweep([v if v is None else v[ROWS:] for v in prims_x], face_x[ROWS:], 1)
        flux_y = sweep([v[:, :COLS] for v in prims_y], face_y[:, :COLS], 0)
        prims_y[3] = None
        ghost_y = sweep([v if v is None else v[:, COLS:] for v in prims_y], face_y[:, COLS:], 0)
        cross_x = jnp.concatenate([flux_x[4], ghost_x[4]], axis=0)
        cross_y = jnp.concatenate([flux_y[4], ghost_y[4]], axis=1)
        edge = 0.25 * (
            (cross_y + roll(cross_y, 1, 1)) - (cross_x + roll(cross_x, 1, 0))
        )
        edge = jnp.where(corner_ok, edge, 0.0)

        from_left = by_sublane(
            corner_in[section, 1], col_in[section, 1, 16:24], corner_in[section, 4]
        )
        from_right = by_sublane(
            corner_in[section, 2], col_in[section, 0, 16:24], corner_in[section, 5]
        )
        from_right = jnp.where(level == 0, roll(from_right, 32, 1), roll(from_right, 64, 1))
        beside = []
        for k in (1, 0):
            part = col_in[section, k, 8:16]
            part = jnp.concatenate([part, roll(part, 4, 0)], axis=1)
            beside.append(roll(part, 2, 0) if k == 1 else part)
        own_sides = jnp.where(sub8[:, :1] < 4, columns[6:7], columns[15:16])
        sub_wide = iota((8, 256), 0)

        def side_window(odd):
            left, right = (roll(v, -16, 1) if odd else v for v in beside)
            left = jnp.where(finer[(0, -1)] > 0.5, left, received[2:3])
            right = jnp.where(finer[(0, 1)] > 0.5, right, received[8:9])
            return jnp.where(sub_wide < 2, left, jnp.where(sub_wide < 6, own_sides, right))

        side_windows = [side_window(False), side_window(True)]
        swapped = (0, 2, 1, 3, 4, 6, 5)

        def windows(c):
            first = jnp.where(lane8 == COLS - 1, ghosted[c, 39:40, COLS:], ghosted[c, 39:40, :COLS])
            second = jnp.where(lane8 == COLS - 1, ghosted[c, 0:1, COLS:], ghosted[c, 0:1, :COLS])

            def at_level(low, high):
                value = jnp.where(level == 0, ghosted[c, low : low + 1], ghosted[c, high : high + 1])
                return jnp.where(lane8 == COLS - 1, value[:, COLS:], value[:, :COLS])

            base = jnp.where(
                sub8 < 2,
                first,
                jnp.where(sub8 < 4, second, jnp.where(sub8 < 6, at_level(7, 15), at_level(8, 16))),
            )
            q, rows_of = c % 4, slice(32 + 8 * (c // 4), 40 + 8 * (c // 4))
            fine = jnp.where(
                upper8,
                roll(row_in[section, 1, rows_of], -2 * q, 0),
                roll(row_in[section, 0, rows_of], -2 * q, 0),
            )
            pair = []
            for odd in range(2):
                value = jnp.where(use_rows, roll(fine, 64, 1) if odd else fine, base)
                value = jnp.where(use_left, roll(from_left, 127 - (16 * c + 8 + odd), 1), value)
                value = jnp.where(use_right, roll(from_right, -(16 * c + 8 + odd), 1), value)
                t = swapped[c]
                half = side_windows[odd][:, COLS * (t // 4) : COLS * (t // 4) + COLS]
                pair.append(jnp.where(in_side, roll(half, 80 - 32 * (t % 4), 1), value))
            return pair

        even, odd = zip(*[windows(c) if c != 3 else (None, None) for c in range(7)])

        def primitives_of(v):
            inv = 1.0 / v[0]
            return v[0], v[1] * inv, v[2] * inv, v[4], v[5], v[6]

        even, odd = primitives_of(even), primitives_of(odd)
        odd_before = [roll(v, 1, 1) for v in odd]
        even_before = [roll(v, 1, 1) for v in even]

        def along_rows(v, centre):
            return sweep([v[0], v[2], v[1], None, centre, v[3]], v[5], 0)[4]

        fine_y = along_rows(even, 0.5 * (even[4] + odd[4])) + along_rows(
            odd_before, 0.5 * (odd_before[4] + even[4])
        )

        def across(v):
            centre = 0.5 * (v[5] + roll(v[5], -1, 0))
            return [v[0], v[1], v[2], centre, v[3]]

        left, right = [], []
        for a, b, c, d in zip(*[across(v) for v in (even_before, odd_before, even, odd)]):
            middle = c - b
            left.append(b + 0.5 * minmod(b - a, middle))
            right.append(c - 0.5 * minmod(middle, d - c))
        left.insert(3, None)
        right.insert(3, None)
        fine_x = riemann(left, right, even[4])[4]
        fine_edge = 0.25 * (fine_y - (fine_x + roll(fine_x, 1, 0)))

        change = [
            (roll(flux_x[a], -1, 1) - flux_x[a])[:, :COLS]
            + (roll(flux_y[b], -1, 0) - flux_y[b])[:ROWS]
            for a, b in ((0, 0), (1, 2), (2, 1), (3, 3), (5, 5))
        ]

        def finish(c, value):
            if section == 0:
                current[c] = jnp.where(cell_ok, value, 0.0)
            else:
                out[c] = jnp.where(cell_ok, 0.5 * (fields[c] + value), 0.0)

        for c in range(5):
            finish(c, state[c] - ratio * change[c])

        sides = jnp.where(sub8 == 0, -fine_edge[2:3], jnp.where(sub8 == 1, -fine_edge[6:7], 0.0))
        sides = jnp.where(in_side, sides, 0.0)
        sides = dot(halves(sides, 0), line_place, ((0,), (0,)))[80:104]
        row24, lane24 = iota((24, COLS), 0), iota((24, COLS), 1)
        part = edge[:24, :COLS]
        on_low, on_high = row24 == 0, row24 == rows
        on_left, on_right = lane24 == 0, lane24 == cols

        def border_flags(row):
            side = finer[(row, 0)]
            first = jnp.maximum(jnp.maximum(side, finer[(0, -1)]), finer[(row, -1)])
            final = jnp.maximum(jnp.maximum(side, finer[(0, 1)]), finer[(row, 1)])
            value = jnp.where(on_left, first, jnp.where(on_right, final, side))
            return jnp.where(lane24 <= cols, value, 0.0) > 0.5

        part = jnp.where(on_left & (finer[(0, -1)] > 0.5), sides, part)
        part = jnp.where(on_right & (finer[(0, 1)] > 0.5), sides, part)
        part = jnp.where(on_low & border_flags(-1), fine_edge[2:3], part)
        part = jnp.where(on_high & border_flags(1), fine_edge[6:7], part)
        top = jnp.concatenate([part, edge[:24, COLS:]], axis=1)
        edge = jnp.concatenate([top, edge[24:]], axis=0)
        finish(5, state[5] - ratio * (roll(edge, -1, 0) - edge)[:ROWS, :COLS])
        finish(6, state[6] + ratio * (roll(edge, -1, 1) - edge)[:ROWS, :COLS])

    for copy in copies:
        copy.wait_send()


def on_device(seg_count, sub_count, fields, region_levels):
    vmem = pl.BlockSpec(memory_space=pltpu.VMEM)
    region_levels = region_levels.T
    fields = pltpu.with_memory_space_constraint(fields, pltpu.HBM)
    region_levels = pltpu.with_memory_space_constraint(region_levels, pltpu.HBM)
    return pl.pallas_call(
        functools.partial(kernel, seg_count, sub_count),
        out_shape=jax.ShapeDtypeStruct(fields.shape, F32),
        in_specs=[pl.BlockSpec(memory_space=pltpu.HBM)] * 2,
        out_specs=vmem,
        scratch_shapes=[
            pltpu.VMEM(fields.shape, F32),
            pltpu.SMEM(region_levels.shape, I32),
            pltpu.VMEM((7, 40, 256), F32),
            pltpu.VMEM((7, ROWS, COLS), F32),
            pltpu.VMEM((2, 2, 48, COLS), F32),
            pltpu.VMEM((2, 2, 48, COLS), F32),
            pltpu.VMEM((2, 6, 8, COLS), F32),
            pltpu.VMEM((2, 6, 8, COLS), F32),
            pltpu.VMEM((2, 2, 24, COLS), F32),
            pltpu.VMEM((2, 2, 24, COLS), F32),
            pltpu.VMEM((6, 256, COLS), BF16),
            pltpu.VMEM((2, 2, 256, COLS), BF16),
            pltpu.VMEM((256, COLS), BF16),
            pltpu.VMEM((256, 3 * COLS), BF16),
            pltpu.SemaphoreType.DMA((2, 8)),
            pltpu.SemaphoreType.DMA((2, 8)),
            pltpu.SemaphoreType.DMA((2,)),
        ],
        compiler_params=pltpu.CompilerParams(
            collective_id=0, has_side_effects=True, vmem_limit_bytes=32 * 1024 * 1024
        ),
    )(fields, region_levels)


def solution(mesh):
    body = functools.partial(on_device, mesh.shape["seg"], mesh.shape["sub"])
    return jax.shard_map(
        body,
        mesh=mesh,
        in_specs=(P(None, "seg", "sub"), P()),
        out_specs=P(None, "seg", "sub"),
        check_vma=False,
    )
```

```python
import functools

import jax
import jax.numpy as jnp
from jax import lax
from jax.experimental import pallas as pl
from jax.experimental.pallas import tpu as pltpu
from jax.sharding import PartitionSpec as P

STEP_SIZE = 0.08
MESH = pl.DeviceIdType.MESH
F32, BF16, I32 = jnp.float32, jnp.bfloat16, jnp.int32
ROWS, COLS = 32, 128
AROUND = [(1, 0), (1, 1), (1, -1), (-1, 0), (-1, 1), (-1, -1), (0, -1), (0, 1)]


def iota(shape, axis):
    return lax.broadcasted_iota(I32, shape, axis)


def pick(level, values):
    return jnp.where(level == 0, values[0], jnp.where(level == 1, values[1], values[2]))


def halves(value, axis):
    high = value.astype(BF16)
    low = (value - high.astype(F32)).astype(BF16)
    return jnp.concatenate([high, low], axis=axis)


def dot(a, b, dims=((1,), (0,))):
    return lax.dot_general(a, b, (dims, ((), ())), preferred_element_type=F32)


def twice(matrix, axis):
    matrix = matrix.astype(BF16)
    return jnp.concatenate([matrix, matrix], axis=axis)


def resample(source, target, delta):
    source = jnp.where(delta < 0, source >> 1, source)
    target = jnp.where(delta > 0, target >> 1, target)
    return jnp.where(source == target, jnp.where(delta < 0, 0.5, 1.0), 0.0).astype(F32)


def roll(value, shift, axis):
    return pltpu.roll(value, shift % value.shape[axis], axis)


def minmod(a, b):
    return jnp.maximum(jnp.minimum(a, b), 0.0) + jnp.minimum(jnp.maximum(a, b), 0.0)


def sweep(primitives, normal, axis):
    left, right = [], []
    for value in primitives:
        if value is None:
            left.append(None)
            right.append(None)
            continue
        before = value - roll(value, 1, axis)
        half = 0.5 * minmod(before, roll(before, -1, axis))
        left.append(roll(value + half, 1, axis))
        right.append(value - half)

    return riemann(left, right, normal)


def riemann(left, right, normal):
    def pieces(values):
        density, speed_n, speed_t, speed_z, field_t, field_z = values
        square = normal * normal + field_t * field_t + field_z * field_z
        moment = density * speed_n
        cons = [density, moment, density * speed_t, None, field_t, field_z]
        flux = [
            moment,
            moment * speed_n + (density + 0.5 * square) - normal * normal,
            moment * speed_t - normal * field_t,
            None,
            field_t * speed_n - normal * speed_t,
            None,
        ]
        if speed_z is not None:
            cons[3] = density * speed_z
            flux[3] = moment * speed_z - normal * field_z
            flux[5] = field_z * speed_n - normal * speed_z
        return flux, cons, jnp.abs(speed_n) + jnp.sqrt(1.0 + square / density)

    flux_l, cons_l, signal_l = pieces(left)
    flux_r, cons_r, signal_r = pieces(right)
    fastest = jnp.maximum(signal_l, signal_r)
    return [
        None if fl is None else 0.5 * ((fl + fr) - fastest * (cr - cl))
        for fl, fr, cl, cr in zip(flux_l, flux_r, cons_l, cons_r)
    ]


def strip_choices(block, upper, sub8, odd_lane):
    same, coarse, fine = block, [], []
    sign = 1 if upper else -1
    edge = 7 if upper else 0
    for comp in range(7):
        value = block[comp]
        if comp == 6:
            pair = roll(value, 1, 0) if upper else value
        else:
            pair = 0.5 * (value + roll(value, sign, 0))
        if comp == 5:
            pair = jnp.where(odd_lane, roll(pair, 1, 1), pair)
        coarse.append(
            jnp.where(
                sub8 == edge,
                pair,
                jnp.where(sub8 == edge - sign, roll(pair, sign, 0), roll(pair, 2 * sign, 0)),
            )
        )
        fine.append(jnp.where(sub8 == edge, value, roll(value, -sign, 0)))
    return same, coarse, fine


def kernel(
    seg_count, sub_count, fields_hbm, levels_hbm, out,
    fields, levels, ghosted, current, row_out, row_in, corner_out, corner_in, col_out, col_in,
    lane_maps, row_maps, fine_map, border_map, send_sem, recv_sem, fetch_sem,
):
    fetches = [
        pltpu.make_async_copy(levels_hbm, levels, fetch_sem.at[0]),
        pltpu.make_async_copy(fields_hbm, fields, fetch_sem.at[1]),
    ]
    for fetch in fetches:
        fetch.start()
    seg, sub = lax.axis_index("seg"), lax.axis_index("sub")

    def place(offset):
        return (
            lax.rem(seg + (seg_count + offset[0]), seg_count),
            lax.rem(sub + (sub_count + offset[1]), sub_count),
        )

    places = [place(offset) for offset in AROUND]
    barrier = pltpu.get_barrier_semaphore()
    for target in places:
        pl.semaphore_signal(barrier, inc=1, device_id=target, device_id_type=MESH)

    i, j = iota((COLS, COLS), 0), iota((COLS, COLS), 1)
    together = (i >> 5) == (j >> 5)
    comp_six = (i >> 5) == 2
    source = (i & ~31) + ((i & 31) >> 1) + ((i & 1) << 4)
    fine_map[...] = twice(jnp.where(source == j, 1.0, 0.0), 0)
    end = jnp.where(j == 8, 0, jnp.where(j == 9, 1, 2 * COLS))
    border_map[:, 0:COLS] = twice(jnp.where((i >> 1) + ((i & 1) << 6) == j, 1.0, 0.0), 0)
    border_map[:, 2 * COLS :] = twice(jnp.where(i == end, 1.0, 0.0), 0)

    fetches[0].wait()
    level = levels[sub, seg]
    near = {offset: levels[p[1], p[0]] for offset, p in zip(AROUND, places)}
    rows = pick(level, (8, 16, 32))
    cols = pick(level, (32, 64, 128))
    ratio = pick(level, [jnp.float32(STEP_SIZE / h) for h in (4.0, 2.0, 1.0)])
    delta = {offset: near[offset] - level for offset in AROUND}

    for k, offset in enumerate(AROUND[:6]):
        if offset[1] == 0:
            matrix = resample(i, j, delta[offset])
        elif offset[1] == 1:
            matrix = jnp.where(j >= 125, resample(i - cols, j - COLS, delta[offset]), 0.0)
        else:
            first = j - pick(near[offset], (32, 64, 0))
            ok = (first >= 0) & (first < 3)
            matrix = jnp.where(ok, resample(i, first, delta[offset]), 0.0)
        lane_maps[k] = twice(matrix, 0)
    border_map[:, COLS : 2 * COLS] = twice(jnp.where(i == end + cols - 2, 1.0, 0.0), 0)
    i, j = i & 31, j & 31
    for k, offset in enumerate(AROUND[6:]):
        d = delta[offset]
        matrix = jnp.where(together, resample(i, j, d), 0.0)
        row_maps[k, 0] = twice(matrix, 0)
        faces = jnp.where(together, jnp.where(i == 2 * j, 1.0, 0.0), 0.0)
        row_maps[k, 1] = twice(jnp.where(comp_six & (d < 0), faces, matrix), 0)
    k, i = iota((16, COLS), 0), iota((16, COLS), 1)
    to_right = k >= 8
    k = k & 7
    is_face = k >= 3
    k = k - jnp.where(is_face, 3, 0) - jnp.where(to_right, 3, 0)
    i = i - jnp.where(to_right, cols, 0)

    def column_pick(d):
        faces = jnp.where(d < 0, jnp.where(i == 2 * k, 1.0, 0.0), resample(i, k, d))
        return jnp.where(is_face, faces, resample(i, k, d))

    raw = jnp.where(i == jnp.where(to_right, k - 2, k - 3), 1.0, 0.0)
    is_raw = (iota((16, COLS), 0) & 7) >= 6
    column_map = twice(
        jnp.where(
            is_raw,
            raw,
            jnp.where(to_right, column_pick(delta[(0, 1)]), column_pick(delta[(0, -1)])),
        ),
        1,
    )
    k, i = iota((16, 256), 0), iota((16, 256), 1)
    column_place = twice(
        jnp.where((k < 3) & (i == k + 253), 1.0, 0.0)
        + jnp.where((k >= 8) & (k < 11) & (i == cols + k - 8), 1.0, 0.0),
        0,
    )
    k, i = iota((8, COLS), 0), iota((8, COLS), 1)
    line_place = twice(
        jnp.where(((k == 0) & (i == 0)) | ((k == 1) & (i == cols)), 1.0, 0.0), 0
    )

    sub8, lane8 = iota((8, COLS), 0), iota((8, COLS), 1)
    odd_lane = (lane8 & 1) == 1
    upper8 = sub8 >= 4
    inside8 = lane8 < cols
    in_side = (lane8 >= 80) & (lane8 < 96)

    def flag(condition):
        return jnp.where(condition, 1.0, 0.0).astype(F32)

    finer = {offset: flag(near[offset] > level) for offset in AROUND}

    def by_sublane(low, middle, high):
        return jnp.where(sub8 < 2, low, jnp.where(sub8 < 6, middle, high))

    finer_left = by_sublane(finer[(-1, -1)], finer[(0, -1)], finer[(1, -1)])
    finer_right = by_sublane(finer[(-1, 1)], finer[(0, 1)], finer[(1, 1)])
    finer_rows = by_sublane(finer[(-1, 0)], 0.0, finer[(1, 0)])
    use_left = jnp.where(lane8 == COLS - 1, finer_left, 0.0) > 0.5
    use_right = jnp.where(lane8 == cols, finer_right, 0.0) > 0.5
    use_rows = jnp.where(inside8, finer_rows, 0.0) > 0.5
    row40, lane40 = iota((40, 256), 0), iota((40, 256), 1)
    corner_ok = (row40 <= rows) & (lane40 <= cols)
    row32, lane32 = iota((ROWS, COLS), 0), iota((ROWS, COLS), 1)
    cell_ok = (row32 < rows) & (lane32 < cols)

    fetches[1].wait()
    copies = []

    def send(section, index, source, target):
        copy = pltpu.make_async_remote_copy(
            src_ref=source,
            dst_ref=target,
            send_sem=send_sem.at[section, index],
            recv_sem=recv_sem.at[section, index],
            device_id=places[index % 8],
            device_id_type=MESH,
        )
        copy.start()
        return copy

    for section in range(2):
        if section == 0:
            state = [jnp.where(cell_ok, fields[c], 0.0) for c in range(7)]
        else:
            state = [current[c] for c in range(7)]

        tops = [pick(level, (v[0:8], v[8:16], v[24:32])) for v in state]
        lows = [v[0:8] for v in state]
        border = [
            jnp.where(
                sub8 < 2,
                roll(top, 2, 0),
                jnp.where(
                    sub8 < 4,
                    roll(low, 2, 0),
                    jnp.where(sub8 < 6, roll(top, 6, 0), roll(low, 6, 0)),
                ),
            )
            for top, low in zip(tops, lows)
        ]
        stacked = jnp.concatenate(state + [jnp.zeros((ROWS, COLS), F32)], axis=0)
        columns = dot(column_map, halves(stacked, 1), ((1,), (1,)))
        border = dot(halves(jnp.concatenate(border, axis=0), 1), border_map[...])
        ends = []
        for part in (border[:, COLS : 2 * COLS], border[:, 2 * COLS :]):
            total = part[0:8]
            for c in range(1, 7):
                total = total + roll(part[8 * c : 8 * c + 8], 16 * c, 1)
            ends.append(total)
        for k in range(2):
            part = columns[8 * k : 8 * k + 8]
            first, second = part[:, :COLS], part[:, COLS:]
            fine = dot(
                jnp.concatenate([halves(first, 1), halves(second, 1)], axis=0), fine_map[...]
            )
            col_out[section, k, 8:16] = by_sublane(roll(fine[8:], 2, 0), ends[1 - k], fine[:8])
            second = jnp.where((lane8 >> 5) == 1, roll(second, -3, 0), second)
            first = dot(halves(first, 1), row_maps[k, 0])
            second = dot(halves(second, 1), row_maps[k, 1])
            col_out[section, k, 0:8] = jnp.where(upper8, roll(second, 4, 0), first)
        for upper in (True, False):
            choices = strip_choices(tops if upper else lows, upper, sub8, odd_lane)
            base = 0 if upper else 3
            for k in (base + 1, base + 2, base):
                d = delta[AROUND[k]]
                chosen = [
                    jnp.where(d == 0, a, jnp.where(d < 0, b, c)) for a, b, c in zip(*choices)
                ]
                chosen.append(jnp.zeros((8, COLS), F32))
                packed = [
                    jnp.where(upper8 == upper, chosen[2 * m], roll(chosen[2 * m + 1], 4, 0))
                    for m in range(4)
                ]
                packed = jnp.concatenate(packed, axis=0)
                packed = dot(halves(packed, 1), lane_maps[k])
                if k != base:
                    corner = packed[0:8] + ends[k - base - 1]
                    for m in range(1, 4):
                        corner = corner + roll(packed[8 * m : 8 * m + 8], 32 * m, 1)
                    corner_out[section, k] = corner
                    continue
                row_out[section, k // 3, 0:32] = packed
                for group in range(2):
                    block = jnp.zeros((8, COLS), F32)
                    for q in range(4 if group == 0 else 3):
                        c = 4 * group + q
                        part = roll(border[8 * c : 8 * c + 8, :COLS], 2 * q, 0)
                        place_of = q if upper else (3 + q) & 3
                        block = jnp.where((sub8 >> 1) == place_of, part, block)
                    row_out[section, k // 3, 32 + 8 * group : 40 + 8 * group] = block
        if section == 0:
            pl.semaphore_wait(barrier, len(AROUND))
        done, copies = copies, []
        for k in range(2):
            copies.append(send(section, 6 + k, col_out.at[section, k], col_in.at[section, k]))
        for k in (1, 2, 4, 5):
            copies.append(
                send(section, k, corner_out.at[section, k], corner_in.at[section, k])
            )
        for k in (0, 3):
            copies.append(
                send(section, k, row_out.at[section, k // 3], row_in.at[section, k // 3])
            )
        for copy in done:
            copy.wait_send()
        for copy in copies:
            copy.wait_recv()

        received = jnp.concatenate(
            [
                jnp.concatenate([part, roll(part, 4, 0)], axis=1)
                for part in (col_in[section, 1, 0:8], col_in[section, 0, 0:8])
            ],
            axis=0,
        )
        sides = dot(halves(received, 0), column_place, ((0,), (0,)))
        for c in range(7):
            def strip(k):
                if k % 3 == 0:
                    block = row_in[section, k // 3, 8 * (c // 2) : 8 * (c // 2) + 8]
                else:
                    block = roll(corner_in[section, k], -32 * (c // 2), 1)
                return roll(block, 4, 0) if c % 2 else block

            low = [
                jnp.where(inside8, strip(0), strip(2)),
                jnp.where(lane8 < 64, strip(2), strip(1)),
            ]
            high = [
                jnp.where(inside8, strip(3), strip(5)),
                jnp.where(lane8 < 64, strip(5), strip(4)),
            ]
            for h in range(2):
                lanes = slice(128 * h, 128 * h + 128)
                for b in range(4):
                    block = sides[32 * c + 8 * b : 32 * c + 8 * b + 8, lanes]
                    if h == 0:
                        block = jnp.where(inside8, state[c][8 * b : 8 * b + 8], block)
                    if b in (1, 2):
                        block = jnp.where(level == b - 1, high[h], block)
                    ghosted[c, 8 * b : 8 * b + 8, lanes] = block
                ghosted[c, 32:40, lanes] = jnp.where(upper8, low[h], high[h])

        density = ghosted[0]
        inverse = 1.0 / density
        speed_x, speed_y, speed_z = (ghosted[c] * inverse for c in (1, 2, 3))
        field_z, face_x, face_y = ghosted[4], ghosted[5], ghosted[6]
        centre_x = 0.5 * (face_x + roll(face_x, -1, 1))
        centre_y = 0.5 * (face_y + roll(face_y, -1, 0))
        prims_x = [density, speed_x, speed_y, speed_z, centre_y, field_z]
        prims_y = [density, speed_y, speed_x, speed_z, centre_x, field_z]
        flux_x = sweep([v[:ROWS] for v in prims_x], face_x[:ROWS], 1)
        prims_x[3] = None
        ghost_x = sweep([v if v is None else v[ROWS:] for v in prims_x], face_x[ROWS:], 1)
        flux_y = sweep([v[:, :COLS] for v in prims_y], face_y[:, :COLS], 0)
        prims_y[3] = None
        ghost_y = sweep([v if v is None else v[:, COLS:] for v in prims_y], face_y[:, COLS:], 0)
        cross_x = jnp.concatenate([flux_x[4], ghost_x[4]], axis=0)
        cross_y = jnp.concatenate([flux_y[4], ghost_y[4]], axis=1)
        edge = 0.25 * (
            (cross_y + roll(cross_y, 1, 1)) - (cross_x + roll(cross_x, 1, 0))
        )
        edge = jnp.where(corner_ok, edge, 0.0)

        from_left = by_sublane(
            corner_in[section, 1], col_in[section, 1, 8:16], corner_in[section, 4]
        )
        from_right = by_sublane(
            corner_in[section, 2], col_in[section, 0, 8:16], corner_in[section, 5]
        )
        from_right = jnp.where(level == 0, roll(from_right, 32, 1), roll(from_right, 64, 1))
        beside = []
        for k in (1, 0):
            part = col_in[section, k, 8:16]
            part = jnp.concatenate([part, roll(part, -2, 0)], axis=1)
            beside.append(roll(part, 2, 0) if k == 1 else part)
        own_sides = jnp.where(sub8[:, :1] < 4, columns[6:7], columns[15:16])
        sub_wide = iota((8, 256), 0)

        def side_window(odd):
            left, right = (roll(v, -16, 1) if odd else v for v in beside)
            left = jnp.where(finer[(0, -1)] > 0.5, left, received[2:3])
            right = jnp.where(finer[(0, 1)] > 0.5, right, received[8:9])
            return jnp.where(sub_wide < 2, left, jnp.where(sub_wide < 6, own_sides, right))

        side_windows = [side_window(False), side_window(True)]
        swapped = (0, 2, 1, 3, 4, 6, 5)

        def windows(c):
            first = jnp.where(lane8 == COLS - 1, ghosted[c, 39:40, COLS:], ghosted[c, 39:40, :COLS])
            second = jnp.where(lane8 == COLS - 1, ghosted[c, 0:1, COLS:], ghosted[c, 0:1, :COLS])

            def at_level(low, high):
                value = jnp.where(level == 0, ghosted[c, low : low + 1], ghosted[c, high : high + 1])
                return jnp.where(lane8 == COLS - 1, value[:, COLS:], value[:, :COLS])

            base = jnp.where(
                sub8 < 2,
                first,
                jnp.where(sub8 < 4, second, jnp.where(sub8 < 6, at_level(7, 15), at_level(8, 16))),
            )
            q, rows_of = c % 4, slice(32 + 8 * (c // 4), 40 + 8 * (c // 4))
            fine = jnp.where(
                upper8,
                roll(row_in[section, 1, rows_of], -2 * q, 0),
                roll(row_in[section, 0, rows_of], -2 * q, 0),
            )
            pair = []
            for odd in range(2):
                value = jnp.where(use_rows, roll(fine, 64, 1) if odd else fine, base)
                value = jnp.where(use_left, roll(from_left, 127 - (16 * c + 8 + odd), 1), value)
                value = jnp.where(use_right, roll(from_right, -(16 * c + 8 + odd), 1), value)
                t = swapped[c]
                half = side_windows[odd][:, COLS * (t // 4) : COLS * (t // 4) + COLS]
                pair.append(jnp.where(in_side, roll(half, 80 - 32 * (t % 4), 1), value))
            return pair

        even, odd = zip(*[windows(c) if c != 3 else (None, None) for c in range(7)])

        def primitives_of(v):
            inv = 1.0 / v[0]
            return v[0], v[1] * inv, v[2] * inv, v[4], v[5], v[6]

        even, odd = primitives_of(even), primitives_of(odd)
        odd_before = [roll(v, 1, 1) for v in odd]
        even_before = [roll(v, 1, 1) for v in even]

        def along_rows(v, centre):
            return sweep([v[0], v[2], v[1], None, centre, v[3]], v[5], 0)[4]

        fine_y = along_rows(even, 0.5 * (even[4] + odd[4])) + along_rows(
            odd_before, 0.5 * (odd_before[4] + even[4])
        )

        def across(v):
            centre = 0.5 * (v[5] + roll(v[5], -1, 0))
            return [v[0], v[1], v[2], centre, v[3]]

        left, right = [], []
        for a, b, c, d in zip(*[across(v) for v in (even_before, odd_before, even, odd)]):
            middle = c - b
            left.append(b + 0.5 * minmod(b - a, middle))
            right.append(c - 0.5 * minmod(middle, d - c))
        left.insert(3, None)
        right.insert(3, None)
        fine_x = riemann(left, right, even[4])[4]
        fine_edge = 0.25 * (fine_y - (fine_x + roll(fine_x, 1, 0)))

        change = [
            (roll(flux_x[a], -1, 1) - flux_x[a])[:, :COLS]
            + (roll(flux_y[b], -1, 0) - flux_y[b])[:ROWS]
            for a, b in ((0, 0), (1, 2), (2, 1), (3, 3), (5, 5))
        ]

        def finish(c, value):
            if section == 0:
                current[c] = jnp.where(cell_ok, value, 0.0)
            else:
                out[c] = jnp.where(cell_ok, 0.5 * (fields[c] + value), 0.0)

        for c in range(5):
            finish(c, state[c] - ratio * change[c])

        sides = jnp.where(sub8 == 0, -fine_edge[2:3], jnp.where(sub8 == 1, -fine_edge[6:7], 0.0))
        sides = jnp.where(in_side, sides, 0.0)
        sides = dot(halves(sides, 0), line_place, ((0,), (0,)))[80:104]
        row24, lane24 = iota((24, COLS), 0), iota((24, COLS), 1)
        part = edge[:24, :COLS]
        on_low, on_high = row24 == 0, row24 == rows
        on_left, on_right = lane24 == 0, lane24 == cols

        def border_flags(row):
            side = finer[(row, 0)]
            first = jnp.maximum(jnp.maximum(side, finer[(0, -1)]), finer[(row, -1)])
            final = jnp.maximum(jnp.maximum(side, finer[(0, 1)]), finer[(row, 1)])
            value = jnp.where(on_left, first, jnp.where(on_right, final, side))
            return jnp.where(lane24 <= cols, value, 0.0) > 0.5

        part = jnp.where(on_left & (finer[(0, -1)] > 0.5), sides, part)
        part = jnp.where(on_right & (finer[(0, 1)] > 0.5), sides, part)
        part = jnp.where(on_low & border_flags(-1), fine_edge[2:3], part)
        part = jnp.where(on_high & border_flags(1), fine_edge[6:7], part)
        top = jnp.concatenate([part, edge[:24, COLS:]], axis=1)
        edge = jnp.concatenate([top, edge[24:]], axis=0)
        finish(5, state[5] - ratio * (roll(edge, -1, 0) - edge)[:ROWS, :COLS])
        finish(6, state[6] + ratio * (roll(edge, -1, 1) - edge)[:ROWS, :COLS])

    for copy in copies:
        copy.wait_send()


def on_device(seg_count, sub_count, fields, region_levels):
    vmem = pl.BlockSpec(memory_space=pltpu.VMEM)
    region_levels = region_levels.T
    fields = pltpu.with_memory_space_constraint(fields, pltpu.HBM)
    region_levels = pltpu.with_memory_space_constraint(region_levels, pltpu.HBM)
    return pl.pallas_call(
        functools.partial(kernel, seg_count, sub_count),
        out_shape=jax.ShapeDtypeStruct(fields.shape, F32),
        in_specs=[pl.BlockSpec(memory_space=pltpu.HBM)] * 2,
        out_specs=vmem,
        scratch_shapes=[
            pltpu.VMEM(fields.shape, F32),
            pltpu.SMEM(region_levels.shape, I32),
            pltpu.VMEM((7, 40, 256), F32),
            pltpu.VMEM((7, ROWS, COLS), F32),
            pltpu.VMEM((2, 2, 48, COLS), F32),
            pltpu.VMEM((2, 2, 48, COLS), F32),
            pltpu.VMEM((2, 6, 8, COLS), F32),
            pltpu.VMEM((2, 6, 8, COLS), F32),
            pltpu.VMEM((2, 2, 16, COLS), F32),
            pltpu.VMEM((2, 2, 16, COLS), F32),
            pltpu.VMEM((6, 256, COLS), BF16),
            pltpu.VMEM((2, 2, 256, COLS), BF16),
            pltpu.VMEM((256, COLS), BF16),
            pltpu.VMEM((256, 3 * COLS), BF16),
            pltpu.SemaphoreType.DMA((2, 8)),
            pltpu.SemaphoreType.DMA((2, 8)),
            pltpu.SemaphoreType.DMA((2,)),
        ],
        compiler_params=pltpu.CompilerParams(
            collective_id=0, has_side_effects=True, vmem_limit_bytes=32 * 1024 * 1024
        ),
    )(fields, region_levels)


def solution(mesh):
    body = functools.partial(on_device, mesh.shape["seg"], mesh.shape["sub"])
    return jax.shard_map(
        body,
        mesh=mesh,
        in_specs=(P(None, "seg", "sub"), P()),
        out_specs=P(None, "seg", "sub"),
        check_vma=False,
    )
```

```python
import functools

import jax
import jax.numpy as jnp
from jax import lax
from jax.experimental import pallas as pl
from jax.experimental.pallas import tpu as pltpu
from jax.sharding import PartitionSpec as P

STEP_SIZE = 0.08
MESH = pl.DeviceIdType.MESH
F32, BF16, I32 = jnp.float32, jnp.bfloat16, jnp.int32
ROWS, COLS = 32, 128
AROUND = [(1, 0), (1, 1), (1, -1), (-1, 0), (-1, 1), (-1, -1), (0, -1), (0, 1)]


def iota(shape, axis):
    return lax.broadcasted_iota(I32, shape, axis)


def pick(level, values):
    return jnp.where(level == 0, values[0], jnp.where(level == 1, values[1], values[2]))


def halves(value, axis):
    high = value.astype(BF16)
    low = (value - high.astype(F32)).astype(BF16)
    return jnp.concatenate([high, low], axis=axis)


def dot(a, b, dims=((1,), (0,))):
    return lax.dot_general(a, b, (dims, ((), ())), preferred_element_type=F32)


def twice(matrix, axis):
    matrix = matrix.astype(BF16)
    return jnp.concatenate([matrix, matrix], axis=axis)


def resample(source, target, delta):
    source = jnp.where(delta < 0, source >> 1, source)
    target = jnp.where(delta > 0, target >> 1, target)
    return jnp.where(source == target, jnp.where(delta < 0, 0.5, 1.0), 0.0).astype(F32)


def roll(value, shift, axis):
    return pltpu.roll(value, shift % value.shape[axis], axis)


def minmod(a, b):
    return jnp.maximum(jnp.minimum(a, b), 0.0) + jnp.minimum(jnp.maximum(a, b), 0.0)


def sweep(primitives, normal, axis):
    chunks = [slice(row, row + 8) for row in range(0, normal.shape[0], 8)]

    def part(values, rows):
        return [None if v is None else v[rows] for v in values]

    if axis == 1:
        pieces = [
            riemann(*reconstruct(part(primitives, rows), axis), normal[rows]) for rows in chunks
        ]
    else:
        left, right = reconstruct(primitives, axis)
        pieces = [riemann(part(left, rows), part(right, rows), normal[rows]) for rows in chunks]
    return [None if v[0] is None else jnp.concatenate(v, axis=0) for v in zip(*pieces)]


def reconstruct(primitives, axis):
    left, right = [], []
    for value in primitives:
        if value is None:
            left.append(None)
            right.append(None)
            continue
        before = value - roll(value, 1, axis)
        half = 0.5 * minmod(before, roll(before, -1, axis))
        left.append(roll(value + half, 1, axis))
        right.append(value - half)

    return left, right


def riemann(left, right, normal):
    def pieces(values):
        density, speed_n, speed_t, speed_z, field_t, field_z = values
        square = normal * normal + field_t * field_t + field_z * field_z
        moment = density * speed_n
        cons = [density, moment, density * speed_t, None, field_t, field_z]
        flux = [
            moment,
            moment * speed_n + (density + 0.5 * square) - normal * normal,
            moment * speed_t - normal * field_t,
            None,
            field_t * speed_n - normal * speed_t,
            None,
        ]
        if speed_z is not None:
            cons[3] = density * speed_z
            flux[3] = moment * speed_z - normal * field_z
            flux[5] = field_z * speed_n - normal * speed_z
        return flux, cons, jnp.abs(speed_n) + jnp.sqrt(1.0 + square / density)

    flux_l, cons_l, signal_l = pieces(left)
    flux_r, cons_r, signal_r = pieces(right)
    fastest = jnp.maximum(signal_l, signal_r)
    return [
        None if fl is None else 0.5 * ((fl + fr) - fastest * (cr - cl))
        for fl, fr, cl, cr in zip(flux_l, flux_r, cons_l, cons_r)
    ]


def strip_choices(block, upper, sub8, odd_lane):
    same, coarse, fine = block, [], []
    sign = 1 if upper else -1
    edge = 7 if upper else 0
    for comp in range(7):
        value = block[comp]
        if comp == 6:
            pair = roll(value, 1, 0) if upper else value
        else:
            pair = 0.5 * (value + roll(value, sign, 0))
        if comp == 5:
            pair = jnp.where(odd_lane, roll(pair, 1, 1), pair)
        coarse.append(
            jnp.where(
                sub8 == edge,
                pair,
                jnp.where(sub8 == edge - sign, roll(pair, sign, 0), roll(pair, 2 * sign, 0)),
            )
        )
        fine.append(jnp.where(sub8 == edge, value, roll(value, -sign, 0)))
    return same, coarse, fine


def kernel(
    seg_count, sub_count, fields_hbm, levels_hbm, out,
    fields, levels, ghosted, current, row_out, row_in, corner_out, corner_in, col_out, col_in,
    lane_maps, row_maps, fine_map, border_map, send_sem, recv_sem, fetch_sem,
):
    fetches = [
        pltpu.make_async_copy(levels_hbm, levels, fetch_sem.at[0]),
        pltpu.make_async_copy(fields_hbm, fields, fetch_sem.at[1]),
    ]
    for fetch in fetches:
        fetch.start()
    seg, sub = lax.axis_index("seg"), lax.axis_index("sub")

    def place(offset):
        return (
            lax.rem(seg + (seg_count + offset[0]), seg_count),
            lax.rem(sub + (sub_count + offset[1]), sub_count),
        )

    places = [place(offset) for offset in AROUND]
    barrier = pltpu.get_barrier_semaphore()
    for target in places:
        pl.semaphore_signal(barrier, inc=1, device_id=target, device_id_type=MESH)

    i, j = iota((COLS, COLS), 0), iota((COLS, COLS), 1)
    together = (i >> 5) == (j >> 5)
    comp_six = (i >> 5) == 2
    source = (i & ~31) + ((i & 31) >> 1) + ((i & 1) << 4)
    fine_map[...] = twice(jnp.where(source == j, 1.0, 0.0), 0)
    end = jnp.where(j == 8, 0, jnp.where(j == 9, 1, 2 * COLS))
    border_map[:, 0:COLS] = twice(jnp.where((i >> 1) + ((i & 1) << 6) == j, 1.0, 0.0), 0)
    border_map[:, 2 * COLS :] = twice(jnp.where(i == end, 1.0, 0.0), 0)

    fetches[0].wait()
    level = levels[sub, seg]
    near = {offset: levels[p[1], p[0]] for offset, p in zip(AROUND, places)}
    rows = pick(level, (8, 16, 32))
    cols = pick(level, (32, 64, 128))
    ratio = pick(level, [jnp.float32(STEP_SIZE / h) for h in (4.0, 2.0, 1.0)])
    delta = {offset: near[offset] - level for offset in AROUND}

    for k, offset in enumerate(AROUND[:6]):
        if offset[1] == 0:
            matrix = resample(i, j, delta[offset])
        elif offset[1] == 1:
            matrix = jnp.where(j >= 125, resample(i - cols, j - COLS, delta[offset]), 0.0)
        else:
            first = j - pick(near[offset], (32, 64, 0))
            ok = (first >= 0) & (first < 3)
            matrix = jnp.where(ok, resample(i, first, delta[offset]), 0.0)
        lane_maps[k] = twice(matrix, 0)
    border_map[:, COLS : 2 * COLS] = twice(jnp.where(i == end + cols - 2, 1.0, 0.0), 0)
    i, j = i & 31, j & 31
    for k, offset in enumerate(AROUND[6:]):
        d = delta[offset]
        matrix = jnp.where(together, resample(i, j, d), 0.0)
        row_maps[k, 0] = twice(matrix, 0)
        faces = jnp.where(together, jnp.where(i == 2 * j, 1.0, 0.0), 0.0)
        row_maps[k, 1] = twice(jnp.where(comp_six & (d < 0), faces, matrix), 0)
    k, i = iota((16, COLS), 0), iota((16, COLS), 1)
    to_right = k >= 8
    k = k & 7
    is_face = k >= 3
    k = k - jnp.where(is_face, 3, 0) - jnp.where(to_right, 3, 0)
    i = i - jnp.where(to_right, cols, 0)

    def column_pick(d):
        faces = jnp.where(d < 0, jnp.where(i == 2 * k, 1.0, 0.0), resample(i, k, d))
        return jnp.where(is_face, faces, resample(i, k, d))

    raw = jnp.where(i == jnp.where(to_right, k - 2, k - 3), 1.0, 0.0)
    is_raw = (iota((16, COLS), 0) & 7) >= 6
    column_map = twice(
        jnp.where(
            is_raw,
            raw,
            jnp.where(to_right, column_pick(delta[(0, 1)]), column_pick(delta[(0, -1)])),
        ),
        1,
    )
    k, i = iota((16, 256), 0), iota((16, 256), 1)
    column_place = twice(
        jnp.where((k < 3) & (i == k + 253), 1.0, 0.0)
        + jnp.where((k >= 8) & (k < 11) & (i == cols + k - 8), 1.0, 0.0),
        0,
    )
    k, i = iota((8, COLS), 0), iota((8, COLS), 1)
    line_place = twice(
        jnp.where(((k == 0) & (i == 0)) | ((k == 1) & (i == cols)), 1.0, 0.0), 0
    )

    sub8, lane8 = iota((8, COLS), 0), iota((8, COLS), 1)
    odd_lane = (lane8 & 1) == 1
    upper8 = sub8 >= 4
    inside8 = lane8 < cols
    in_side = (lane8 >= 80) & (lane8 < 96)

    def flag(condition):
        return jnp.where(condition, 1.0, 0.0).astype(F32)

    finer = {offset: flag(near[offset] > level) for offset in AROUND}

    def by_sublane(low, middle, high):
        return jnp.where(sub8 < 2, low, jnp.where(sub8 < 6, middle, high))

    finer_left = by_sublane(finer[(-1, -1)], finer[(0, -1)], finer[(1, -1)])
    finer_right = by_sublane(finer[(-1, 1)], finer[(0, 1)], finer[(1, 1)])
    finer_rows = by_sublane(finer[(-1, 0)], 0.0, finer[(1, 0)])
    use_left = jnp.where(lane8 == COLS - 1, finer_left, 0.0) > 0.5
    use_right = jnp.where(lane8 == cols, finer_right, 0.0) > 0.5
    use_rows = jnp.where(inside8, finer_rows, 0.0) > 0.5
    row40, lane40 = iota((40, 256), 0), iota((40, 256), 1)
    corner_ok = (row40 <= rows) & (lane40 <= cols)
    row32, lane32 = iota((ROWS, COLS), 0), iota((ROWS, COLS), 1)
    cell_ok = (row32 < rows) & (lane32 < cols)

    fetches[1].wait()
    copies = []

    def send(section, index, source, target):
        copy = pltpu.make_async_remote_copy(
            src_ref=source,
            dst_ref=target,
            send_sem=send_sem.at[section, index],
            recv_sem=recv_sem.at[section, index],
            device_id=places[index % 8],
            device_id_type=MESH,
        )
        copy.start()
        return copy

    for section in range(2):
        if section == 0:
            state = [jnp.where(cell_ok, fields[c], 0.0) for c in range(7)]
        else:
            state = [current[c] for c in range(7)]

        tops = [pick(level, (v[0:8], v[8:16], v[24:32])) for v in state]
        lows = [v[0:8] for v in state]
        border = [
            jnp.where(
                sub8 < 2,
                roll(top, 2, 0),
                jnp.where(
                    sub8 < 4,
                    roll(low, 2, 0),
                    jnp.where(sub8 < 6, roll(top, 6, 0), roll(low, 6, 0)),
                ),
            )
            for top, low in zip(tops, lows)
        ]
        stacked = jnp.concatenate(state + [jnp.zeros((ROWS, COLS), F32)], axis=0)
        columns = dot(column_map, halves(stacked, 1), ((1,), (1,)))
        border = dot(halves(jnp.concatenate(border, axis=0), 1), border_map[...])
        ends = []
        for part in (border[:, COLS : 2 * COLS], border[:, 2 * COLS :]):
            total = part[0:8]
            for c in range(1, 7):
                total = total + roll(part[8 * c : 8 * c + 8], 16 * c, 1)
            ends.append(total)
        for k in range(2):
            part = columns[8 * k : 8 * k + 8]
            first, second = part[:, :COLS], part[:, COLS:]
            fine = dot(
                jnp.concatenate([halves(first, 1), halves(second, 1)], axis=0), fine_map[...]
            )
            col_out[section, k, 8:16] = by_sublane(roll(fine[8:], 2, 0), ends[1 - k], fine[:8])
            second = jnp.where((lane8 >> 5) == 1, roll(second, -3, 0), second)
            first = dot(halves(first, 1), row_maps[k, 0])
            second = dot(halves(second, 1), row_maps[k, 1])
            col_out[section, k, 0:8] = jnp.where(upper8, roll(second, 4, 0), first)
        for upper in (True, False):
            choices = strip_choices(tops if upper else lows, upper, sub8, odd_lane)
            base = 0 if upper else 3
            for k in (base + 1, base + 2, base):
                d = delta[AROUND[k]]
                chosen = [
                    jnp.where(d == 0, a, jnp.where(d < 0, b, c)) for a, b, c in zip(*choices)
                ]
                chosen.append(jnp.zeros((8, COLS), F32))
                packed = [
                    jnp.where(upper8 == upper, chosen[2 * m], roll(chosen[2 * m + 1], 4, 0))
                    for m in range(4)
                ]
                packed = jnp.concatenate(packed, axis=0)
                packed = dot(halves(packed, 1), lane_maps[k])
                if k != base:
                    corner = packed[0:8] + ends[k - base - 1]
                    for m in range(1, 4):
                        corner = corner + roll(packed[8 * m : 8 * m + 8], 32 * m, 1)
                    corner_out[section, k] = corner
                    continue
                row_out[section, k // 3, 0:32] = packed
                for group in range(2):
                    block = jnp.zeros((8, COLS), F32)
                    for q in range(4 if group == 0 else 3):
                        c = 4 * group + q
                        part = roll(border[8 * c : 8 * c + 8, :COLS], 2 * q, 0)
                        place_of = q if upper else (3 + q) & 3
                        block = jnp.where((sub8 >> 1) == place_of, part, block)
                    row_out[section, k // 3, 32 + 8 * group : 40 + 8 * group] = block
        if section == 0:
            pl.semaphore_wait(barrier, len(AROUND))
        done, copies = copies, []
        for k in range(2):
            copies.append(send(section, 6 + k, col_out.at[section, k], col_in.at[section, k]))
        for k in (1, 2, 4, 5):
            copies.append(
                send(section, k, corner_out.at[section, k], corner_in.at[section, k])
            )
        for k in (0, 3):
            copies.append(
                send(section, k, row_out.at[section, k // 3], row_in.at[section, k // 3])
            )
        for copy in done:
            copy.wait_send()
        for copy in copies:
            copy.wait_recv()

        received = jnp.concatenate(
            [
                jnp.concatenate([part, roll(part, 4, 0)], axis=1)
                for part in (col_in[section, 1, 0:8], col_in[section, 0, 0:8])
            ],
            axis=0,
        )
        sides = dot(halves(received, 0), column_place, ((0,), (0,)))
        for c in range(7):
            def strip(k):
                if k % 3 == 0:
                    block = row_in[section, k // 3, 8 * (c // 2) : 8 * (c // 2) + 8]
                else:
                    block = roll(corner_in[section, k], -32 * (c // 2), 1)
                return roll(block, 4, 0) if c % 2 else block

            low = [
                jnp.where(inside8, strip(0), strip(2)),
                jnp.where(lane8 < 64, strip(2), strip(1)),
            ]
            high = [
                jnp.where(inside8, strip(3), strip(5)),
                jnp.where(lane8 < 64, strip(5), strip(4)),
            ]
            for h in range(2):
                lanes = slice(128 * h, 128 * h + 128)
                for b in range(4):
                    block = sides[32 * c + 8 * b : 32 * c + 8 * b + 8, lanes]
                    if h == 0:
                        block = jnp.where(inside8, state[c][8 * b : 8 * b + 8], block)
                    if b in (1, 2):
                        block = jnp.where(level == b - 1, high[h], block)
                    ghosted[c, 8 * b : 8 * b + 8, lanes] = block
                ghosted[c, 32:40, lanes] = jnp.where(upper8, low[h], high[h])

        density = ghosted[0]
        inverse = 1.0 / density
        speed_x, speed_y, speed_z = (ghosted[c] * inverse for c in (1, 2, 3))
        field_z, face_x, face_y = ghosted[4], ghosted[5], ghosted[6]
        centre_x = 0.5 * (face_x + roll(face_x, -1, 1))
        centre_y = 0.5 * (face_y + roll(face_y, -1, 0))
        prims_x = [density, speed_x, speed_y, speed_z, centre_y, field_z]
        prims_y = [density, speed_y, speed_x, speed_z, centre_x, field_z]
        flux_x = sweep([v[:ROWS] for v in prims_x], face_x[:ROWS], 1)
        prims_x[3] = None
        ghost_x = sweep([v if v is None else v[ROWS:] for v in prims_x], face_x[ROWS:], 1)
        flux_y = sweep([v[:, :COLS] for v in prims_y], face_y[:, :COLS], 0)
        prims_y[3] = None
        ghost_y = sweep([v if v is None else v[:, COLS:] for v in prims_y], face_y[:, COLS:], 0)
        cross_x = jnp.concatenate([flux_x[4], ghost_x[4]], axis=0)
        cross_y = jnp.concatenate([flux_y[4], ghost_y[4]], axis=1)
        edge = 0.25 * (
            (cross_y + roll(cross_y, 1, 1)) - (cross_x + roll(cross_x, 1, 0))
        )
        edge = jnp.where(corner_ok, edge, 0.0)

        from_left = by_sublane(
            corner_in[section, 1], col_in[section, 1, 8:16], corner_in[section, 4]
        )
        from_right = by_sublane(
            corner_in[section, 2], col_in[section, 0, 8:16], corner_in[section, 5]
        )
        from_right = jnp.where(level == 0, roll(from_right, 32, 1), roll(from_right, 64, 1))
        beside = []
        for k in (1, 0):
            part = col_in[section, k, 8:16]
            part = jnp.concatenate([part, roll(part, -2, 0)], axis=1)
            beside.append(roll(part, 2, 0) if k == 1 else part)
        own_sides = jnp.where(sub8[:, :1] < 4, columns[6:7], columns[15:16])
        sub_wide = iota((8, 256), 0)

        def side_window(odd):
            left, right = (roll(v, -16, 1) if odd else v for v in beside)
            left = jnp.where(finer[(0, -1)] > 0.5, left, received[2:3])
            right = jnp.where(finer[(0, 1)] > 0.5, right, received[8:9])
            return jnp.where(sub_wide < 2, left, jnp.where(sub_wide < 6, own_sides, right))

        side_windows = [side_window(False), side_window(True)]
        swapped = (0, 2, 1, 3, 4, 6, 5)

        def windows(c):
            first = jnp.where(lane8 == COLS - 1, ghosted[c, 39:40, COLS:], ghosted[c, 39:40, :COLS])
            second = jnp.where(lane8 == COLS - 1, ghosted[c, 0:1, COLS:], ghosted[c, 0:1, :COLS])

            def at_level(low, high):
                value = jnp.where(level == 0, ghosted[c, low : low + 1], ghosted[c, high : high + 1])
                return jnp.where(lane8 == COLS - 1, value[:, COLS:], value[:, :COLS])

            base = jnp.where(
                sub8 < 2,
                first,
                jnp.where(sub8 < 4, second, jnp.where(sub8 < 6, at_level(7, 15), at_level(8, 16))),
            )
            q, rows_of = c % 4, slice(32 + 8 * (c // 4), 40 + 8 * (c // 4))
            fine = jnp.where(
                upper8,
                roll(row_in[section, 1, rows_of], -2 * q, 0),
                roll(row_in[section, 0, rows_of], -2 * q, 0),
            )
            pair = []
            for odd in range(2):
                value = jnp.where(use_rows, roll(fine, 64, 1) if odd else fine, base)
                value = jnp.where(use_left, roll(from_left, 127 - (16 * c + 8 + odd), 1), value)
                value = jnp.where(use_right, roll(from_right, -(16 * c + 8 + odd), 1), value)
                t = swapped[c]
                half = side_windows[odd][:, COLS * (t // 4) : COLS * (t // 4) + COLS]
                pair.append(jnp.where(in_side, roll(half, 80 - 32 * (t % 4), 1), value))
            return pair

        even, odd = zip(*[windows(c) if c != 3 else (None, None) for c in range(7)])

        def primitives_of(v):
            inv = 1.0 / v[0]
            return v[0], v[1] * inv, v[2] * inv, v[4], v[5], v[6]

        even, odd = primitives_of(even), primitives_of(odd)
        odd_before = [roll(v, 1, 1) for v in odd]
        even_before = [roll(v, 1, 1) for v in even]

        def along_rows(v, centre):
            return sweep([v[0], v[2], v[1], None, centre, v[3]], v[5], 0)[4]

        fine_y = along_rows(even, 0.5 * (even[4] + odd[4])) + along_rows(
            odd_before, 0.5 * (odd_before[4] + even[4])
        )

        def across(v):
            centre = 0.5 * (v[5] + roll(v[5], -1, 0))
            return [v[0], v[1], v[2], centre, v[3]]

        left, right = [], []
        for a, b, c, d in zip(*[across(v) for v in (even_before, odd_before, even, odd)]):
            middle = c - b
            left.append(b + 0.5 * minmod(b - a, middle))
            right.append(c - 0.5 * minmod(middle, d - c))
        left.insert(3, None)
        right.insert(3, None)
        fine_x = riemann(left, right, even[4])[4]
        fine_edge = 0.25 * (fine_y - (fine_x + roll(fine_x, 1, 0)))

        change = [
            (roll(flux_x[a], -1, 1) - flux_x[a])[:, :COLS]
            + (roll(flux_y[b], -1, 0) - flux_y[b])[:ROWS]
            for a, b in ((0, 0), (1, 2), (2, 1), (3, 3), (5, 5))
        ]

        def finish(c, value):
            if section == 0:
                current[c] = jnp.where(cell_ok, value, 0.0)
            else:
                out[c] = jnp.where(cell_ok, 0.5 * (fields[c] + value), 0.0)

        for c in range(5):
            finish(c, state[c] - ratio * change[c])

        sides = jnp.where(sub8 == 0, -fine_edge[2:3], jnp.where(sub8 == 1, -fine_edge[6:7], 0.0))
        sides = jnp.where(in_side, sides, 0.0)
        sides = dot(halves(sides, 0), line_place, ((0,), (0,)))[80:104]
        row24, lane24 = iota((24, COLS), 0), iota((24, COLS), 1)
        part = edge[:24, :COLS]
        on_low, on_high = row24 == 0, row24 == rows
        on_left, on_right = lane24 == 0, lane24 == cols

        def border_flags(row):
            side = finer[(row, 0)]
            first = jnp.maximum(jnp.maximum(side, finer[(0, -1)]), finer[(row, -1)])
            final = jnp.maximum(jnp.maximum(side, finer[(0, 1)]), finer[(row, 1)])
            value = jnp.where(on_left, first, jnp.where(on_right, final, side))
            return jnp.where(lane24 <= cols, value, 0.0) > 0.5

        part = jnp.where(on_left & (finer[(0, -1)] > 0.5), sides, part)
        part = jnp.where(on_right & (finer[(0, 1)] > 0.5), sides, part)
        part = jnp.where(on_low & border_flags(-1), fine_edge[2:3], part)
        part = jnp.where(on_high & border_flags(1), fine_edge[6:7], part)
        top = jnp.concatenate([part, edge[:24, COLS:]], axis=1)
        edge = jnp.concatenate([top, edge[24:]], axis=0)
        finish(5, state[5] - ratio * (roll(edge, -1, 0) - edge)[:ROWS, :COLS])
        finish(6, state[6] + ratio * (roll(edge, -1, 1) - edge)[:ROWS, :COLS])

    for copy in copies:
        copy.wait_send()


def on_device(seg_count, sub_count, fields, region_levels):
    vmem = pl.BlockSpec(memory_space=pltpu.VMEM)
    region_levels = region_levels.T
    fields = pltpu.with_memory_space_constraint(fields, pltpu.HBM)
    region_levels = pltpu.with_memory_space_constraint(region_levels, pltpu.HBM)
    return pl.pallas_call(
        functools.partial(kernel, seg_count, sub_count),
        out_shape=jax.ShapeDtypeStruct(fields.shape, F32),
        in_specs=[pl.BlockSpec(memory_space=pltpu.HBM)] * 2,
        out_specs=vmem,
        scratch_shapes=[
            pltpu.VMEM(fields.shape, F32),
            pltpu.SMEM(region_levels.shape, I32),
            pltpu.VMEM((7, 40, 256), F32),
            pltpu.VMEM((7, ROWS, COLS), F32),
            pltpu.VMEM((2, 2, 48, COLS), F32),
            pltpu.VMEM((2, 2, 48, COLS), F32),
            pltpu.VMEM((2, 6, 8, COLS), F32),
            pltpu.VMEM((2, 6, 8, COLS), F32),
            pltpu.VMEM((2, 2, 16, COLS), F32),
            pltpu.VMEM((2, 2, 16, COLS), F32),
            pltpu.VMEM((6, 256, COLS), BF16),
            pltpu.VMEM((2, 2, 256, COLS), BF16),
            pltpu.VMEM((256, COLS), BF16),
            pltpu.VMEM((256, 3 * COLS), BF16),
            pltpu.SemaphoreType.DMA((2, 8)),
            pltpu.SemaphoreType.DMA((2, 8)),
            pltpu.SemaphoreType.DMA((2,)),
        ],
        compiler_params=pltpu.CompilerParams(
            collective_id=0, has_side_effects=True, vmem_limit_bytes=32 * 1024 * 1024
        ),
    )(fields, region_levels)


def solution(mesh):
    body = functools.partial(on_device, mesh.shape["seg"], mesh.shape["sub"])
    return jax.shard_map(
        body,
        mesh=mesh,
        in_specs=(P(None, "seg", "sub"), P()),
        out_specs=P(None, "seg", "sub"),
        check_vma=False,
    )
```

```python
import functools

import jax
import jax.numpy as jnp
from jax import lax
from jax.experimental import pallas as pl
from jax.experimental.pallas import tpu as pltpu
from jax.sharding import PartitionSpec as P

STEP_SIZE = 0.08
MESH = pl.DeviceIdType.MESH
F32, BF16, I32 = jnp.float32, jnp.bfloat16, jnp.int32
ROWS, COLS = 32, 128
AROUND = [(1, 0), (1, 1), (1, -1), (-1, 0), (-1, 1), (-1, -1), (0, -1), (0, 1)]


def iota(shape, axis):
    return lax.broadcasted_iota(I32, shape, axis)


def pick(level, values):
    return jnp.where(level == 0, values[0], jnp.where(level == 1, values[1], values[2]))


def halves(value, axis):
    high = value.astype(BF16)
    low = (value - high.astype(F32)).astype(BF16)
    return jnp.concatenate([high, low], axis=axis)


def dot(a, b, dims=((1,), (0,))):
    return lax.dot_general(a, b, (dims, ((), ())), preferred_element_type=F32)


def twice(matrix, axis):
    matrix = matrix.astype(BF16)
    return jnp.concatenate([matrix, matrix], axis=axis)


def resample(source, target, delta):
    source = jnp.where(delta < 0, source >> 1, source)
    target = jnp.where(delta > 0, target >> 1, target)
    return jnp.where(source == target, jnp.where(delta < 0, 0.5, 1.0), 0.0).astype(F32)


def roll(value, shift, axis):
    return pltpu.roll(value, shift % value.shape[axis], axis)


def minmod(a, b):
    return jnp.maximum(jnp.minimum(a, b), 0.0) + jnp.minimum(jnp.maximum(a, b), 0.0)


def sweep(primitives, normal, axis):
    left, right = [], []
    for value in primitives:
        if value is None:
            left.append(None)
            right.append(None)
            continue
        before = value - roll(value, 1, axis)
        half = 0.5 * minmod(before, roll(before, -1, axis))
        left.append(roll(value + half, 1, axis))
        right.append(value - half)

    return riemann(left, right, normal)


def riemann(left, right, normal):
    def pieces(values):
        density, speed_n, speed_t, speed_z, field_t, field_z = values
        square = normal * normal + field_t * field_t + field_z * field_z
        moment = density * speed_n
        cons = [density, moment, density * speed_t, None, field_t, field_z]
        flux = [
            moment,
            moment * speed_n + (density + 0.5 * square) - normal * normal,
            moment * speed_t - normal * field_t,
            None,
            field_t * speed_n - normal * speed_t,
            None,
        ]
        if speed_z is not None:
            cons[3] = density * speed_z
            flux[3] = moment * speed_z - normal * field_z
            flux[5] = field_z * speed_n - normal * speed_z
        return flux, cons, jnp.abs(speed_n) + jnp.sqrt(1.0 + square / density)

    flux_l, cons_l, signal_l = pieces(left)
    flux_r, cons_r, signal_r = pieces(right)
    fastest = jnp.maximum(signal_l, signal_r)
    return [
        None if fl is None else 0.5 * ((fl + fr) - fastest * (cr - cl))
        for fl, fr, cl, cr in zip(flux_l, flux_r, cons_l, cons_r)
    ]


def strip_choices(block, upper, sub8, odd_lane):
    same, coarse, fine = block, [], []
    sign = 1 if upper else -1
    edge = 7 if upper else 0
    for comp in range(7):
        value = block[comp]
        if comp == 6:
            pair = roll(value, 1, 0) if upper else value
        else:
            pair = 0.5 * (value + roll(value, sign, 0))
        if comp == 5:
            pair = jnp.where(odd_lane, roll(pair, 1, 1), pair)
        coarse.append(
            jnp.where(
                sub8 == edge,
                pair,
                jnp.where(sub8 == edge - sign, roll(pair, sign, 0), roll(pair, 2 * sign, 0)),
            )
        )
        fine.append(jnp.where(sub8 == edge, value, roll(value, -sign, 0)))
    return same, coarse, fine


def kernel(
    seg_count, sub_count, fields_hbm, levels_hbm, out,
    fields, levels, ghosted, current, row_out, row_in, corner_out, corner_in, col_out, col_in,
    lane_maps, row_maps, fine_map, border_map, send_sem, recv_sem, fetch_sem,
):
    fetches = [
        pltpu.make_async_copy(levels_hbm, levels, fetch_sem.at[0]),
        pltpu.make_async_copy(fields_hbm, fields, fetch_sem.at[1]),
    ]
    seg, sub = lax.axis_index("seg"), lax.axis_index("sub")

    def place(offset):
        return (
            lax.rem(seg + (seg_count + offset[0]), seg_count),
            lax.rem(sub + (sub_count + offset[1]), sub_count),
        )

    places = [place(offset) for offset in AROUND]
    barrier = pltpu.get_barrier_semaphore()
    for target in places:
        pl.semaphore_signal(barrier, inc=1, device_id=target, device_id_type=MESH)
    for fetch in fetches:
        fetch.start()

    i, j = iota((COLS, COLS), 0), iota((COLS, COLS), 1)
    together = (i >> 5) == (j >> 5)
    comp_six = (i >> 5) == 2
    source = (i & ~31) + ((i & 31) >> 1) + ((i & 1) << 4)
    fine_map[...] = twice(jnp.where(source == j, 1.0, 0.0), 0)
    end = jnp.where(j == 8, 0, jnp.where(j == 9, 1, 2 * COLS))
    border_map[:, 0:COLS] = twice(jnp.where((i >> 1) + ((i & 1) << 6) == j, 1.0, 0.0), 0)
    border_map[:, 2 * COLS :] = twice(jnp.where(i == end, 1.0, 0.0), 0)

    fetches[0].wait()
    level = levels[sub, seg]
    near = {offset: levels[p[1], p[0]] for offset, p in zip(AROUND, places)}
    rows = pick(level, (8, 16, 32))
    cols = pick(level, (32, 64, 128))
    ratio = pick(level, [jnp.float32(STEP_SIZE / h) for h in (4.0, 2.0, 1.0)])
    delta = {offset: near[offset] - level for offset in AROUND}

    for k, offset in enumerate(AROUND[:6]):
        if offset[1] == 0:
            matrix = resample(i, j, delta[offset])
        elif offset[1] == 1:
            matrix = jnp.where(j >= 125, resample(i - cols, j - COLS, delta[offset]), 0.0)
        else:
            first = j - pick(near[offset], (32, 64, 0))
            ok = (first >= 0) & (first < 3)
            matrix = jnp.where(ok, resample(i, first, delta[offset]), 0.0)
        lane_maps[k] = twice(matrix, 0)
    border_map[:, COLS : 2 * COLS] = twice(jnp.where(i == end + cols - 2, 1.0, 0.0), 0)
    i, j = i & 31, j & 31
    for k, offset in enumerate(AROUND[6:]):
        d = delta[offset]
        matrix = jnp.where(together, resample(i, j, d), 0.0)
        row_maps[k, 0] = twice(matrix, 0)
        faces = jnp.where(together, jnp.where(i == 2 * j, 1.0, 0.0), 0.0)
        row_maps[k, 1] = twice(jnp.where(comp_six & (d < 0), faces, matrix), 0)
    k, i = iota((16, COLS), 0), iota((16, COLS), 1)
    to_right = k >= 8
    k = k & 7
    is_face = k >= 3
    k = k - jnp.where(is_face, 3, 0) - jnp.where(to_right, 3, 0)
    i = i - jnp.where(to_right, cols, 0)

    def column_pick(d):
        faces = jnp.where(d < 0, jnp.where(i == 2 * k, 1.0, 0.0), resample(i, k, d))
        return jnp.where(is_face, faces, resample(i, k, d))

    raw = jnp.where(i == jnp.where(to_right, k - 2, k - 3), 1.0, 0.0)
    is_raw = (iota((16, COLS), 0) & 7) >= 6
    column_map = twice(
        jnp.where(
            is_raw,
            raw,
            jnp.where(to_right, column_pick(delta[(0, 1)]), column_pick(delta[(0, -1)])),
        ),
        1,
    )
    k, i = iota((16, 256), 0), iota((16, 256), 1)
    column_place = twice(
        jnp.where((k < 3) & (i == k + 253), 1.0, 0.0)
        + jnp.where((k >= 8) & (k < 11) & (i == cols + k - 8), 1.0, 0.0),
        0,
    )
    k, i = iota((8, COLS), 0), iota((8, COLS), 1)
    line_place = twice(
        jnp.where(((k == 0) & (i == 0)) | ((k == 1) & (i == cols)), 1.0, 0.0), 0
    )

    sub8, lane8 = iota((8, COLS), 0), iota((8, COLS), 1)
    odd_lane = (lane8 & 1) == 1
    upper8 = sub8 >= 4
    inside8 = lane8 < cols
    in_side = (lane8 >= 80) & (lane8 < 96)

    def flag(condition):
        return jnp.where(condition, 1.0, 0.0).astype(F32)

    finer = {offset: flag(near[offset] > level) for offset in AROUND}

    def by_sublane(low, middle, high):
        return jnp.where(sub8 < 2, low, jnp.where(sub8 < 6, middle, high))

    finer_left = by_sublane(finer[(-1, -1)], finer[(0, -1)], finer[(1, -1)])
    finer_right = by_sublane(finer[(-1, 1)], finer[(0, 1)], finer[(1, 1)])
    finer_rows = by_sublane(finer[(-1, 0)], 0.0, finer[(1, 0)])
    use_left = jnp.where(lane8 == COLS - 1, finer_left, 0.0) > 0.5
    use_right = jnp.where(lane8 == cols, finer_right, 0.0) > 0.5
    use_rows = jnp.where(inside8, finer_rows, 0.0) > 0.5
    row40, lane40 = iota((40, 256), 0), iota((40, 256), 1)
    corner_ok = (row40 <= rows) & (lane40 <= cols)
    row32, lane32 = iota((ROWS, COLS), 0), iota((ROWS, COLS), 1)
    cell_ok = (row32 < rows) & (lane32 < cols)

    fetches[1].wait()
    copies = []

    def send(section, index, source, target):
        copy = pltpu.make_async_remote_copy(
            src_ref=source,
            dst_ref=target,
            send_sem=send_sem.at[section, index],
            recv_sem=recv_sem.at[section, index],
            device_id=places[index % 8],
            device_id_type=MESH,
        )
        copy.start()
        return copy

    for section in range(2):
        if section == 0:
            state = [jnp.where(cell_ok, fields[c], 0.0) for c in range(7)]
        else:
            state = [current[c] for c in range(7)]

        tops = [pick(level, (v[0:8], v[8:16], v[24:32])) for v in state]
        lows = [v[0:8] for v in state]
        border = [
            jnp.where(
                sub8 < 2,
                roll(top, 2, 0),
                jnp.where(
                    sub8 < 4,
                    roll(low, 2, 0),
                    jnp.where(sub8 < 6, roll(top, 6, 0), roll(low, 6, 0)),
                ),
            )
            for top, low in zip(tops, lows)
        ]
        stacked = jnp.concatenate(state + [jnp.zeros((ROWS, COLS), F32)], axis=0)
        columns = dot(column_map, halves(stacked, 1), ((1,), (1,)))
        border = dot(halves(jnp.concatenate(border, axis=0), 1), border_map[...])
        ends = []
        for part in (border[:, COLS : 2 * COLS], border[:, 2 * COLS :]):
            total = part[0:8]
            for c in range(1, 7):
                total = total + roll(part[8 * c : 8 * c + 8], 16 * c, 1)
            ends.append(total)
        for k in range(2):
            part = columns[8 * k : 8 * k + 8]
            first, second = part[:, :COLS], part[:, COLS:]
            fine = dot(
                jnp.concatenate([halves(first, 1), halves(second, 1)], axis=0), fine_map[...]
            )
            col_out[section, k, 8:16] = by_sublane(roll(fine[8:], 2, 0), ends[1 - k], fine[:8])
            second = jnp.where((lane8 >> 5) == 1, roll(second, -3, 0), second)
            first = dot(halves(first, 1), row_maps[k, 0])
            second = dot(halves(second, 1), row_maps[k, 1])
            col_out[section, k, 0:8] = jnp.where(upper8, roll(second, 4, 0), first)
        done, copies = copies, []
        if section == 1:
            for k in range(2):
                copies.append(send(section, 6 + k, col_out.at[section, k], col_in.at[section, k]))
        for upper in (True, False):
            choices = strip_choices(tops if upper else lows, upper, sub8, odd_lane)
            base = 0 if upper else 3
            for k in (base + 1, base + 2, base):
                d = delta[AROUND[k]]
                chosen = [
                    jnp.where(d == 0, a, jnp.where(d < 0, b, c)) for a, b, c in zip(*choices)
                ]
                chosen.append(jnp.zeros((8, COLS), F32))
                packed = [
                    jnp.where(upper8 == upper, chosen[2 * m], roll(chosen[2 * m + 1], 4, 0))
                    for m in range(4)
                ]
                packed = jnp.concatenate(packed, axis=0)
                packed = dot(halves(packed, 1), lane_maps[k])
                if k != base:
                    corner = packed[0:8] + ends[k - base - 1]
                    for m in range(1, 4):
                        corner = corner + roll(packed[8 * m : 8 * m + 8], 32 * m, 1)
                    corner_out[section, k] = corner
                    continue
                row_out[section, k // 3, 0:32] = packed
                for group in range(2):
                    block = jnp.zeros((8, COLS), F32)
                    for q in range(4 if group == 0 else 3):
                        c = 4 * group + q
                        part = roll(border[8 * c : 8 * c + 8, :COLS], 2 * q, 0)
                        place_of = q if upper else (3 + q) & 3
                        block = jnp.where((sub8 >> 1) == place_of, part, block)
                    row_out[section, k // 3, 32 + 8 * group : 40 + 8 * group] = block
        if section == 0:
            pl.semaphore_wait(barrier, len(AROUND))
            for k in range(2):
                copies.append(send(section, 6 + k, col_out.at[section, k], col_in.at[section, k]))
        for k in (1, 2, 4, 5):
            copies.append(
                send(section, k, corner_out.at[section, k], corner_in.at[section, k])
            )
        for k in (0, 3):
            copies.append(
                send(section, k, row_out.at[section, k // 3], row_in.at[section, k // 3])
            )
        for copy in done:
            copy.wait_send()
        for copy in copies:
            copy.wait_recv()

        received = jnp.concatenate(
            [
                jnp.concatenate([part, roll(part, 4, 0)], axis=1)
                for part in (col_in[section, 1, 0:8], col_in[section, 0, 0:8])
            ],
            axis=0,
        )
        sides = dot(halves(received, 0), column_place, ((0,), (0,)))
        for c in range(7):
            def strip(k):
                if k % 3 == 0:
                    block = row_in[section, k // 3, 8 * (c // 2) : 8 * (c // 2) + 8]
                else:
                    block = roll(corner_in[section, k], -32 * (c // 2), 1)
                return roll(block, 4, 0) if c % 2 else block

            low = [
                jnp.where(inside8, strip(0), strip(2)),
                jnp.where(lane8 < 64, strip(2), strip(1)),
            ]
            high = [
                jnp.where(inside8, strip(3), strip(5)),
                jnp.where(lane8 < 64, strip(5), strip(4)),
            ]
            for h in range(2):
                lanes = slice(128 * h, 128 * h + 128)
                for b in range(4):
                    block = sides[32 * c + 8 * b : 32 * c + 8 * b + 8, lanes]
                    if h == 0:
                        block = jnp.where(inside8, state[c][8 * b : 8 * b + 8], block)
                    if b in (1, 2):
                        block = jnp.where(level == b - 1, high[h], block)
                    ghosted[c, 8 * b : 8 * b + 8, lanes] = block
                ghosted[c, 32:40, lanes] = jnp.where(upper8, low[h], high[h])

        density = ghosted[0]
        inverse = 1.0 / density
        speed_x, speed_y, speed_z = (ghosted[c] * inverse for c in (1, 2, 3))
        field_z, face_x, face_y = ghosted[4], ghosted[5], ghosted[6]
        centre_x = 0.5 * (face_x + roll(face_x, -1, 1))
        centre_y = 0.5 * (face_y + roll(face_y, -1, 0))
        prims_x = [density, speed_x, speed_y, speed_z, centre_y, field_z]
        prims_y = [density, speed_y, speed_x, speed_z, centre_x, field_z]
        flux_x = sweep([v[:ROWS] for v in prims_x], face_x[:ROWS], 1)
        prims_x[3] = None
        ghost_x = sweep([v if v is None else v[ROWS:] for v in prims_x], face_x[ROWS:], 1)
        flux_y = sweep([v[:, :COLS] for v in prims_y], face_y[:, :COLS], 0)
        prims_y[3] = None
        ghost_y = sweep([v if v is None else v[:, COLS:] for v in prims_y], face_y[:, COLS:], 0)
        cross_x = jnp.concatenate([flux_x[4], ghost_x[4]], axis=0)
        cross_y = jnp.concatenate([flux_y[4], ghost_y[4]], axis=1)
        edge = 0.25 * (
            (cross_y + roll(cross_y, 1, 1)) - (cross_x + roll(cross_x, 1, 0))
        )
        edge = jnp.where(corner_ok, edge, 0.0)

        from_left = by_sublane(
            corner_in[section, 1], col_in[section, 1, 8:16], corner_in[section, 4]
        )
        from_right = by_sublane(
            corner_in[section, 2], col_in[section, 0, 8:16], corner_in[section, 5]
        )
        from_right = jnp.where(level == 0, roll(from_right, 32, 1), roll(from_right, 64, 1))
        beside = []
        for k in (1, 0):
            part = col_in[section, k, 8:16]
            part = jnp.concatenate([part, roll(part, -2, 0)], axis=1)
            beside.append(roll(part, 2, 0) if k == 1 else part)
        own_sides = jnp.where(sub8[:, :1] < 4, columns[6:7], columns[15:16])
        sub_wide = iota((8, 256), 0)

        def side_window(odd):
            left, right = (roll(v, -16, 1) if odd else v for v in beside)
            left = jnp.where(finer[(0, -1)] > 0.5, left, received[2:3])
            right = jnp.where(finer[(0, 1)] > 0.5, right, received[8:9])
            return jnp.where(sub_wide < 2, left, jnp.where(sub_wide < 6, own_sides, right))

        side_windows = [side_window(False), side_window(True)]
        swapped = (0, 2, 1, 3, 4, 6, 5)

        def windows(c):
            first = jnp.where(lane8 == COLS - 1, ghosted[c, 39:40, COLS:], ghosted[c, 39:40, :COLS])
            second = jnp.where(lane8 == COLS - 1, ghosted[c, 0:1, COLS:], ghosted[c, 0:1, :COLS])

            def at_level(low, high):
                value = jnp.where(level == 0, ghosted[c, low : low + 1], ghosted[c, high : high + 1])
                return jnp.where(lane8 == COLS - 1, value[:, COLS:], value[:, :COLS])

            base = jnp.where(
                sub8 < 2,
                first,
                jnp.where(sub8 < 4, second, jnp.where(sub8 < 6, at_level(7, 15), at_level(8, 16))),
            )
            q, rows_of = c % 4, slice(32 + 8 * (c // 4), 40 + 8 * (c // 4))
            fine = jnp.where(
                upper8,
                roll(row_in[section, 1, rows_of], -2 * q, 0),
                roll(row_in[section, 0, rows_of], -2 * q, 0),
            )
            pair = []
            for odd in range(2):
                value = jnp.where(use_rows, roll(fine, 64, 1) if odd else fine, base)
                value = jnp.where(use_left, roll(from_left, 127 - (16 * c + 8 + odd), 1), value)
                value = jnp.where(use_right, roll(from_right, -(16 * c + 8 + odd), 1), value)
                t = swapped[c]
                half = side_windows[odd][:, COLS * (t // 4) : COLS * (t // 4) + COLS]
                pair.append(jnp.where(in_side, roll(half, 80 - 32 * (t % 4), 1), value))
            return pair

        even, odd = zip(*[windows(c) if c != 3 else (None, None) for c in range(7)])

        def primitives_of(v):
            inv = 1.0 / v[0]
            return v[0], v[1] * inv, v[2] * inv, v[4], v[5], v[6]

        even, odd = primitives_of(even), primitives_of(odd)
        odd_before = [roll(v, 1, 1) for v in odd]
        even_before = [roll(v, 1, 1) for v in even]

        def along_rows(v, centre):
            return sweep([v[0], v[2], v[1], None, centre, v[3]], v[5], 0)[4]

        fine_y = along_rows(even, 0.5 * (even[4] + odd[4])) + along_rows(
            odd_before, 0.5 * (odd_before[4] + even[4])
        )

        def across(v):
            centre = 0.5 * (v[5] + roll(v[5], -1, 0))
            return [v[0], v[1], v[2], centre, v[3]]

        left, right = [], []
        for a, b, c, d in zip(*[across(v) for v in (even_before, odd_before, even, odd)]):
            middle = c - b
            left.append(b + 0.5 * minmod(b - a, middle))
            right.append(c - 0.5 * minmod(middle, d - c))
        left.insert(3, None)
        right.insert(3, None)
        fine_x = riemann(left, right, even[4])[4]
        fine_edge = 0.25 * (fine_y - (fine_x + roll(fine_x, 1, 0)))

        change = [
            (roll(flux_x[a], -1, 1) - flux_x[a])[:, :COLS]
            + (roll(flux_y[b], -1, 0) - flux_y[b])[:ROWS]
            for a, b in ((0, 0), (1, 2), (2, 1), (3, 3), (5, 5))
        ]

        def finish(c, value):
            if section == 0:
                current[c] = jnp.where(cell_ok, value, 0.0)
            else:
                out[c] = jnp.where(cell_ok, 0.5 * (fields[c] + value), 0.0)

        for c in range(5):
            finish(c, state[c] - ratio * change[c])

        sides = jnp.where(sub8 == 0, -fine_edge[2:3], jnp.where(sub8 == 1, -fine_edge[6:7], 0.0))
        sides = jnp.where(in_side, sides, 0.0)
        sides = dot(halves(sides, 0), line_place, ((0,), (0,)))[80:104]
        row24, lane24 = iota((24, COLS), 0), iota((24, COLS), 1)
        part = edge[:24, :COLS]
        on_low, on_high = row24 == 0, row24 == rows
        on_left, on_right = lane24 == 0, lane24 == cols

        def border_flags(row):
            side = finer[(row, 0)]
            first = jnp.maximum(jnp.maximum(side, finer[(0, -1)]), finer[(row, -1)])
            final = jnp.maximum(jnp.maximum(side, finer[(0, 1)]), finer[(row, 1)])
            value = jnp.where(on_left, first, jnp.where(on_right, final, side))
            return jnp.where(lane24 <= cols, value, 0.0) > 0.5

        part = jnp.where(on_left & (finer[(0, -1)] > 0.5), sides, part)
        part = jnp.where(on_right & (finer[(0, 1)] > 0.5), sides, part)
        part = jnp.where(on_low & border_flags(-1), fine_edge[2:3], part)
        part = jnp.where(on_high & border_flags(1), fine_edge[6:7], part)
        top = jnp.concatenate([part, edge[:24, COLS:]], axis=1)
        edge = jnp.concatenate([top, edge[24:]], axis=0)
        finish(5, state[5] - ratio * (roll(edge, -1, 0) - edge)[:ROWS, :COLS])
        finish(6, state[6] + ratio * (roll(edge, -1, 1) - edge)[:ROWS, :COLS])

    for copy in copies:
        copy.wait_send()


def on_device(seg_count, sub_count, fields, region_levels):
    vmem = pl.BlockSpec(memory_space=pltpu.VMEM)
    region_levels = region_levels.T
    fields = pltpu.with_memory_space_constraint(fields, pltpu.HBM)
    region_levels = pltpu.with_memory_space_constraint(region_levels, pltpu.HBM)
    return pl.pallas_call(
        functools.partial(kernel, seg_count, sub_count),
        out_shape=jax.ShapeDtypeStruct(fields.shape, F32),
        in_specs=[pl.BlockSpec(memory_space=pltpu.HBM)] * 2,
        out_specs=vmem,
        scratch_shapes=[
            pltpu.VMEM(fields.shape, F32),
            pltpu.SMEM(region_levels.shape, I32),
            pltpu.VMEM((7, 40, 256), F32),
            pltpu.VMEM((7, ROWS, COLS), F32),
            pltpu.VMEM((2, 2, 48, COLS), F32),
            pltpu.VMEM((2, 2, 48, COLS), F32),
            pltpu.VMEM((2, 6, 8, COLS), F32),
            pltpu.VMEM((2, 6, 8, COLS), F32),
            pltpu.VMEM((2, 2, 16, COLS), F32),
            pltpu.VMEM((2, 2, 16, COLS), F32),
            pltpu.VMEM((6, 256, COLS), BF16),
            pltpu.VMEM((2, 2, 256, COLS), BF16),
            pltpu.VMEM((256, COLS), BF16),
            pltpu.VMEM((256, 3 * COLS), BF16),
            pltpu.SemaphoreType.DMA((2, 8)),
            pltpu.SemaphoreType.DMA((2, 8)),
            pltpu.SemaphoreType.DMA((2,)),
        ],
        compiler_params=pltpu.CompilerParams(
            collective_id=0, has_side_effects=True, vmem_limit_bytes=32 * 1024 * 1024
        ),
    )(fields, region_levels)


def solution(mesh):
    body = functools.partial(on_device, mesh.shape["seg"], mesh.shape["sub"])
    return jax.shard_map(
        body,
        mesh=mesh,
        in_specs=(P(None, "seg", "sub"), P()),
        out_specs=P(None, "seg", "sub"),
        check_vma=False,
    )
```
